128 devices in a mesh: grp: 4 (over y_lo, core), lat: 32 (over z, x, y_hi).
Axes of the slice: x: 4, y: 4 (y_hi: 2, y_lo: 2; y = y_hi * 2 + y_lo), z: 4, core: 2. Of those that a mesh axis runs over, the one named last changes fastest.
Arguments:
- eigvecs: bfloat16 [256, 32, 6, 16384], P('grp', None, None, 'lat'), may hold values from -6 to 6
- solutions: bfloat16 [4, 32, 32, 6, 16384], P('grp', None, None, None, 'lat'), may hold values from -6 to 6
- source_index: int32 [4], replicated, may hold values from 0 to 255
- source_time: int32 [1], replicated, may hold values from 0 to 31
- dilution: int32 [4, 4], replicated, may hold values from 0 to 3, each once within a row
Outputs:
- perambulator: float32 [32, 256, 256], P('lat', 'grp')
- sources: bfloat16 [4, 4, 4, 6, 16384], P('grp', None, None, None, 'lat')
The draws below stay inside these ranges and needn't reach their ends.
Inputs may be any that keep to these rules, and one draw needn't show every extreme that they name: `dilution`: each row is a permutation of 0 to 3.
All inputs are finite; a program needn't handle non-finite values.
Results may differ from the reference program's by a relative error of at most 0.001.
Values may be sent and summed in bfloat16 or wider, within the bound.
No kernel may reach another device: no remote copies, remote signals or barrier semaphores. Data moves between devices by JAX's collectives and lax.ppermute only.
A program may use at most 256 MiB of HBM per device.

```python
import math
import jax
import jax.numpy as jnp
from jax import lax

NEV = 256
COMP = 6
SPIN = 4
MASS = 2
NSRC = 4
SOLS = 32
TW = 32
SPACE_ALL = 16384


def with_ends(array, rng, smallest, high):
    longest = array.shape.index(max(array.shape))
    spots = []
    for shift in (0, 1):
        where = [jax.random.randint(jax.random.fold_in(rng, axis), (), 0, length) for axis, length in enumerate(array.shape)]
        where[longest] = (where[longest] + shift) % array.shape[longest]
        spots.append(tuple(where))
    return array.at[spots[0]].set(smallest).at[spots[1]].set(high)


def strengthened(values, rng, source, target, blocks, factor):
    owner, partner = [(jnp.arange(values.shape[position]) // (values.shape[position] // blocks)).reshape([-1 if axis == position else 1 for axis in range(values.ndim)]) for position in (source, target)]
    chosen = jax.random.permutation(rng, blocks)[partner]
    strong = (owner == chosen) | (owner == (partner + blocks // 2) % blocks)
    return jnp.where(strong, factor * values, values)


def block_scale(stream_key, shape, shards, low, top_value):
    loudness = 1.0
    for axis_at, blocks in shards:
        heights = jax.random.uniform(jax.random.fold_in(jax.random.fold_in(stream_key, 6), axis_at), (blocks,), jnp.float32, low / len(shards), top_value / len(shards))
        loudness = loudness * jnp.repeat(jnp.exp(heights), shape[axis_at] // blocks).reshape((-1,) + (1,) * (len(shape) - 1 - axis_at))
    return loudness


def gaussian(key, extent, scale, limit, shards=(), kind=jnp.bfloat16):
    entries = scale * jax.random.normal(key, extent, jnp.float32)
    if shards:
        entries = entries * block_scale(key, extent, shards, -0.22, 0.18)
    return jnp.clip(entries, -limit, limit).astype(kind)


def gaussian_with(rng, dims, scale, limit, cuts, heavy, kind=jnp.bfloat16):
    result = scale * jax.random.normal(rng, dims, jnp.float32)
    if cuts:
        result = result * block_scale(rng, dims, cuts, -0.22, 0.18)
    return jnp.clip(strengthened(result, jax.random.fold_in(rng, 3), *heavy), -limit, limit).astype(kind)


def setup_inputs(seed: int = 0) -> dict:
    key_list = jax.random.split(jax.random.key(seed), 6)
    eigvecs = gaussian(key_list[0], (NEV, TW, COMP, SPACE_ALL), 1.0, 6.0, ((0, 4), (3, 32)))
    solutions = gaussian_with(key_list[1], (SPIN, SOLS, TW, COMP, SPACE_ALL), 1.0, 6.0, ((0, 4), (4, 32)), (4, 2, 32, 2.75))
    source_index = with_ends(jax.random.randint(key_list[2], (NSRC,), 0, NEV), jax.random.fold_in(key_list[2], 1), 0, NEV - 1).astype(jnp.int32)
    source_time = jax.random.randint(key_list[3], (1,), 0, TW).astype(jnp.int32)
    dilution = jax.vmap(lambda own: jax.random.permutation(own, SPIN))(jax.random.split(key_list[4], NSRC)).reshape((NSRC, SPIN)).astype(jnp.int32)
    return {"eigvecs": eigvecs, "solutions": solutions, "source_index": source_index, "source_time": source_time, "dilution": dilution}


def make_columns(block):
    groups, count, times, comps, sites = block.shape
    parts = block.reshape(groups, count, times, comps // 2, 2, sites)
    turned = jnp.stack([parts[:, :, :, :, 1, :], -parts[:, :, :, :, 0, :]], axis=4)
    both = jnp.stack([parts, turned], axis=2)
    return both.reshape(groups, count * 2, times, comps, sites)

def reorder(tau, dilution, masses):
    times, vecs, groups, width = tau.shape
    nsources = dilution.shape[0]
    view = tau.reshape(times, vecs, groups, masses, nsources, width // (masses * nsources))
    spin_grid = jnp.arange(groups, dtype=jnp.int32)
    mask = jnp.transpose(dilution)[None, :, :] == spin_grid[:, None, None]
    picked = jnp.where(mask[None, None, :, :, None, :, None], view[:, :, None], jnp.zeros((), jnp.float32))
    return lax.optimization_barrier(jnp.sum(picked, axis=3)).reshape(times, vecs, groups * width)

def reference(eigvecs, solutions, source_index, source_time, dilution):
    slice_now = lax.dynamic_index_in_dim(eigvecs, source_time[0].astype(jnp.int32), 1, keepdims=False)
    chosen = jnp.take(slice_now, source_index, axis=0)
    spin_mask = jnp.arange(SPIN, dtype=jnp.int32)[None, None, :] == jnp.transpose(dilution)[:, :, None]
    sources = jnp.where(spin_mask[:, :, :, None, None], chosen[None, :, None, :, :], jnp.zeros((), jnp.bfloat16)).astype(jnp.bfloat16)
    columns = make_columns(solutions)

    def one_slice(t):
        vecs = lax.dynamic_index_in_dim(eigvecs, t, 1, keepdims=False).astype(jnp.float32).reshape(NEV, -1)
        cols = lax.dynamic_index_in_dim(columns, t, 2, keepdims=False).astype(jnp.float32).reshape(SPIN * 2 * SOLS, -1)
        return jnp.dot(vecs, cols.T, precision=lax.Precision.HIGHEST)
    tau = lax.map(one_slice, jnp.arange(TW, dtype=jnp.int32)).reshape(TW, NEV, SPIN, 2 * SOLS)
    scale = 1.0 / math.sqrt(COMP * SPACE_ALL)
    return (reorder(tau, dilution, MASS) * scale, sources)
```

```python
import functools
import math

import jax
import jax.numpy as jnp
from jax import lax
from jax.experimental import pallas as pl
from jax.experimental.pallas import tpu as pltpu
from jax.sharding import Mesh
from jax.sharding import PartitionSpec as P

MASS = 2
RAW = 8
SWAP = [(0, 1), (1, 0)]


def tie(value, *after):
    return lax.optimization_barrier((value, *after))[0]


def swap(value, axis):
    return lax.ppermute(value, axis, SWAP)


def by_time(block):
    n, _, comps, sites = block.shape
    parts = block.reshape(n, 4, 4, 2, comps, sites).transpose(2, 1, 3, 4, 0, 5)
    return parts.reshape(4, 8, comps // 2, 2 * n, sites)


def dot_kernel(count, *refs):
    cols, (own, other), outs = refs[:count], refs[count : count + 2], refs[count + 2 :]
    width = own.shape[3] // 2
    for at in range(own.shape[1]):
        for col, out in zip(cols, outs):
            n = col.shape[3] // 2
            halves = []
            for vecs in (own, other):
                total = None
                for colour in range(vecs.shape[2]):
                    term = lax.dot_general(
                        col[0, at, colour],
                        vecs[0, at, colour],
                        (((1,), (1,)), ((), ())),
                        preferred_element_type=jnp.float32,
                    )
                    total = term if total is None else total + term
                real = total[:n, :width] + total[n:, width:]
                imag = total[n:, :width] - total[:n, width:]
                halves.append((real, imag))
            for part in range(2):
                out[0, at, part] = jnp.concatenate([halves[0][part], halves[1][part]], axis=1)


def project(cols, own, other, first, size, step):
    _, inner, colours, rows, sites = own.shape
    spec = lambda n, off: pl.BlockSpec(
        (1, step, colours, n, sites), lambda i, j, off=off: (i + off, j, 0, 0, 0)
    )
    in_specs = [spec(c.shape[3], 0) for c in cols] + [spec(rows, first)] * 2
    out_specs = [
        pl.BlockSpec((1, step, 2, c.shape[3] // 2, rows), lambda i, j: (i, j, 0, 0, 0))
        for c in cols
    ]
    out_shape = [
        jax.ShapeDtypeStruct((size, inner, 2, c.shape[3] // 2, rows), jnp.float32) for c in cols
    ]
    total = sum(c.shape[3] for c in cols)
    return pl.pallas_call(
        functools.partial(dot_kernel, len(cols)),
        grid=(size, inner // step),
        in_specs=in_specs,
        out_specs=out_specs,
        out_shape=out_shape,
        compiler_params=pltpu.CompilerParams(vmem_limit_bytes=48 * 2**20),
        cost_estimate=pl.CostEstimate(
            flops=2 * size * inner * colours * sites * total * 2 * rows,
            bytes_accessed=2 * size * inner * colours * sites * (total + 2 * rows),
            transcendentals=0,
        ),
        name="project",
    )(*cols, own, other)


def pick(value, index):
    return lax.dynamic_index_in_dim(value, index, 0, keepdims=False)


def sum_z(part):
    me = lax.axis_index("z")
    slabs = jnp.swapaxes(part, 0, 1)
    total = pick(slabs, me)
    got = [
        lax.ppermute(pick(slabs, (me + k) % 4), "z", [(i, (i + k) % 4) for i in range(4)])
        for k in (1, 3, 2)
    ]
    return total + got[0] + got[1] + got[2]


def sum_x(part, first, size):
    me = lax.axis_index("x")
    clip = lambda i: jnp.clip(i - first, 0, size - 1)
    total = pick(part, clip(me)) if size > 1 else part[0]
    for k in (1, 3, 2):
        send = pick(part, clip((me + k) % 4)) if size > 1 else part[0]
        pairs = [(i, (i + k) % 4) for i in range(4) if first <= (i + k) % 4 < first + size]
        total = total + lax.ppermute(send, "x", pairs)
    return total


def sum_yh(part):
    me = lax.axis_index("yh")
    return pick(part, me) + swap(pick(part, 1 - me), "yh")


def local(eigvecs, solutions, source_index, source_time, dilution):
    owned, times, comps, sites = eigvecs.shape
    count = solutions.shape[1]
    nsources, spins = dilution.shape
    scale = 1.0 / math.sqrt(comps * sites * 32)
    core = lax.axis_index("c")
    group = 2 * lax.axis_index("yl") + core
    sols = solutions[0]

    raw = swap(sols[:RAW], "yl")
    mine = by_time(sols)
    late = by_time(sols[RAW:])
    send = [late[x] for x in range(4)]
    got = [swap(send[0], "yl")]
    got.append(swap(tie(send[1], raw), "yl"))
    got.append(swap(tie(send[2], got[0]), "yl"))
    got.append(swap(tie(send[3], got[1]), "yl"))

    own = by_time(eigvecs)
    other = swap(own, "c")

    def rows(part):
        x, inner, _, n, lanes = part.shape
        return part.reshape(x, 4, 2, 2 * n, lanes)

    a, b = project([mine, by_time(raw)], own, other, 0, 4, 4)
    first = sum_x(sum_z(jnp.concatenate([rows(a), rows(b)], axis=3)), 0, 4)
    tail = []
    mid = [project([got[x][None]], own, other, x, 1, 4)[0] for x in range(3)]
    mid = sum_x(sum_z(rows(jnp.concatenate(mid, axis=0))), 0, 3)
    last = project([got[3][None]], own, other, 3, 1, 4)[0]
    last = sum_x(sum_z(rows(last)), 3, 1)

    main = sum_yh(jnp.concatenate([first, mid], axis=1))
    main_c = swap(main, "c")
    last = sum_yh(last)
    last_c = swap(last, "c")
    is_last = lax.axis_index("x") == 3

    def assemble(main, last, half):
        main = main[:, half * owned : (half + 1) * owned]
        last = last[:, half * owned : (half + 1) * owned]
        n0, n1 = 2 * count, 2 * count + 2 * RAW
        home = main[:n0].reshape(2, count, owned)
        early = main[n0:n1].reshape(2, RAW, owned)
        rest = jnp.where(is_last, last, main[n1:]).reshape(2, count - RAW, owned)
        return home, jnp.concatenate([early, rest], axis=1)

    h0, y0 = assemble(main, last, 0)
    h1, y1 = assemble(main_c, last_c, 1)
    tau = jnp.stack([h0, h1, y0, y1])
    order = jnp.stack([group, group ^ 1, group ^ 2, group ^ 3])
    spin_of = jnp.take(jnp.transpose(dilution), order, axis=0)
    mask = spin_of[:, None, :] == jnp.arange(spins, dtype=jnp.int32)[None, :, None]
    view = tau.reshape(4, 1, 2, MASS, nsources, count // (MASS * nsources), owned)
    picked = jnp.where(mask[:, :, None, None, :, None, None], view, 0.0)
    result = jnp.sum(picked, axis=0).reshape(spins, 2, count, owned) * scale
    result = result.transpose(3, 0, 2, 1).reshape(1, owned, spins * count * 2)

    slice_now = lax.dynamic_index_in_dim(eigvecs, source_time[0], 1, keepdims=False)
    owners = source_index // owned
    chosen = jnp.take(slice_now, source_index - owners * owned, axis=0)
    chosen = jnp.where((owners == group)[:, None, None], chosen, 0).astype(jnp.bfloat16)
    chosen = chosen + swap(chosen, "c")
    chosen = chosen + swap(chosen, "yl")
    my_spins = lax.dynamic_index_in_dim(dilution, group, 1, keepdims=False)
    spin_mask = jnp.arange(spins, dtype=jnp.int32)[None, :] == my_spins[:, None]
    sources = jnp.where(
        spin_mask[:, :, None, None], chosen[:, None, :, :], jnp.zeros((), jnp.bfloat16)
    )
    return result, sources[None]


def solution(mesh):
    split = Mesh(mesh.devices.reshape(2, 2, 4, 4, 2), ("yl", "c", "z", "x", "yh"))
    grp, lat = ("yl", "c"), ("z", "x", "yh")
    return jax.shard_map(
        local,
        mesh=split,
        in_specs=(P(grp, None, None, lat), P(grp, None, None, None, lat), P(), P(), P()),
        out_specs=(P(lat, grp, None), P(grp, None, None, None, lat)),
        check_vma=False,
    )
```

```python
import functools
import math

import jax
import jax.numpy as jnp
from jax import lax
from jax.experimental import pallas as pl
from jax.experimental.pallas import tpu as pltpu
from jax.sharding import Mesh
from jax.sharding import PartitionSpec as P

MASS = 2
RAW = 8
SWAP = [(0, 1), (1, 0)]


def swap(value, axis):
    return lax.ppermute(value, axis, SWAP)


HINT = pl.CostEstimate(flops=1000, bytes_accessed=1000, transcendentals=0)


def by_time_kernel(cuts, block, *outs):
    for k in range(block.shape[1]):
        turned = jnp.swapaxes(block[:, k], 0, 1)
        for t in range(turned.shape[0]):
            for (low, high), out in zip(cuts, outs):
                out[t // 2, 0, t % 2, k] = turned[t, low:high]


def by_time(block, cuts):
    n, comps, times, sites = block.shape
    return pl.pallas_call(
        functools.partial(by_time_kernel, cuts),
        grid=(4,),
        in_specs=[pl.BlockSpec((n, comps, times // 4, sites), lambda z: (0, 0, z, 0))],
        out_specs=[
            pl.BlockSpec((4, 1, 2, comps, h - l, sites), lambda z: (0, z, 0, 0, 0, 0))
            for l, h in cuts
        ],
        out_shape=[
            jax.ShapeDtypeStruct((4, 4, 2, comps, h - l, sites), block.dtype) for l, h in cuts
        ],
        compiler_params=pltpu.CompilerParams(vmem_limit_bytes=48 * 2**20),
        cost_estimate=HINT,
        name="by_time",
    )(block)


def rows_of(block):
    x, z, yh, comps, n, sites = block.shape
    return block.reshape(x, z * yh, comps // 2, 2 * n, sites)


ANY = pl.BlockSpec(memory_space=pl.ANY)


def carve_kernel(block, *refs):
    refs[-1][...] = block[0]


def carve(late, x, *after):
    _, inner, colours, n, sites = late.shape
    return pl.pallas_call(
        carve_kernel,
        grid=(4,),
        in_specs=[pl.BlockSpec((1, inner // 4, colours, n, sites), lambda i: (x, i, 0, 0, 0))]
        + [ANY] * len(after),
        out_specs=pl.BlockSpec((inner // 4, colours, n, sites), lambda i: (i, 0, 0, 0)),
        out_shape=jax.ShapeDtypeStruct((inner, colours, n, sites), late.dtype),
        compiler_params=pltpu.CompilerParams(vmem_limit_bytes=60 * 2**20),
        cost_estimate=HINT,
        name="carve",
    )(late, *after)


def choose_kernel(owned, rows, at, block, *refs):
    group, time, index = at[0], at[1], at[2 + pl.program_id(0)]
    row = lax.broadcasted_iota(jnp.int32, block.shape[1:], 1)
    here = jnp.where(index // owned == group, time % rows, -1)
    kept = jnp.where(row == here, block[0].astype(jnp.float32), 0.0)
    refs[-1][0] = jnp.sum(kept, axis=1).astype(block.dtype)


def choose(vecs, source_index, source_time, group, after):
    owned, comps, _, sites = vecs.shape
    rows = 16
    at = jnp.concatenate([group[None], source_time, source_index])
    return pl.pallas_call(
        functools.partial(choose_kernel, owned, rows),
        grid_spec=pltpu.PrefetchScalarGridSpec(
            num_scalar_prefetch=1,
            grid=(source_index.shape[0],),
            in_specs=[
                pl.BlockSpec(
                    (1, comps, rows, sites), lambda i, at: (at[2 + i] % owned, 0, at[1] // rows, 0)
                ),
                ANY,
            ],
            out_specs=pl.BlockSpec((1, comps, sites), lambda i, at: (i, 0, 0)),
        ),
        out_shape=jax.ShapeDtypeStruct((source_index.shape[0], comps, sites), vecs.dtype),
        compiler_params=pltpu.CompilerParams(vmem_limit_bytes=60 * 2**20),
        cost_estimate=HINT,
        name="choose",
    )(at, vecs, after)


def dot_kernel(count, *refs):
    cols, (own, other), outs = refs[:count], refs[count : count + 2], refs[-count:]
    width = own.shape[3] // 2
    for at in range(own.shape[1]):
        for col, out in zip(cols, outs):
            n = col.shape[3] // 2
            halves = []
            for vecs in (own, other):
                total = None
                for colour in range(vecs.shape[2]):
                    term = lax.dot_general(
                        col[0, at, colour],
                        vecs[0, at, colour],
                        (((1,), (1,)), ((), ())),
                        preferred_element_type=jnp.float32,
                    )
                    total = term if total is None else total + term
                real = total[:n, :width] + total[n:, width:]
                imag = total[n:, :width] - total[:n, width:]
                halves.append((real, imag))
            for part in range(2):
                out[0, at, part] = jnp.concatenate([halves[0][part], halves[1][part]], axis=1)


def project(cols, own, other, first, size, step, *after):
    _, inner, colours, rows, sites = own.shape
    spec = lambda n, off: pl.BlockSpec(
        (1, step, colours, n, sites), lambda i, j, off=off: (i + off, j, 0, 0, 0)
    )
    in_specs = [spec(c.shape[3], 0) for c in cols] + [spec(rows, first)] * 2 + [ANY] * len(after)
    out_specs = [
        pl.BlockSpec((1, step, 2, c.shape[3] // 2, rows), lambda i, j: (i, j, 0, 0, 0))
        for c in cols
    ]
    out_shape = [
        jax.ShapeDtypeStruct((size, inner, 2, c.shape[3] // 2, rows), jnp.float32) for c in cols
    ]
    return pl.pallas_call(
        functools.partial(dot_kernel, len(cols)),
        grid=(size, inner // step),
        in_specs=in_specs,
        out_specs=out_specs,
        out_shape=out_shape,
        compiler_params=pltpu.CompilerParams(vmem_limit_bytes=48 * 2**20),
        cost_estimate=HINT,
        name="project",
    )(*cols, own, other, *after)


def pick(value, index):
    return lax.dynamic_index_in_dim(value, index, 0, keepdims=False)


def sum_z(part):
    me = lax.axis_index("z")
    slabs = jnp.swapaxes(part, 0, 1)
    total = pick(slabs, me)
    got = [
        lax.ppermute(pick(slabs, (me + k) % 4), "z", [(i, (i + k) % 4) for i in range(4)])
        for k in (1, 3, 2)
    ]
    return total + got[0] + got[1] + got[2]


def sum_x(part, first, size):
    me = lax.axis_index("x")
    clip = lambda i: jnp.clip(i - first, 0, size - 1)
    total = pick(part, clip(me)) if size > 1 else part[0]
    for k in (1, 3, 2):
        send = pick(part, clip((me + k) % 4)) if size > 1 else part[0]
        pairs = [(i, (i + k) % 4) for i in range(4) if first <= (i + k) % 4 < first + size]
        total = total + lax.ppermute(send, "x", pairs)
    return total


def sum_yh(part):
    me = lax.axis_index("yh")
    return pick(part, me) + swap(pick(part, 1 - me), "yh")


def local(eigvecs, solutions, source_index, source_time, dilution):
    owned, times, comps, sites = eigvecs.shape
    count = solutions.shape[1]
    nsources, spins = dilution.shape
    scale = 1.0 / math.sqrt(comps * sites * 32)
    core = lax.axis_index("c")
    group = 2 * lax.axis_index("yl") + core
    sols = solutions[0].transpose(0, 2, 1, 3)
    vecs = eigvecs.transpose(0, 2, 1, 3)

    raw = swap(sols[:RAW], "yl")
    other = swap(vecs, "c")
    early, late = by_time(sols, ((0, RAW), (RAW, count)))
    late = rows_of(late)
    send = [carve(late, 0), carve(late, 1, raw)]
    got = [swap(send[0], "yl"), swap(send[1], "yl")]
    send.append(carve(late, 2, got[0]))
    got.append(swap(send[2], "yl"))
    send.append(carve(late, 3, got[1]))
    got.append(swap(send[3], "yl"))

    whole = ((0, owned),)
    own = rows_of(by_time(vecs, whole)[0])
    other = rows_of(by_time(other, whole)[0])
    raw = rows_of(by_time(raw, ((0, RAW),))[0])

    def rows(part):
        x, inner, _, n, lanes = part.shape
        return part.reshape(x, 4, 2, 2 * n, lanes)

    def against(x, *after):
        return rows(project([got[x][None]], own, other, x, 1, 4, *after)[0])

    parts = project([rows_of(early), late, raw], own, other, 0, 4, 4)
    first_z = sum_z(jnp.concatenate([rows(p) for p in parts], axis=3))
    chosen = choose(vecs, source_index, source_time, group, first_z)
    first = sum_x(first_z, 0, 4)
    mid = [against(0, first_z, send[2])]
    mid.append(against(1, first, mid[0], send[3]))
    mid_z = sum_z(jnp.concatenate(mid, axis=0))
    last = [against(2, mid_z)]
    mid = sum_x(mid_z, 0, 2)
    main = sum_yh(jnp.concatenate([first, mid], axis=1))
    main_c = swap(main, "c")
    last.append(against(3, main_c, last[0]))
    last = sum_x(sum_z(jnp.concatenate(last, axis=0)), 2, 2)
    last = sum_yh(last)
    last_c = swap(last, "c")
    is_last = lax.axis_index("x") >= 2

    def assemble(main, last, half):
        main = main[:, half * owned : (half + 1) * owned]
        last = last[:, half * owned : (half + 1) * owned]
        cut = [2 * RAW, 2 * count, 2 * (count + RAW)]
        view = lambda v: v.reshape(2, -1, owned)
        home = jnp.concatenate([view(main[: cut[0]]), view(main[cut[0] : cut[1]])], axis=1)
        rest = jnp.where(is_last, last, main[cut[2] :])
        away = jnp.concatenate([view(main[cut[1] : cut[2]]), view(rest)], axis=1)
        return home, away

    h0, y0 = assemble(main, last, 0)
    h1, y1 = assemble(main_c, last_c, 1)
    tau = jnp.stack([h0, h1, y0, y1])
    order = jnp.stack([group, group ^ 1, group ^ 2, group ^ 3])
    spin_of = jnp.take(jnp.transpose(dilution), order, axis=0)
    mask = spin_of[:, None, :] == jnp.arange(spins, dtype=jnp.int32)[None, :, None]
    view = tau.reshape(4, 1, 2, MASS, nsources, count // (MASS * nsources), owned)
    picked = jnp.where(mask[:, :, None, None, :, None, None], view, 0.0)
    result = jnp.sum(picked, axis=0).reshape(spins, 2, count, owned) * scale
    result = result.transpose(3, 0, 2, 1).reshape(1, owned, spins * count * 2)

    chosen = chosen + swap(chosen, "c")
    chosen = chosen + swap(chosen, "yl")
    my_spins = lax.dynamic_index_in_dim(dilution, group, 1, keepdims=False)
    spin_mask = jnp.arange(spins, dtype=jnp.int32)[None, :] == my_spins[:, None]
    sources = jnp.where(
        spin_mask[:, :, None, None], chosen[:, None, :, :], jnp.zeros((), jnp.bfloat16)
    )
    return result, sources[None]


def solution(mesh):
    split = Mesh(mesh.devices.reshape(2, 2, 4, 4, 2), ("yl", "c", "z", "x", "yh"))
    grp, lat = ("yl", "c"), ("z", "x", "yh")
    return jax.shard_map(
        local,
        mesh=split,
        in_specs=(P(grp, None, None, lat), P(grp, None, None, None, lat), P(), P(), P()),
        out_specs=(P(lat, grp, None), P(grp, None, None, None, lat)),
        check_vma=False,
    )
```

```python
import functools
import math

import jax
import jax.numpy as jnp
from jax import lax
from jax.experimental import pallas as pl
from jax.experimental.pallas import tpu as pltpu
from jax.sharding import Mesh
from jax.sharding import PartitionSpec as P

MASS = 2
RAW = 8
SWAP = [(0, 1), (1, 0)]


def swap(value, axis):
    return lax.ppermute(value, axis, SWAP)


HINT = pl.CostEstimate(flops=1000, bytes_accessed=1000, transcendentals=0)


def by_time_kernel(cuts, block, *outs):
    for k in range(block.shape[1]):
        turned = jnp.swapaxes(block[:, k], 0, 1)
        for (low, high, first, size), out in zip(cuts, outs):
            for t in range(2 * size):
                out[t // 2, 0, t % 2, k] = turned[2 * first + t, low:high]


def by_time(block, cuts):
    n, comps, times, sites = block.shape
    return pl.pallas_call(
        functools.partial(by_time_kernel, cuts),
        grid=(4,),
        in_specs=[pl.BlockSpec((n, comps, times // 4, sites), lambda z: (0, 0, z, 0))],
        out_specs=[
            pl.BlockSpec((size, 1, 2, comps, high - low, sites), lambda z: (0, z, 0, 0, 0, 0))
            for low, high, _, size in cuts
        ],
        out_shape=[
            jax.ShapeDtypeStruct((size, 4, 2, comps, high - low, sites), block.dtype)
            for low, high, _, size in cuts
        ],
        compiler_params=pltpu.CompilerParams(vmem_limit_bytes=56 * 2**20),
        cost_estimate=HINT,
        name="by_time",
    )(block)


def rows_of(block):
    x, z, yh, comps, n, sites = block.shape
    return block.reshape(x, z * yh, comps // 2, 2 * n, sites)


ANY = pl.BlockSpec(memory_space=pl.ANY)


def choose_kernel(owned, rows, at, block, *refs):
    group, time, index = at[0], at[1], at[2 + pl.program_id(0)]
    row = lax.broadcasted_iota(jnp.int32, block.shape[1:], 1)
    here = jnp.where(index // owned == group, time % rows, -1)
    kept = jnp.where(row == here, block[0].astype(jnp.float32), 0.0)
    refs[-1][0] = jnp.sum(kept, axis=1).astype(block.dtype)


def choose(vecs, source_index, source_time, group, after):
    owned, comps, _, sites = vecs.shape
    rows = 16
    at = jnp.concatenate([group[None], source_time, source_index])
    return pl.pallas_call(
        functools.partial(choose_kernel, owned, rows),
        grid_spec=pltpu.PrefetchScalarGridSpec(
            num_scalar_prefetch=1,
            grid=(source_index.shape[0],),
            in_specs=[
                pl.BlockSpec(
                    (1, comps, rows, sites), lambda i, at: (at[2 + i] % owned, 0, at[1] // rows, 0)
                ),
                ANY,
            ],
            out_specs=pl.BlockSpec((1, comps, sites), lambda i, at: (i, 0, 0)),
        ),
        out_shape=jax.ShapeDtypeStruct((source_index.shape[0], comps, sites), vecs.dtype),
        compiler_params=pltpu.CompilerParams(vmem_limit_bytes=60 * 2**20),
        cost_estimate=HINT,
        name="choose",
    )(at, vecs, after)


def dot_kernel(count, *refs):
    cols, (own, other), outs = refs[:count], refs[count : count + 2], refs[-count:]
    width = own.shape[3] // 2
    for at in range(own.shape[1]):
        total = None
        for colour in range(own.shape[2]):
            term = lax.dot_general(
                jnp.concatenate([col[0, at, colour] for col in cols], axis=0),
                jnp.concatenate([own[0, at, colour], other[0, at, colour]], axis=0),
                (((1,), (1,)), ((), ())),
                preferred_element_type=jnp.float32,
            )
            total = term if total is None else total + term
        row = 0
        for col, out in zip(cols, outs):
            n = col.shape[3] // 2
            re, im = total[row : row + n], total[row + n : row + 2 * n]
            row += 2 * n
            real, imag = [], []
            for left in (0, 2 * width):
                mid, right = left + width, left + 2 * width
                real.append(re[:, left:mid] + im[:, mid:right])
                imag.append(im[:, left:mid] - re[:, mid:right])
            out[0, at, 0] = jnp.concatenate(real, axis=1)
            out[0, at, 1] = jnp.concatenate(imag, axis=1)


def project(cols, own, other, first, size, step, *after):
    _, inner, colours, rows, sites = own.shape
    spec = lambda n, off: pl.BlockSpec(
        (1, step, colours, n, sites), lambda i, j, off=off: (i + off, j, 0, 0, 0)
    )
    in_specs = [spec(c.shape[3], 0) for c in cols] + [spec(rows, first)] * 2 + [ANY] * len(after)
    out_specs = [
        pl.BlockSpec((1, step, 2, c.shape[3] // 2, rows), lambda i, j: (i, j, 0, 0, 0))
        for c in cols
    ]
    out_shape = [
        jax.ShapeDtypeStruct((size, inner, 2, c.shape[3] // 2, rows), jnp.float32) for c in cols
    ]
    return pl.pallas_call(
        functools.partial(dot_kernel, len(cols)),
        grid=(size, inner // step),
        in_specs=in_specs,
        out_specs=out_specs,
        out_shape=out_shape,
        compiler_params=pltpu.CompilerParams(vmem_limit_bytes=48 * 2**20),
        cost_estimate=HINT,
        name="project",
    )(*cols, own, other, *after)


def pick(value, index):
    return lax.dynamic_index_in_dim(value, index, 0, keepdims=False)


def sum_z(part):
    me = lax.axis_index("z")
    slabs = jnp.swapaxes(part, 0, 1)
    total = pick(slabs, me)
    got = [
        lax.ppermute(pick(slabs, (me + k) % 4), "z", [(i, (i + k) % 4) for i in range(4)])
        for k in (1, 3, 2)
    ]
    return total + got[0] + got[1] + got[2]


def sum_x(part, first, size):
    me = lax.axis_index("x")
    clip = lambda i: jnp.clip(i - first, 0, size - 1)
    total = pick(part, clip(me)) if size > 1 else part[0]
    for k in (1, 3, 2):
        send = pick(part, clip((me + k) % 4)) if size > 1 else part[0]
        pairs = [(i, (i + k) % 4) for i in range(4) if first <= (i + k) % 4 < first + size]
        total = total + lax.ppermute(send, "x", pairs)
    return total


def sum_yh(part):
    me = lax.axis_index("yh")
    return pick(part, me) + swap(pick(part, 1 - me), "yh")


def local(eigvecs, solutions, source_index, source_time, dilution):
    owned, times, comps, sites = eigvecs.shape
    count = solutions.shape[1]
    nsources, spins = dilution.shape
    scale = 1.0 / math.sqrt(comps * sites * 32)
    core = lax.axis_index("c")
    group = 2 * lax.axis_index("yl") + core
    sols = solutions[0].transpose(0, 2, 1, 3)
    vecs = eigvecs.transpose(0, 2, 1, 3)

    raw = swap(sols[:RAW], "yl")
    other = swap(vecs, "c")
    sent = ((RAW, count, 0, 2), (RAW, count, 2, 1), (RAW, count, 3, 1))
    mine, *send = by_time(sols, ((0, count, 0, 4), *sent))
    got = [swap(rows_of(part), "yl") for part in send]

    whole = ((0, owned, 0, 4),)
    own = rows_of(by_time(vecs, whole)[0])
    other = rows_of(by_time(other, whole)[0])
    raw = rows_of(by_time(raw, ((0, RAW, 0, 4),))[0])

    def rows(part):
        x, inner, _, n, lanes = part.shape
        return part.reshape(x, 4, 2, 2 * n, lanes)

    def against(part, x, step, *after):
        return rows(project([part], own, other, x, part.shape[0], step, *after)[0])

    parts = project([rows_of(mine), raw], own, other, 0, 4, 8)
    first_z = sum_z(jnp.concatenate([rows(p) for p in parts], axis=3))
    chosen = choose(vecs, source_index, source_time, group, first_z)
    first = sum_x(first_z, 0, 4)
    mid = [against(got[0], 0, 8, first_z)]
    mid.append(against(got[1], 2, 4, first))
    mid = sum_x(sum_z(jnp.concatenate(mid, axis=0)), 0, 3)
    main = sum_yh(jnp.concatenate([first, mid], axis=1))
    main_c = swap(main, "c")
    last = sum_yh(sum_x(sum_z(against(got[2], 3, 2, mid)), 3, 1))
    last_c = swap(last, "c")
    is_last = lax.axis_index("x") == 3

    def assemble(main, last, half):
        main = main[:, half * owned : (half + 1) * owned]
        last = last[:, half * owned : (half + 1) * owned]
        view = lambda v: v.reshape(2, -1, owned)
        cut = [2 * count, 2 * (count + RAW)]
        home = view(main[: cut[0]])
        rest = jnp.where(is_last, last, main[cut[1] :])
        away = jnp.concatenate([view(main[cut[0] : cut[1]]), view(rest)], axis=1)
        return home, away

    h0, y0 = assemble(main, last, 0)
    h1, y1 = assemble(main_c, last_c, 1)
    tau = jnp.stack([h0, h1, y0, y1])
    order = jnp.stack([group, group ^ 1, group ^ 2, group ^ 3])
    spin_of = jnp.take(jnp.transpose(dilution), order, axis=0)
    mask = spin_of[:, None, :] == jnp.arange(spins, dtype=jnp.int32)[None, :, None]
    view = tau.reshape(4, 1, 2, MASS, nsources, count // (MASS * nsources), owned)
    picked = jnp.where(mask[:, :, None, None, :, None, None], view, 0.0)
    result = jnp.sum(picked, axis=0).reshape(spins, 2, count, owned) * scale
    result = result.transpose(3, 0, 2, 1).reshape(1, owned, spins * count * 2)

    chosen = chosen + swap(chosen, "c")
    chosen = chosen + swap(chosen, "yl")
    my_spins = lax.dynamic_index_in_dim(dilution, group, 1, keepdims=False)
    spin_mask = jnp.arange(spins, dtype=jnp.int32)[None, :] == my_spins[:, None]
    sources = jnp.where(
        spin_mask[:, :, None, None], chosen[:, None, :, :], jnp.zeros((), jnp.bfloat16)
    )
    return result, sources[None]


def solution(mesh):
    split = Mesh(mesh.devices.reshape(2, 2, 4, 4, 2), ("yl", "c", "z", "x", "yh"))
    grp, lat = ("yl", "c"), ("z", "x", "yh")
    return jax.shard_map(
        local,
        mesh=split,
        in_specs=(P(grp, None, None, lat), P(grp, None, None, None, lat), P(), P(), P()),
        out_specs=(P(lat, grp, None), P(grp, None, None, None, lat)),
        check_vma=False,
    )
```

```python
import functools
import math

import jax
import jax.numpy as jnp
from jax import lax
from jax.experimental import pallas as pl
from jax.experimental.pallas import tpu as pltpu
from jax.sharding import Mesh
from jax.sharding import PartitionSpec as P

MASS = 2
RAW = 8
SWAP = [(0, 1), (1, 0)]


def swap(value, axis):
    return lax.ppermute(value, axis, SWAP)


ANY = pl.BlockSpec(memory_space=pl.ANY)
HINT = pl.CostEstimate(flops=1000, bytes_accessed=1000, transcendentals=0)


def by_time_kernel(cuts, block, *refs):
    outs = refs[-len(cuts) :]
    for k in range(block.shape[1]):
        turned = jnp.swapaxes(block[:, k], 0, 1)
        for (low, high, x, nx, y, ny), out in zip(cuts, outs):
            for i in range(nx):
                for j in range(ny):
                    out[i, 0, j, k] = turned[2 * (x + i) + y + j, low:high]


def by_time(block, cuts, *after):
    n, comps, times, sites = block.shape
    return pl.pallas_call(
        functools.partial(by_time_kernel, cuts),
        grid=(4,),
        in_specs=[pl.BlockSpec((n, comps, times // 4, sites), lambda z: (0, 0, z, 0))]
        + [ANY] * len(after),
        out_specs=[
            pl.BlockSpec((nx, 1, ny, comps, high - low, sites), lambda z: (0, z, 0, 0, 0, 0))
            for low, high, _, nx, _, ny in cuts
        ],
        out_shape=[
            jax.ShapeDtypeStruct((nx, 4, ny, comps, high - low, sites), block.dtype)
            for low, high, _, nx, _, ny in cuts
        ],
        compiler_params=pltpu.CompilerParams(vmem_limit_bytes=(56 if n > RAW else 16) * 2**20),
        cost_estimate=HINT,
        name="by_time",
    )(block, *after)


def rows_of(block):
    x, z, yh, comps, n, sites = block.shape
    return block.reshape(x, z * yh, comps // 2, 2 * n, sites)


def choose_kernel(owned, rows, at, block, out):
    group, time, index = at[0], at[1], at[2 + pl.program_id(0)]
    row = lax.broadcasted_iota(jnp.int32, block.shape[1:], 1)
    here = jnp.where(index // owned == group, time % rows, -1)
    kept = jnp.where(row == here, block[0].astype(jnp.float32), 0.0)
    out[0] = jnp.sum(kept, axis=1).astype(block.dtype)


def choose(vecs, source_index, source_time, group):
    owned, comps, _, sites = vecs.shape
    rows = 16
    at = jnp.concatenate([group[None], source_time, source_index])
    return pl.pallas_call(
        functools.partial(choose_kernel, owned, rows),
        grid_spec=pltpu.PrefetchScalarGridSpec(
            num_scalar_prefetch=1,
            grid=(source_index.shape[0],),
            in_specs=[
                pl.BlockSpec(
                    (1, comps, rows, sites), lambda i, at: (at[2 + i] % owned, 0, at[1] // rows, 0)
                )
            ],
            out_specs=pl.BlockSpec((1, comps, sites), lambda i, at: (i, 0, 0)),
        ),
        out_shape=jax.ShapeDtypeStruct((source_index.shape[0], comps, sites), vecs.dtype),
        compiler_params=pltpu.CompilerParams(vmem_limit_bytes=60 * 2**20),
        cost_estimate=HINT,
        name="choose",
    )(at, vecs)


def dot_kernel(count, *refs):
    cols, (own, other), outs = refs[:count], refs[count : count + 2], refs[-count:]
    width = own.shape[3] // 2
    for at in range(own.shape[1]):
        total = None
        for colour in range(own.shape[2]):
            term = lax.dot_general(
                jnp.concatenate([col[0, at, colour] for col in cols], axis=0),
                jnp.concatenate([own[0, at, colour], other[0, at, colour]], axis=0),
                (((1,), (1,)), ((), ())),
                preferred_element_type=jnp.float32,
            )
            total = term if total is None else total + term
        row = 0
        for col, out in zip(cols, outs):
            n = col.shape[3] // 2
            re, im = total[row : row + n], total[row + n : row + 2 * n]
            row += 2 * n
            real, imag = [], []
            for left in (0, 2 * width):
                mid, right = left + width, left + 2 * width
                real.append(re[:, left:mid] + im[:, mid:right])
                imag.append(im[:, left:mid] - re[:, mid:right])
            out[0, at, 0] = jnp.concatenate(real, axis=1)
            out[0, at, 1] = jnp.concatenate(imag, axis=1)


def project(cols, own, other, x, y, step, *after):
    size, inner, colours, _, sites = cols[0].shape
    rows, stride = own.shape[3], own.shape[1] // inner
    spec = lambda n, stride=1, x=0, y=0: pl.BlockSpec(
        (1, step, colours, n, sites), lambda i, j: (i + x, j * stride + y, 0, 0, 0)
    )
    in_specs = [spec(c.shape[3]) for c in cols] + [spec(rows, stride, x, y)] * 2
    in_specs += [ANY] * len(after)
    out_specs = [
        pl.BlockSpec((1, step, 2, c.shape[3] // 2, rows), lambda i, j: (i, j, 0, 0, 0))
        for c in cols
    ]
    out_shape = [
        jax.ShapeDtypeStruct((size, inner, 2, c.shape[3] // 2, rows), jnp.float32) for c in cols
    ]
    return pl.pallas_call(
        functools.partial(dot_kernel, len(cols)),
        grid=(size, inner // step),
        in_specs=in_specs,
        out_specs=out_specs,
        out_shape=out_shape,
        compiler_params=pltpu.CompilerParams(vmem_limit_bytes=48 * 2**20),
        cost_estimate=HINT,
        name="project",
    )(*cols, own, other, *after)


def pick(value, index):
    return lax.dynamic_index_in_dim(value, index, 0, keepdims=False)


def sum_z(part):
    me = lax.axis_index("z")
    slabs = jnp.swapaxes(part, 0, 1)
    total = pick(slabs, me)
    got = [
        lax.ppermute(pick(slabs, (me + k) % 4), "z", [(i, (i + k) % 4) for i in range(4)])
        for k in (1, 3, 2)
    ]
    return total + got[0] + got[1] + got[2]


def sum_x(part, first, size):
    me = lax.axis_index("x")
    clip = lambda i: jnp.clip(i - first, 0, size - 1)
    total = pick(part, clip(me)) if size > 1 else part[0]
    for k in (1, 3, 2):
        send = pick(part, clip((me + k) % 4)) if size > 1 else part[0]
        pairs = [(i, (i + k) % 4) for i in range(4) if first <= (i + k) % 4 < first + size]
        total = total + lax.ppermute(send, "x", pairs)
    return total


def sum_yh(part):
    me = lax.axis_index("yh")
    return pick(part, me) + swap(pick(part, 1 - me), "yh")


def local(eigvecs, solutions, source_index, source_time, dilution):
    owned, times, comps, sites = eigvecs.shape
    count = solutions.shape[1]
    nsources, spins = dilution.shape
    scale = 1.0 / math.sqrt(comps * sites * 32)
    core = lax.axis_index("c")
    group = 2 * lax.axis_index("yl") + core
    sols = solutions[0].transpose(0, 2, 1, 3)
    vecs = eigvecs.transpose(0, 2, 1, 3)

    raw = swap(sols[:RAW], "yl")
    other = swap(vecs, "c")
    chosen = choose(vecs, source_index, source_time, group)
    sent = [(RAW, count, *cut) for cut in ((0, 2, 0, 2), (2, 1, 0, 2), (3, 1, 0, 1), (3, 1, 1, 1))]
    mine, *send = by_time(sols, ((0, count, 0, 4, 0, 2), *sent), chosen)
    got = [swap(rows_of(part), "yl") for part in send]

    chosen = lax.psum(chosen, ("yl", "c"))

    whole = ((0, owned, 0, 4, 0, 2),)
    own = rows_of(by_time(vecs, whole, chosen)[0])
    other = rows_of(by_time(other, whole)[0])
    raw = rows_of(by_time(raw, ((0, RAW, 0, 4, 0, 2),), chosen)[0])

    def rows(part):
        x, inner, _, n, lanes = part.shape
        return part.reshape(x, 4, inner // 4, 2 * n, lanes)

    def against(part, x, y, step, *after):
        return rows(project([part], own, other, x, y, step, *after)[0])

    parts = project([rows_of(mine), raw], own, other, 0, 0, 8)
    first_z = sum_z(jnp.concatenate([rows(p) for p in parts], axis=3))
    first = sum_x(first_z, 0, 4)
    mid = [against(got[0], 0, 0, 8, first_z)]
    mid.append(against(got[1], 2, 0, 4, first))
    mid = sum_x(sum_z(jnp.concatenate(mid, axis=0)), 0, 3)
    main = sum_yh(jnp.concatenate([first, mid], axis=1))
    main_c = swap(main, "c")
    last = [against(got[2], 3, 0, 1, mid), against(got[3], 3, 1, 1, mid)]
    last = sum_yh(sum_x(sum_z(jnp.concatenate(last, axis=2)), 3, 1))
    last_c = swap(last, "c")
    is_last = lax.axis_index("x") == 3

    def assemble(main, last, half):
        main = main[:, half * owned : (half + 1) * owned]
        last = last[:, half * owned : (half + 1) * owned]
        view = lambda v: v.reshape(2, -1, owned)
        cut = [2 * count, 2 * (count + RAW)]
        home = view(main[: cut[0]])
        rest = jnp.where(is_last, last, main[cut[1] :])
        away = jnp.concatenate([view(main[cut[0] : cut[1]]), view(rest)], axis=1)
        return home, away

    h0, y0 = assemble(main, last, 0)
    h1, y1 = assemble(main_c, last_c, 1)
    tau = jnp.stack([h0, h1, y0, y1])
    order = jnp.stack([group, group ^ 1, group ^ 2, group ^ 3])
    spin_of = jnp.take(jnp.transpose(dilution), order, axis=0)
    mask = spin_of[:, None, :] == jnp.arange(spins, dtype=jnp.int32)[None, :, None]
    view = tau.reshape(4, 1, 2, MASS, nsources, count // (MASS * nsources), owned)
    picked = jnp.where(mask[:, :, None, None, :, None, None], view, 0.0)
    result = jnp.sum(picked, axis=0).reshape(spins, 2, count, owned) * scale
    result = result.transpose(3, 0, 2, 1).reshape(1, owned, spins * count * 2)

    my_spins = lax.dynamic_index_in_dim(dilution, group, 1, keepdims=False)
    spin_mask = jnp.arange(spins, dtype=jnp.int32)[None, :] == my_spins[:, None]
    sources = jnp.where(
        spin_mask[:, :, None, None], chosen[:, None, :, :], jnp.zeros((), jnp.bfloat16)
    )
    return result, sources[None]


def solution(mesh):
    split = Mesh(mesh.devices.reshape(2, 2, 4, 4, 2), ("yl", "c", "z", "x", "yh"))
    grp, lat = ("yl", "c"), ("z", "x", "yh")
    return jax.shard_map(
        local,
        mesh=split,
        in_specs=(P(grp, None, None, lat), P(grp, None, None, None, lat), P(), P(), P()),
        out_specs=(P(lat, grp, None), P(grp, None, None, None, lat)),
        check_vma=False,
    )
```

```python
import functools
import math

import jax
import jax.numpy as jnp
from jax import lax
from jax.experimental import pallas as pl
from jax.experimental.pallas import tpu as pltpu
from jax.sharding import Mesh
from jax.sharding import PartitionSpec as P

MASS = 2
RAW = 8
SWAP = [(0, 1), (1, 0)]


def swap(value, axis):
    return lax.ppermute(value, axis, SWAP)


ANY = pl.BlockSpec(memory_space=pl.ANY)
HINT = pl.CostEstimate(flops=1000, bytes_accessed=1000, transcendentals=0)


def by_time_kernel(cuts, block, *refs):
    outs = refs[-len(cuts) :]
    comps = refs[-1].shape[3]
    for k in range(comps):
        if len(block.shape) == 4:
            part = block[:, k]
        else:
            part = jnp.stack([block[n * comps + k] for n in range(block.shape[0] // comps)])
        turned = jnp.swapaxes(part, 0, 1)
        for (low, high, x, nx, y, ny), out in zip(cuts, outs):
            for i in range(nx):
                for j in range(ny):
                    out[i, 0, j, k] = turned[2 * (x + i) + y + j, low:high]


def by_time(block, cuts, *after):
    if block.ndim == 4:
        n, comps, times, sites = block.shape
        spec = pl.BlockSpec((n, comps, times // 4, sites), lambda z: (0, 0, z, 0))
    else:
        n, comps = RAW, block.shape[0] // RAW
        _, times, sites = block.shape
        spec = pl.BlockSpec((n * comps, times // 4, sites), lambda z: (0, z, 0))
    return pl.pallas_call(
        functools.partial(by_time_kernel, cuts),
        grid=(4,),
        in_specs=[spec] + [ANY] * len(after),
        out_specs=[
            pl.BlockSpec((nx, 1, ny, comps, high - low, sites), lambda z: (0, z, 0, 0, 0, 0))
            for low, high, _, nx, _, ny in cuts
        ],
        out_shape=[
            jax.ShapeDtypeStruct((nx, 4, ny, comps, high - low, sites), block.dtype)
            for low, high, _, nx, _, ny in cuts
        ],
        compiler_params=pltpu.CompilerParams(vmem_limit_bytes=(56 if n > RAW else 16) * 2**20),
        cost_estimate=HINT,
        name="by_time",
    )(block, *after)


def rows_of(block):
    x, z, yh, comps, n, sites = block.shape
    return block.reshape(x, z * yh, comps // 2, 2 * n, sites)


def front_kernel(owned, at, sols, vecs, out, lines, slab, sems):
    count, comps, rows, _ = lines.shape
    whole = pltpu.make_async_copy(
        sols.at[pl.ds(0, RAW * comps)], out.at[pl.ds(0, RAW * comps)], sems.at[count]
    )
    whole.start()
    group, time = at[0], at[1]
    copies = []
    for s in range(count):
        copies.append(
            pltpu.make_async_copy(
                vecs.at[at[2 + s] % owned, :, pl.ds(pl.multiple_of(time // rows * rows, rows), rows)],
                lines.at[s],
                sems.at[s],
            )
        )
        copies[s].start()
    row = lax.broadcasted_iota(jnp.int32, lines.shape[1:], 1)
    for s in range(count):
        copies[s].wait()
        here = jnp.where(at[2 + s] // owned == group, time % rows, -1)
        kept = jnp.sum(jnp.where(row == here, lines[s].astype(jnp.float32), 0.0), axis=1)
        slab[s] = jnp.concatenate([kept, jnp.zeros_like(kept[:2])], axis=0).astype(slab.dtype)
    last = pltpu.make_async_copy(slab, out.at[RAW * comps], sems.at[count + 1])
    last.start()
    last.wait()
    whole.wait()


def front(sols, vecs, source_index, source_time, group):
    owned, comps, times, sites = vecs.shape
    count = source_index.shape[0]
    at = jnp.concatenate([group[None], source_time, source_index])
    out = pl.pallas_call(
        functools.partial(front_kernel, owned),
        in_specs=[pl.BlockSpec(memory_space=pltpu.SMEM), ANY, ANY],
        out_specs=ANY,
        out_shape=jax.ShapeDtypeStruct((RAW * comps + 1, count, times // count, sites), sols.dtype),
        scratch_shapes=[
            pltpu.VMEM((count, comps, 16, sites), sols.dtype),
            pltpu.VMEM((count, times // count, sites), sols.dtype),
            pltpu.SemaphoreType.DMA((count + 2,)),
        ],
        compiler_params=pltpu.CompilerParams(vmem_limit_bytes=56 * 2**20),
        cost_estimate=HINT,
        name="front",
    )(at, sols.reshape(-1, count, times // count, sites), vecs)
    return out.reshape(RAW * comps + 1, times, sites)


def product(cols, own, other):
    return lax.dot_general(
        jnp.concatenate(cols, axis=0),
        jnp.concatenate([own, other], axis=0),
        (((1,), (1,)), ((), ())),
        preferred_element_type=jnp.float32,
    )


def real_imag(total, row, n):
    width = total.shape[1] // 4
    re, im = total[row : row + n], total[row + n : row + 2 * n]
    real, imag = [], []
    for left in (0, 2 * width):
        mid, right = left + width, left + 2 * width
        real.append(re[:, left:mid] + im[:, mid:right])
        imag.append(im[:, left:mid] - re[:, mid:right])
    return jnp.concatenate(real, axis=1), jnp.concatenate(imag, axis=1)


def dot_kernel(count, *refs):
    cols, (own, other), outs = refs[:count], refs[count : count + 2], refs[-count:]
    for at in range(own.shape[1]):
        total = None
        for colour in range(own.shape[2]):
            term = product(
                [col[0, at, colour] for col in cols], own[0, at, colour], other[0, at, colour]
            )
            total = term if total is None else total + term
        row = 0
        for col, out in zip(cols, outs):
            n = col.shape[3] // 2
            out[0, at, 0], out[0, at, 1] = real_imag(total, row, n)
            row += 2 * n


def pieces_kernel(count, *refs):
    total = None
    for at in range(count):
        col, own, other = refs[3 * at : 3 * at + 3]
        for colour in range(own.shape[1]):
            term = product([col[0, colour]], own[0, colour], other[0, colour])
            total = term if total is None else total + term
    out = refs[-1]
    n = out.shape[2]
    parts = real_imag(total, 0, n)
    for part in range(2):
        if len(refs) == 3 * count + 1:
            out[0, part] = parts[part]
        else:
            out[0, part] = refs[3 * count][0, part] + parts[part]


def project_pieces(pieces, before=None):
    inner, colours, n2, sites = pieces[0][0].shape
    rows = pieces[0][1].shape[2]
    spec = lambda shape: pl.BlockSpec((1,) + shape[1:], lambda j: (j, 0, 0, 0))
    args = [array for piece in pieces for array in piece]
    if before is not None:
        args.append(before)
    out = (inner, 2, n2 // 2, rows)
    return pl.pallas_call(
        functools.partial(pieces_kernel, len(pieces)),
        grid=(inner,),
        in_specs=[spec(array.shape) for array in args],
        out_specs=spec(out),
        out_shape=jax.ShapeDtypeStruct(out, jnp.float32),
        compiler_params=pltpu.CompilerParams(vmem_limit_bytes=16 * 2**20),
        cost_estimate=HINT,
        name="project_pieces",
    )(*args)


def project(cols, own, other, x, y, step, *after):
    size, inner, colours, _, sites = cols[0].shape
    rows, stride = own.shape[3], own.shape[1] // inner
    spec = lambda n, stride=1, x=0, y=0: pl.BlockSpec(
        (1, step, colours, n, sites), lambda i, j: (i + x, j * stride + y, 0, 0, 0)
    )
    in_specs = [spec(c.shape[3]) for c in cols] + [spec(rows, stride, x, y)] * 2
    in_specs += [ANY] * len(after)
    out_specs = [
        pl.BlockSpec((1, step, 2, c.shape[3] // 2, rows), lambda i, j: (i, j, 0, 0, 0))
        for c in cols
    ]
    out_shape = [
        jax.ShapeDtypeStruct((size, inner, 2, c.shape[3] // 2, rows), jnp.float32) for c in cols
    ]
    return pl.pallas_call(
        functools.partial(dot_kernel, len(cols)),
        grid=(size, inner // step),
        in_specs=in_specs,
        out_specs=out_specs,
        out_shape=out_shape,
        compiler_params=pltpu.CompilerParams(vmem_limit_bytes=48 * 2**20),
        cost_estimate=HINT,
        name="project",
    )(*cols, own, other, *after)


def pick(value, index):
    return lax.dynamic_index_in_dim(value, index, 0, keepdims=False)


def share_z(slabs):
    me = lax.axis_index("z")
    got = [
        lax.ppermute(pick(slabs, (me + k) % 4), "z", [(i, (i + k) % 4) for i in range(4)])
        for k in (1, 3, 2)
    ]
    return [pick(slabs, me), *got]


def sum_z(part):
    got = share_z(jnp.swapaxes(part, 0, 1))
    return got[0] + got[1] + got[2] + got[3]


def sum_x(part, first, size):
    me = lax.axis_index("x")
    clip = lambda i: jnp.clip(i - first, 0, size - 1)
    total = pick(part, clip(me)) if size > 1 else part[0]
    for k in (1, 3, 2):
        send = pick(part, clip((me + k) % 4)) if size > 1 else part[0]
        pairs = [(i, (i + k) % 4) for i in range(4) if first <= (i + k) % 4 < first + size]
        total = total + lax.ppermute(send, "x", pairs)
    return total


def sum_yh(part):
    me = lax.axis_index("yh")
    return pick(part, me) + swap(pick(part, 1 - me), "yh")


def local(eigvecs, solutions, source_index, source_time, dilution):
    owned, times, comps, sites = eigvecs.shape
    count = solutions.shape[1]
    nsources, spins = dilution.shape
    scale = 1.0 / math.sqrt(comps * sites * 32)
    core = lax.axis_index("c")
    group = 2 * lax.axis_index("yl") + core
    sols = solutions[0].transpose(0, 2, 1, 3)
    vecs = eigvecs.transpose(0, 2, 1, 3)

    first_part = front(sols, vecs, source_index, source_time, group)
    raw = swap(first_part, "yl")
    other = swap(vecs, "c")
    sent = [(RAW, count, x, nx, 0, 2) for x, nx in ((0, 2), (2, 1), (3, 1))]
    mine, *send = by_time(sols, ((0, count, 0, 4, 0, 2), *sent), first_part)
    got = [swap(rows_of(part), "yl") for part in send[:2]]
    shared = [part.reshape(2, comps // 2, -1, sites) for part in share_z(send[2][0])]
    got_last = [swap(part, "yl") for part in shared]

    whole = (0, owned, 0, 4, 0, 2)
    late = (0, owned, 3, 1, 0, 2)
    own, own_late = by_time(vecs, (whole, late))
    other, other_late = by_time(other, (whole, late))
    own, other = rows_of(own), rows_of(other)
    lines = raw[RAW * comps] + first_part[RAW * comps]
    raw = rows_of(by_time(raw, ((0, RAW, 0, 4, 0, 2),), other)[0])

    mine_z = share_z(own_late[0])
    theirs_z = [pick(other_late[0], lax.axis_index("z"))] + [swap(p, "c") for p in mine_z[1:]]
    pieces = [
        (s, *(v.reshape(2, comps // 2, 2 * owned, sites) for v in pair))
        for s, *pair in zip(got_last, mine_z, theirs_z)
    ]

    def rows(part):
        x, inner, _, n, lanes = part.shape
        return part.reshape(x, 4, inner // 4, 2 * n, lanes)

    def against(part, x, y, step, *after):
        return rows(project([part], own, other, x, y, step, *after)[0])

    parts = project([rows_of(mine), raw], own, other, 0, 0, 8, *shared[1:], *mine_z[1:])
    first_z = sum_z(jnp.concatenate([rows(p) for p in parts], axis=3))
    first = sum_x(first_z, 0, 4)
    mid = [against(got[0], 0, 0, 8, first, *theirs_z[1:])]
    mid.append(against(got[1], 2, 0, 4, mid[0]))
    mid = sum_x(sum_z(jnp.concatenate(mid, axis=0)), 0, 3)
    last = project_pieces(pieces[3:], project_pieces(pieces[:3]))
    last = sum_x(last.reshape(1, 2, -1, 2 * owned), 3, 1)
    late = jnp.where(lax.axis_index("x") == 3, last, mid)
    here = sum_yh(jnp.concatenate([first, late], axis=1))
    there = swap(here, "c")

    def assemble(sums, half):
        sums = sums[:, half * owned : (half + 1) * owned]
        view = lambda v: v.reshape(2, -1, owned)
        cut = [2 * count, 2 * (count + RAW)]
        away = [view(sums[cut[0] : cut[1]]), view(sums[cut[1] :])]
        return view(sums[: cut[0]]), jnp.concatenate(away, axis=1)

    h0, y0 = assemble(here, 0)
    h1, y1 = assemble(there, 1)
    tau = jnp.stack([h0, h1, y0, y1])
    order = jnp.stack([group, group ^ 1, group ^ 2, group ^ 3])
    spin_of = jnp.take(jnp.transpose(dilution), order, axis=0)
    mask = spin_of[:, None, :] == jnp.arange(spins, dtype=jnp.int32)[None, :, None]
    view = tau.reshape(4, 1, 2, MASS, nsources, count // (MASS * nsources), owned)
    picked = jnp.where(mask[:, :, None, None, :, None, None], view, 0.0)
    result = jnp.sum(picked, axis=0).reshape(spins, 2, count, owned) * scale
    result = result.transpose(3, 0, 2, 1).reshape(1, owned, spins * count * 2)

    lines = lines + swap(lines, "c")
    chosen = lines.reshape(nsources, -1, sites)[:, :comps]
    my_spins = lax.dynamic_index_in_dim(dilution, group, 1, keepdims=False)
    spin_mask = jnp.arange(spins, dtype=jnp.int32)[None, :] == my_spins[:, None]
    sources = jnp.where(
        spin_mask[:, :, None, None], chosen[:, None, :, :], jnp.zeros((), jnp.bfloat16)
    )
    return result, sources[None]


def solution(mesh):
    split = Mesh(mesh.devices.reshape(2, 2, 4, 4, 2), ("yl", "c", "z", "x", "yh"))
    grp, lat = ("yl", "c"), ("z", "x", "yh")
    return jax.shard_map(
        local,
        mesh=split,
        in_specs=(P(grp, None, None, lat), P(grp, None, None, None, lat), P(), P(), P()),
        out_specs=(P(lat, grp, None), P(grp, None, None, None, lat)),
        check_vma=False,
    )
```

```python
import functools
import math

import jax
import jax.numpy as jnp
from jax import lax
from jax.experimental import pallas as pl
from jax.experimental.pallas import tpu as pltpu
from jax.sharding import Mesh
from jax.sharding import PartitionSpec as P

MASS = 2
RAW = 8
SWAP = [(0, 1), (1, 0)]


def swap(value, axis):
    return lax.ppermute(value, axis, SWAP)


ANY = pl.BlockSpec(memory_space=pl.ANY)
HINT = pl.CostEstimate(flops=1000, bytes_accessed=1000, transcendentals=0)


def by_time_kernel(cuts, block, *refs):
    outs = refs[-len(cuts) :]
    comps = refs[-1].shape[3]
    for k in range(comps):
        if len(block.shape) == 4:
            part = block[:, k]
        else:
            part = jnp.stack([block[n * comps + k] for n in range(block.shape[0] // comps)])
        turned = jnp.swapaxes(part, 0, 1)
        for (low, high, x, nx, y, ny), out in zip(cuts, outs):
            for i in range(nx):
                for j in range(ny):
                    out[i, 0, j, k] = turned[2 * (x + i) + y + j, low:high]


def by_time(block, cuts, *after):
    if block.ndim == 4:
        n, comps, times, sites = block.shape
        spec = pl.BlockSpec((n, comps, times // 4, sites), lambda z: (0, 0, z, 0))
    else:
        n, comps = RAW, block.shape[0] // RAW
        _, times, sites = block.shape
        spec = pl.BlockSpec((n * comps, times // 4, sites), lambda z: (0, z, 0))
    return pl.pallas_call(
        functools.partial(by_time_kernel, cuts),
        grid=(4,),
        in_specs=[spec] + [ANY] * len(after),
        out_specs=[
            pl.BlockSpec((nx, 1, ny, comps, high - low, sites), lambda z: (0, z, 0, 0, 0, 0))
            for low, high, _, nx, _, ny in cuts
        ],
        out_shape=[
            jax.ShapeDtypeStruct((nx, 4, ny, comps, high - low, sites), block.dtype)
            for low, high, _, nx, _, ny in cuts
        ],
        compiler_params=pltpu.CompilerParams(vmem_limit_bytes=(56 if n > RAW else 16) * 2**20),
        cost_estimate=HINT,
        name="by_time",
    )(block, *after)


def rows_of(block):
    x, z, yh, comps, n, sites = block.shape
    return block.reshape(x, z * yh, comps // 2, 2 * n, sites)


def hold_kernel(*refs):
    pass


def hold(value, *after):
    return pl.pallas_call(
        hold_kernel,
        in_specs=[ANY] * (1 + len(after)),
        out_specs=ANY,
        out_shape=jax.ShapeDtypeStruct(value.shape, value.dtype),
        input_output_aliases={0: 0},
        cost_estimate=HINT,
        name="hold",
    )(value, *after)


def front_kernel(owned, at, sols, vecs, out, lines, slab, held, sems):
    count, comps, rows, _ = lines.shape
    group, time = at[0], at[1]
    span = held.shape[0] // 4
    part = lambda ref, i: ref.at[pl.ds(i * span, span)]
    into = [
        pltpu.make_async_copy(part(sols, i), part(held, i), sems.at[i]) for i in range(4)
    ]
    outof = [
        pltpu.make_async_copy(part(held, i), part(out, i), sems.at[4 + i]) for i in range(4)
    ]
    first = pl.multiple_of(time // rows * rows, rows)
    picks = [
        pltpu.make_async_copy(
            vecs.at[at[2 + s] % owned, :, pl.ds(first, rows)], lines.at[s], sems.at[8 + s]
        )
        for s in range(count)
    ]
    last = pltpu.make_async_copy(slab, out.at[held.shape[0]], sems.at[8 + count])
    for copy in into + picks:
        copy.start()
    for i in range(4):
        into[i].wait()
        outof[i].start()
    row = lax.broadcasted_iota(jnp.int32, lines.shape[1:], 1)
    for s in range(count):
        picks[s].wait()
        here = jnp.where(at[2 + s] // owned == group, time % rows, -1)
        kept = jnp.sum(jnp.where(row == here, lines[s].astype(jnp.float32), 0.0), axis=1)
        slab[s] = jnp.concatenate([kept, jnp.zeros_like(kept[:2])], axis=0).astype(slab.dtype)
    last.start()
    for i in range(4):
        outof[i].wait()
    last.wait()


def front(sols, vecs, source_index, source_time, group):
    owned, comps, times, sites = vecs.shape
    count = source_index.shape[0]
    at = jnp.concatenate([group[None], source_time, source_index])
    out = pl.pallas_call(
        functools.partial(front_kernel, owned),
        in_specs=[pl.BlockSpec(memory_space=pltpu.SMEM), ANY, ANY],
        out_specs=ANY,
        out_shape=jax.ShapeDtypeStruct((RAW * comps + 1, count, times // count, sites), sols.dtype),
        scratch_shapes=[
            pltpu.VMEM((count, comps, 16, sites), sols.dtype),
            pltpu.VMEM((count, times // count, sites), sols.dtype),
            pltpu.VMEM((RAW * comps, count, times // count, sites), sols.dtype),
            pltpu.SemaphoreType.DMA((9 + count,)),
        ],
        compiler_params=pltpu.CompilerParams(vmem_limit_bytes=56 * 2**20),
        cost_estimate=HINT,
        name="front",
    )(at, sols.reshape(-1, count, times // count, sites), vecs)
    return out.reshape(RAW * comps + 1, times, sites)


def product(cols, own, other):
    return lax.dot_general(
        jnp.concatenate(cols, axis=0),
        jnp.concatenate([own, other], axis=0),
        (((1,), (1,)), ((), ())),
        preferred_element_type=jnp.float32,
    )


def real_imag(total, row, n):
    width = total.shape[1] // 4
    re, im = total[row : row + n], total[row + n : row + 2 * n]
    real, imag = [], []
    for left in (0, 2 * width):
        mid, right = left + width, left + 2 * width
        real.append(re[:, left:mid] + im[:, mid:right])
        imag.append(im[:, left:mid] - re[:, mid:right])
    return jnp.concatenate(real, axis=1), jnp.concatenate(imag, axis=1)


def dot_kernel(count, *refs):
    cols, (own, other), outs = refs[:count], refs[count : count + 2], refs[-count:]
    for at in range(own.shape[1]):
        total = None
        for colour in range(own.shape[2]):
            term = product(
                [col[0, at, colour] for col in cols], own[0, at, colour], other[0, at, colour]
            )
            total = term if total is None else total + term
        row = 0
        for col, out in zip(cols, outs):
            n = col.shape[3] // 2
            out[0, at, 0], out[0, at, 1] = real_imag(total, row, n)
            row += 2 * n


def pieces_kernel(count, *refs):
    total = None
    for at in range(count):
        col, own, other = refs[3 * at : 3 * at + 3]
        for colour in range(own.shape[1]):
            term = product([col[0, colour]], own[0, colour], other[0, colour])
            total = term if total is None else total + term
    out = refs[-1]
    n = out.shape[2]
    parts = real_imag(total, 0, n)
    for part in range(2):
        if len(refs) == 3 * count + 1:
            out[0, part] = parts[part]
        else:
            out[0, part] = refs[3 * count][0, part] + parts[part]


def project_pieces(pieces, before=None):
    inner, colours, n2, sites = pieces[0][0].shape
    rows = pieces[0][1].shape[2]
    spec = lambda shape: pl.BlockSpec((1,) + shape[1:], lambda j: (j, 0, 0, 0))
    args = [array for piece in pieces for array in piece]
    if before is not None:
        args.append(before)
    out = (inner, 2, n2 // 2, rows)
    return pl.pallas_call(
        functools.partial(pieces_kernel, len(pieces)),
        grid=(inner,),
        in_specs=[spec(array.shape) for array in args],
        out_specs=spec(out),
        out_shape=jax.ShapeDtypeStruct(out, jnp.float32),
        compiler_params=pltpu.CompilerParams(vmem_limit_bytes=16 * 2**20),
        cost_estimate=HINT,
        name="project_pieces",
    )(*args)


def project(cols, own, other, x, y, step, *after):
    size, inner, colours, _, sites = cols[0].shape
    rows, stride = own.shape[3], own.shape[1] // inner
    spec = lambda n, stride=1, x=0, y=0: pl.BlockSpec(
        (1, step, colours, n, sites), lambda i, j: (i + x, j * stride + y, 0, 0, 0)
    )
    in_specs = [spec(c.shape[3]) for c in cols] + [spec(rows, stride, x, y)] * 2
    in_specs += [ANY] * len(after)
    out_specs = [
        pl.BlockSpec((1, step, 2, c.shape[3] // 2, rows), lambda i, j: (i, j, 0, 0, 0))
        for c in cols
    ]
    out_shape = [
        jax.ShapeDtypeStruct((size, inner, 2, c.shape[3] // 2, rows), jnp.float32) for c in cols
    ]
    return pl.pallas_call(
        functools.partial(dot_kernel, len(cols)),
        grid=(size, inner // step),
        in_specs=in_specs,
        out_specs=out_specs,
        out_shape=out_shape,
        compiler_params=pltpu.CompilerParams(vmem_limit_bytes=48 * 2**20),
        cost_estimate=HINT,
        name="project",
    )(*cols, own, other, *after)


def pick(value, index):
    return lax.dynamic_index_in_dim(value, index, 0, keepdims=False)


def share_z(slabs):
    me = lax.axis_index("z")
    got = [
        lax.ppermute(pick(slabs, (me + k) % 4), "z", [(i, (i + k) % 4) for i in range(4)])
        for k in (1, 3, 2)
    ]
    return [pick(slabs, me), *got]


def sum_z(part):
    got = share_z(jnp.swapaxes(part, 0, 1))
    return got[0] + got[1] + got[2] + got[3]


def sum_x(part, first, size):
    me = lax.axis_index("x")
    clip = lambda i: jnp.clip(i - first, 0, size - 1)
    total = pick(part, clip(me)) if size > 1 else part[0]
    for k in (1, 3, 2):
        send = pick(part, clip((me + k) % 4)) if size > 1 else part[0]
        pairs = [(i, (i + k) % 4) for i in range(4) if first <= (i + k) % 4 < first + size]
        total = total + lax.ppermute(send, "x", pairs)
    return total


def sum_yh(part):
    me = lax.axis_index("yh")
    return pick(part, me) + swap(pick(part, 1 - me), "yh")


def local(eigvecs, solutions, source_index, source_time, dilution):
    owned, times, comps, sites = eigvecs.shape
    count = solutions.shape[1]
    nsources, spins = dilution.shape
    scale = 1.0 / math.sqrt(comps * sites * 32)
    core = lax.axis_index("c")
    group = 2 * lax.axis_index("yl") + core
    sols = solutions[0].transpose(0, 2, 1, 3)
    vecs = eigvecs.transpose(0, 2, 1, 3)

    first_part = front(sols, vecs, source_index, source_time, group)
    raw = swap(first_part, "yl")
    other = swap(vecs, "c")
    sent = [(RAW, count, x, nx, 0, 2) for x, nx in ((0, 2), (2, 1), (3, 1))]
    mine, *send = by_time(sols, ((0, count, 0, 4, 0, 2), *sent), first_part)
    send = [rows_of(part) for part in send]
    shared = share_z(send[2].reshape(4, 2, comps // 2, -1, sites))

    whole = (0, owned, 0, 4, 0, 2)
    late = (0, owned, 3, 1, 0, 2)
    own, own_late = by_time(vecs, (whole, late))
    other, other_late = by_time(other, (whole, late))
    own, other = rows_of(own), rows_of(other)
    got = [swap(send[0], "yl"), swap(hold(send[1], raw, own, other), "yl")]
    lines = raw[RAW * comps] + first_part[RAW * comps]
    raw = rows_of(by_time(raw, ((0, RAW, 0, 4, 0, 2),), other)[0])

    def rows(part):
        x, inner, _, n, lanes = part.shape
        return part.reshape(x, 4, inner // 4, 2 * n, lanes)

    def against(part, x, y, step, *after):
        return rows(project([part], own, other, x, y, step, *after)[0])

    parts = project([rows_of(mine), raw], own, other, 0, 0, 8)
    first_z = sum_z(jnp.concatenate([rows(p) for p in parts], axis=3))
    first = sum_x(first_z, 0, 4)
    most = swap(hold(jnp.concatenate(shared[:3]), got[0], first), "yl")
    rest = swap(hold(shared[3], got[1]), "yl")
    got_last = [most[:2], most[2:4], most[4:], rest]

    mine_z = share_z(own_late[0])
    theirs_z = [pick(other_late[0], lax.axis_index("z"))] + [swap(p, "c") for p in mine_z[1:]]
    pieces = [
        (s, *(v.reshape(2, comps // 2, 2 * owned, sites) for v in pair))
        for s, *pair in zip(got_last, mine_z, theirs_z)
    ]

    mid = [against(got[0], 0, 0, 8, first)]
    mid.append(against(got[1], 2, 0, 4, mid[0], *theirs_z[1:]))
    mid = sum_x(sum_z(jnp.concatenate(mid, axis=0)), 0, 3)
    last = project_pieces(pieces[3:], project_pieces(pieces[:3]))
    last = sum_x(last.reshape(1, 2, -1, 2 * owned), 3, 1)
    late = jnp.where(lax.axis_index("x") == 3, last, mid)
    here = sum_yh(jnp.concatenate([first, late], axis=1))
    there = swap(here, "c")

    def assemble(sums, half):
        sums = sums[:, half * owned : (half + 1) * owned]
        view = lambda v: v.reshape(2, -1, owned)
        cut = [2 * count, 2 * (count + RAW)]
        away = [view(sums[cut[0] : cut[1]]), view(sums[cut[1] :])]
        return view(sums[: cut[0]]), jnp.concatenate(away, axis=1)

    h0, y0 = assemble(here, 0)
    h1, y1 = assemble(there, 1)
    tau = jnp.stack([h0, h1, y0, y1])
    order = jnp.stack([group, group ^ 1, group ^ 2, group ^ 3])
    spin_of = jnp.take(jnp.transpose(dilution), order, axis=0)
    mask = spin_of[:, None, :] == jnp.arange(spins, dtype=jnp.int32)[None, :, None]
    view = tau.reshape(4, 1, 2, MASS, nsources, count // (MASS * nsources), owned)
    picked = jnp.where(mask[:, :, None, None, :, None, None], view, 0.0)
    result = jnp.sum(picked, axis=0).reshape(spins, 2, count, owned) * scale
    result = result.transpose(3, 0, 2, 1).reshape(1, owned, spins * count * 2)

    lines = lines + swap(lines, "c")
    chosen = lines.reshape(nsources, -1, sites)[:, :comps]
    my_spins = lax.dynamic_index_in_dim(dilution, group, 1, keepdims=False)
    spin_mask = jnp.arange(spins, dtype=jnp.int32)[None, :] == my_spins[:, None]
    sources = jnp.where(
        spin_mask[:, :, None, None], chosen[:, None, :, :], jnp.zeros((), jnp.bfloat16)
    )
    return result, sources[None]


def solution(mesh):
    split = Mesh(mesh.devices.reshape(2, 2, 4, 4, 2), ("yl", "c", "z", "x", "yh"))
    grp, lat = ("yl", "c"), ("z", "x", "yh")
    return jax.shard_map(
        local,
        mesh=split,
        in_specs=(P(grp, None, None, lat), P(grp, None, None, None, lat), P(), P(), P()),
        out_specs=(P(lat, grp, None), P(grp, None, None, None, lat)),
        check_vma=False,
    )
```

```python
import functools
import math

import jax
import jax.numpy as jnp
from jax import lax
from jax.experimental import pallas as pl
from jax.experimental.pallas import tpu as pltpu
from jax.sharding import Mesh
from jax.sharding import PartitionSpec as P

MASS = 2
RAW = 8
SWAP = [(0, 1), (1, 0)]


def swap(value, axis):
    return lax.ppermute(value, axis, SWAP)


ANY = pl.BlockSpec(memory_space=pl.ANY)
HINT = pl.CostEstimate(flops=1000, bytes_accessed=1000, transcendentals=0)


def by_time_kernel(cuts, block, *refs):
    outs = refs[-len(cuts) :]
    comps = refs[-1].shape[3]
    for k in range(comps):
        if len(block.shape) == 4:
            part = block[:, k]
        else:
            part = jnp.stack([block[n * comps + k] for n in range(block.shape[0] // comps)])
        turned = jnp.swapaxes(part, 0, 1)
        for (low, high, x, nx, y, ny), out in zip(cuts, outs):
            for i in range(nx):
                for j in range(ny):
                    out[i, 0, j, k] = turned[2 * (x + i) + y + j, low:high]


def by_time(block, cuts, *after):
    if block.ndim == 4:
        n, comps, times, sites = block.shape
        spec = pl.BlockSpec((n, comps, times // 4, sites), lambda z: (0, 0, z, 0))
    else:
        n, comps = RAW, block.shape[0] // RAW
        _, times, sites = block.shape
        spec = pl.BlockSpec((n * comps, times // 4, sites), lambda z: (0, z, 0))
    return pl.pallas_call(
        functools.partial(by_time_kernel, cuts),
        grid=(4,),
        in_specs=[spec] + [ANY] * len(after),
        out_specs=[
            pl.BlockSpec((nx, 1, ny, comps, high - low, sites), lambda z: (0, z, 0, 0, 0, 0))
            for low, high, _, nx, _, ny in cuts
        ],
        out_shape=[
            jax.ShapeDtypeStruct((nx, 4, ny, comps, high - low, sites), block.dtype)
            for low, high, _, nx, _, ny in cuts
        ],
        compiler_params=pltpu.CompilerParams(vmem_limit_bytes=(56 if n > RAW else 16) * 2**20),
        cost_estimate=HINT,
        name="by_time",
    )(block, *after)


def rows_of(block):
    x, z, yh, comps, n, sites = block.shape
    return block.reshape(x, z * yh, comps // 2, 2 * n, sites)


def mark(value):
    while value.ndim > 2:
        value = value[0]
    return value


def hold_kernel(*refs):
    pass


def hold(value, *after):
    return pl.pallas_call(
        hold_kernel,
        in_specs=[ANY] * (1 + len(after)),
        out_specs=ANY,
        out_shape=jax.ShapeDtypeStruct(value.shape, value.dtype),
        input_output_aliases={0: 0},
        cost_estimate=HINT,
        name="hold",
    )(value, *map(mark, after))


def front_kernel(owned, at, sols, vecs, out, lines, slab, held, sems):
    count, comps, rows, _ = lines.shape
    group, time = at[0], at[1]
    span = held.shape[0] // 4
    part = lambda ref, i: ref.at[pl.ds(i * span, span)]
    into = [
        pltpu.make_async_copy(part(sols, i), part(held, i), sems.at[i]) for i in range(4)
    ]
    outof = [
        pltpu.make_async_copy(part(held, i), part(out, i), sems.at[4 + i]) for i in range(4)
    ]
    first = pl.multiple_of(time // rows * rows, rows)
    picks = [
        pltpu.make_async_copy(
            vecs.at[at[2 + s] % owned, :, pl.ds(first, rows)], lines.at[s], sems.at[8 + s]
        )
        for s in range(count)
    ]
    last = pltpu.make_async_copy(slab, out.at[held.shape[0]], sems.at[8 + count])
    for copy in into + picks:
        copy.start()
    for i in range(4):
        into[i].wait()
        outof[i].start()
    row = lax.broadcasted_iota(jnp.int32, lines.shape[1:], 1)
    for s in range(count):
        picks[s].wait()
        here = jnp.where(at[2 + s] // owned == group, time % rows, -1)
        kept = jnp.sum(jnp.where(row == here, lines[s].astype(jnp.float32), 0.0), axis=1)
        slab[s] = jnp.concatenate([kept, jnp.zeros_like(kept[:2])], axis=0).astype(slab.dtype)
    last.start()
    for i in range(4):
        outof[i].wait()
    last.wait()


def front(sols, vecs, source_index, source_time, group):
    owned, comps, times, sites = vecs.shape
    count = source_index.shape[0]
    at = jnp.concatenate([group[None], source_time, source_index])
    out = pl.pallas_call(
        functools.partial(front_kernel, owned),
        in_specs=[pl.BlockSpec(memory_space=pltpu.SMEM), ANY, ANY],
        out_specs=ANY,
        out_shape=jax.ShapeDtypeStruct((RAW * comps + 1, count, times // count, sites), sols.dtype),
        scratch_shapes=[
            pltpu.VMEM((count, comps, 16, sites), sols.dtype),
            pltpu.VMEM((count, times // count, sites), sols.dtype),
            pltpu.VMEM((RAW * comps, count, times // count, sites), sols.dtype),
            pltpu.SemaphoreType.DMA((9 + count,)),
        ],
        compiler_params=pltpu.CompilerParams(vmem_limit_bytes=56 * 2**20),
        cost_estimate=HINT,
        name="front",
    )(at, sols.reshape(-1, count, times // count, sites), vecs)
    return out.reshape(RAW * comps + 1, times, sites)


def product(cols, own, other):
    return lax.dot_general(
        jnp.concatenate(cols, axis=0),
        jnp.concatenate([own, other], axis=0),
        (((1,), (1,)), ((), ())),
        preferred_element_type=jnp.float32,
    )


def real_imag(total, row, n):
    width = total.shape[1] // 4
    re, im = total[row : row + n], total[row + n : row + 2 * n]
    real, imag = [], []
    for left in (0, 2 * width):
        mid, right = left + width, left + 2 * width
        real.append(re[:, left:mid] + im[:, mid:right])
        imag.append(im[:, left:mid] - re[:, mid:right])
    return jnp.concatenate(real, axis=1), jnp.concatenate(imag, axis=1)


def dot_kernel(count, *refs):
    cols, (own, other), outs = refs[:count], refs[count : count + 2], refs[-count:]
    for at in range(own.shape[1]):
        total = None
        for colour in range(own.shape[2]):
            term = product(
                [col[0, at, colour] for col in cols], own[0, at, colour], other[0, at, colour]
            )
            total = term if total is None else total + term
        row = 0
        for col, out in zip(cols, outs):
            n = col.shape[3] // 2
            out[0, at, 0], out[0, at, 1] = real_imag(total, row, n)
            row += 2 * n


def pieces_kernel(col, own, other, out):
    total = None
    for colour in range(own.shape[1]):
        term = product([col[0, colour]], own[0, colour], other[0, colour])
        total = term if total is None else total + term
    here = pl.program_id(0)
    for part, value in enumerate(real_imag(total, 0, out.shape[1])):
        out[part] = jnp.where(here == 0, value, out[part] + value)


def project_pieces(cols, own, other, *after):
    count, _, n2, _ = cols.shape
    rows = own.shape[2]
    spec = lambda v: pl.BlockSpec((1,) + v.shape[1:], lambda i: (i, 0, 0, 0))
    return pl.pallas_call(
        pieces_kernel,
        grid=(count,),
        in_specs=[spec(cols), spec(own), spec(other)] + [ANY] * len(after),
        out_specs=pl.BlockSpec((2, n2 // 2, rows), lambda i: (0, 0, 0)),
        out_shape=jax.ShapeDtypeStruct((2, n2 // 2, rows), jnp.float32),
        compiler_params=pltpu.CompilerParams(vmem_limit_bytes=16 * 2**20),
        cost_estimate=HINT,
        name="project_pieces",
    )(cols, own, other, *after)


def project(cols, own, other, x, y, step, *after):
    size, inner, colours, _, sites = cols[0].shape
    rows, stride = own.shape[3], own.shape[1] // inner
    spec = lambda n, stride=1, x=0, y=0: pl.BlockSpec(
        (1, step, colours, n, sites), lambda i, j: (i + x, j * stride + y, 0, 0, 0)
    )
    in_specs = [spec(c.shape[3]) for c in cols] + [spec(rows, stride, x, y)] * 2
    in_specs += [ANY] * len(after)
    out_specs = [
        pl.BlockSpec((1, step, 2, c.shape[3] // 2, rows), lambda i, j: (i, j, 0, 0, 0))
        for c in cols
    ]
    out_shape = [
        jax.ShapeDtypeStruct((size, inner, 2, c.shape[3] // 2, rows), jnp.float32) for c in cols
    ]
    return pl.pallas_call(
        functools.partial(dot_kernel, len(cols)),
        grid=(size, inner // step),
        in_specs=in_specs,
        out_specs=out_specs,
        out_shape=out_shape,
        compiler_params=pltpu.CompilerParams(vmem_limit_bytes=(60 if size == 4 else 40) * 2**20),
        cost_estimate=HINT,
        name="project",
    )(*cols, own, other, *after)


def pick(value, index):
    return lax.dynamic_index_in_dim(value, index, 0, keepdims=False)


def share_z(slabs):
    me = lax.axis_index("z")
    got = [
        lax.ppermute(pick(slabs, (me + k) % 4), "z", [(i, (i + k) % 4) for i in range(4)])
        for k in (1, 3, 2)
    ]
    return [pick(slabs, me), *got]


def sum_z(slabs):
    got = share_z(slabs)
    return got[0] + got[1] + got[2] + got[3]


def sum_x(slabs):
    me = lax.axis_index("x")
    total = pick(slabs, me)
    for k in (1, 3, 2):
        pairs = [(i, (i + k) % 4) for i in range(4)]
        total = total + lax.ppermute(pick(slabs, (me + k) % 4), "x", pairs)
    return total


def sum_yh(part):
    me = lax.axis_index("yh")
    return pick(part, me) + swap(pick(part, 1 - me), "yh")


def local(eigvecs, solutions, source_index, source_time, dilution):
    owned, times, comps, sites = eigvecs.shape
    count = solutions.shape[1]
    nsources, spins = dilution.shape
    scale = 1.0 / math.sqrt(comps * sites * 32)
    core = lax.axis_index("c")
    group = 2 * lax.axis_index("yl") + core
    sols = solutions[0].transpose(0, 2, 1, 3)
    vecs = eigvecs.transpose(0, 2, 1, 3)

    first_part = front(sols, vecs, source_index, source_time, group)
    raw = swap(first_part, "yl")
    other = swap(vecs, "c")
    parts = ((0, 1, 0, 2), (1, 1, 0, 2), (2, 1, 0, 2), (3, 1, 0, 1), (3, 1, 1, 1))
    sent = [(RAW, count, *part) for part in parts]
    mine, *send = by_time(sols, ((0, count, 0, 4, 0, 2), *sent), mark(first_part))
    send = [rows_of(part) for part in send]
    got = [swap(send[0], "yl"), swap(hold(send[1], raw), "yl")]
    got += [swap(hold(send[2], got[0]), "yl"), swap(hold(send[3], got[1]), "yl")]

    whole, late = (0, owned, 0, 4, 0, 2), (0, owned, 3, 1, 1, 1)
    own, own_late = by_time(vecs, (whole, late), mark(send[0]))
    other = by_time(other, (whole,))[0]
    own, other = rows_of(own), rows_of(other)
    lines = raw[RAW * comps] + first_part[RAW * comps]
    lines = lines + swap(lines, "c")
    raw_rows = rows_of(by_time(raw, ((0, RAW, 0, 4, 0, 2),), mark(other), lines)[0])

    def against(part, x, y, step, *after):
        out = project([part], own, other, x, y, step, *map(mark, after))[0]
        return out.reshape(out.shape[0], 4, -1, 2 * (count - RAW), 2 * owned)

    slabs = [v.reshape(4, comps // 2, -1, sites) for v in (send[4], own_late)]
    spread = jnp.stack(share_z(hold(jnp.concatenate(slabs, axis=2), raw)))
    cut = send[4].shape[3]
    spread_s, spread_v = spread[:, :, :cut], spread[:, :, cut:]
    spread_w = swap(spread_v, "c")

    first = project([rows_of(mine), raw_rows], own, other, 0, 0, 8)
    first = [v.reshape(4, 4, 2, -1, 2 * owned) for v in first]
    first = sum_x(jnp.concatenate(first, axis=3))
    first = sum_z(hold(first, spread_v))

    early = [against(got[0], 0, 0, 4, first), against(got[1], 1, 0, 4, first, spread_w)]
    early = sum_z(jnp.concatenate([v[0] for v in early], axis=1))
    mid = [against(got[2], 2, 0, 4, early)[0]]
    got.append(swap(hold(spread_s, mid[0]), "yl"))
    mid.append(against(got[3], 3, 0, 1, mid[0])[0])
    mid = sum_z(jnp.concatenate(mid, axis=1))
    last = project_pieces(got[4], spread_v, spread_w)
    last = last.reshape(1, -1, 2 * owned)
    late = sum_x(jnp.concatenate([early, mid, last]).reshape(4, 2, -1, 2 * owned))

    here = sum_yh(jnp.concatenate([first, late], axis=1))
    there = swap(here, "c")

    def assemble(sums, half):
        sums = sums[:, half * owned : (half + 1) * owned]
        view = lambda v: v.reshape(2, -1, owned)
        cut = [2 * count, 2 * (count + RAW)]
        away = [view(sums[cut[0] : cut[1]]), view(sums[cut[1] :])]
        return view(sums[: cut[0]]), jnp.concatenate(away, axis=1)

    h0, y0 = assemble(here, 0)
    h1, y1 = assemble(there, 1)
    tau = jnp.stack([h0, h1, y0, y1])
    order = jnp.stack([group, group ^ 1, group ^ 2, group ^ 3])
    spin_of = jnp.take(jnp.transpose(dilution), order, axis=0)
    mask = spin_of[:, None, :] == jnp.arange(spins, dtype=jnp.int32)[None, :, None]
    view = tau.reshape(4, 1, 2, MASS, nsources, count // (MASS * nsources), owned)
    picked = jnp.where(mask[:, :, None, None, :, None, None], view, 0.0)
    result = jnp.sum(picked, axis=0).reshape(spins, 2, count, owned) * scale
    result = result.transpose(3, 0, 2, 1).reshape(1, owned, spins * count * 2)

    chosen = lines.reshape(nsources, -1, sites)[:, :comps]
    my_spins = lax.dynamic_index_in_dim(dilution, group, 1, keepdims=False)
    spin_mask = jnp.arange(spins, dtype=jnp.int32)[None, :] == my_spins[:, None]
    sources = jnp.where(
        spin_mask[:, :, None, None], chosen[:, None, :, :], jnp.zeros((), jnp.bfloat16)
    )
    return result, sources[None]


def solution(mesh):
    split = Mesh(mesh.devices.reshape(2, 2, 4, 4, 2), ("yl", "c", "z", "x", "yh"))
    grp, lat = ("yl", "c"), ("z", "x", "yh")
    return jax.shard_map(
        local,
        mesh=split,
        in_specs=(P(grp, None, None, lat), P(grp, None, None, None, lat), P(), P(), P()),
        out_specs=(P(lat, grp, None), P(grp, None, None, None, lat)),
        check_vma=False,
    )
```

```python
import functools
import math

import jax
import jax.numpy as jnp
from jax import lax
from jax.experimental import pallas as pl
from jax.experimental.pallas import tpu as pltpu
from jax.sharding import Mesh
from jax.sharding import PartitionSpec as P

MASS = 2
RAW = 8
SWAP = [(0, 1), (1, 0)]


def swap(value, axis):
    return lax.ppermute(value, axis, SWAP)


ANY = pl.BlockSpec(memory_space=pl.ANY)
HINT = pl.CostEstimate(flops=1000, bytes_accessed=1000, transcendentals=0)


def by_time_kernel(cuts, block, *refs):
    outs = refs[-len(cuts) :]
    comps = refs[-1].shape[3]
    for k in range(comps):
        if len(block.shape) == 4:
            part = block[:, k]
        else:
            part = jnp.stack([block[n * comps + k] for n in range(block.shape[0] // comps)])
        turned = jnp.swapaxes(part, 0, 1)
        for (low, high, x, nx, y, ny), out in zip(cuts, outs):
            for i in range(nx):
                for j in range(ny):
                    out[i, 0, j, k] = turned[2 * (x + i) + y + j, low:high]


def by_time(block, cuts, *after):
    if block.ndim == 4:
        n, comps, times, sites = block.shape
        spec = pl.BlockSpec((n, comps, times // 4, sites), lambda z: (0, 0, z, 0))
    else:
        n, comps = RAW, block.shape[0] // RAW
        _, times, sites = block.shape
        spec = pl.BlockSpec((n * comps, times // 4, sites), lambda z: (0, z, 0))
    return pl.pallas_call(
        functools.partial(by_time_kernel, cuts),
        grid=(4,),
        in_specs=[spec] + [ANY] * len(after),
        out_specs=[
            pl.BlockSpec((nx, 1, ny, comps, high - low, sites), lambda z: (0, z, 0, 0, 0, 0))
            for low, high, _, nx, _, ny in cuts
        ],
        out_shape=[
            jax.ShapeDtypeStruct((nx, 4, ny, comps, high - low, sites), block.dtype)
            for low, high, _, nx, _, ny in cuts
        ],
        compiler_params=pltpu.CompilerParams(vmem_limit_bytes=(56 if n > RAW else 16) * 2**20),
        cost_estimate=HINT,
        name="by_time",
    )(block, *after)


def rows_of(block):
    x, z, yh, comps, n, sites = block.shape
    return block.reshape(x, z * yh, comps // 2, 2 * n, sites)


def mark(value):
    while value.ndim > 2:
        value = value[0]
    return value


def hold_kernel(*refs):
    pass


def hold(value, *after):
    return pl.pallas_call(
        hold_kernel,
        in_specs=[ANY] * (1 + len(after)),
        out_specs=ANY,
        out_shape=jax.ShapeDtypeStruct(value.shape, value.dtype),
        input_output_aliases={0: 0},
        cost_estimate=HINT,
        name="hold",
    )(value, *map(mark, after))


def front_kernel(owned, at, sols, vecs, out, lines, slab, held, sems):
    count, comps, rows, _ = lines.shape
    group, time = at[0], at[1]
    span = held.shape[0] // 4
    part = lambda ref, i: ref.at[pl.ds(i * span, span)]
    into = [
        pltpu.make_async_copy(part(sols, i), part(held, i), sems.at[i]) for i in range(4)
    ]
    outof = [
        pltpu.make_async_copy(part(held, i), part(out, i), sems.at[4 + i]) for i in range(4)
    ]
    first = pl.multiple_of(time // rows * rows, rows)
    picks = [
        pltpu.make_async_copy(
            vecs.at[at[2 + s] % owned, :, pl.ds(first, rows)], lines.at[s], sems.at[8 + s]
        )
        for s in range(count)
    ]
    last = pltpu.make_async_copy(slab, out.at[held.shape[0]], sems.at[8 + count])
    for copy in into + picks:
        copy.start()
    for i in range(4):
        into[i].wait()
        outof[i].start()
    row = lax.broadcasted_iota(jnp.int32, lines.shape[1:], 1)
    for s in range(count):
        picks[s].wait()
        here = jnp.where(at[2 + s] // owned == group, time % rows, -1)
        kept = jnp.sum(jnp.where(row == here, lines[s].astype(jnp.float32), 0.0), axis=1)
        slab[s] = jnp.concatenate([kept, jnp.zeros_like(kept[:2])], axis=0).astype(slab.dtype)
    last.start()
    for i in range(4):
        outof[i].wait()
    last.wait()


def front(sols, vecs, source_index, source_time, group):
    owned, comps, times, sites = vecs.shape
    count = source_index.shape[0]
    at = jnp.concatenate([group[None], source_time, source_index])
    out = pl.pallas_call(
        functools.partial(front_kernel, owned),
        in_specs=[pl.BlockSpec(memory_space=pltpu.SMEM), ANY, ANY],
        out_specs=ANY,
        out_shape=jax.ShapeDtypeStruct((RAW * comps + 1, count, times // count, sites), sols.dtype),
        scratch_shapes=[
            pltpu.VMEM((count, comps, 16, sites), sols.dtype),
            pltpu.VMEM((count, times // count, sites), sols.dtype),
            pltpu.VMEM((RAW * comps, count, times // count, sites), sols.dtype),
            pltpu.SemaphoreType.DMA((9 + count,)),
        ],
        compiler_params=pltpu.CompilerParams(vmem_limit_bytes=56 * 2**20),
        cost_estimate=HINT,
        name="front",
    )(at, sols.reshape(-1, count, times // count, sites), vecs)
    return out.reshape(RAW * comps + 1, times, sites)


def product(cols, own, other):
    return lax.dot_general(
        jnp.concatenate(cols, axis=0),
        jnp.concatenate([own, other], axis=0),
        (((1,), (1,)), ((), ())),
        preferred_element_type=jnp.float32,
    )


def real_imag(total, row, n):
    width = total.shape[1] // 4
    re, im = total[row : row + n], total[row + n : row + 2 * n]
    real, imag = [], []
    for left in (0, 2 * width):
        mid, right = left + width, left + 2 * width
        real.append(re[:, left:mid] + im[:, mid:right])
        imag.append(im[:, left:mid] - re[:, mid:right])
    return jnp.concatenate(real, axis=1), jnp.concatenate(imag, axis=1)


def dot_kernel(count, *refs):
    cols, (own, other), outs = refs[:count], refs[count : count + 2], refs[-count:]
    for at in range(own.shape[1]):
        total = None
        for colour in range(own.shape[2]):
            term = product(
                [col[0, at, colour] for col in cols], own[0, at, colour], other[0, at, colour]
            )
            total = term if total is None else total + term
        row = 0
        for col, out in zip(cols, outs):
            n = col.shape[3] // 2
            out[0, at, 0], out[0, at, 1] = real_imag(total, row, n)
            row += 2 * n


def pieces_kernel(col, own, other, out):
    total = None
    for colour in range(own.shape[1]):
        term = product([col[0, colour]], own[0, colour], other[0, colour])
        total = term if total is None else total + term
    here = pl.program_id(0)
    for part, value in enumerate(real_imag(total, 0, out.shape[1])):
        out[part] = jnp.where(here == 0, value, out[part] + value)


def project_pieces(cols, own, other, *after):
    count, _, n2, _ = cols.shape
    rows = own.shape[2]
    spec = lambda v: pl.BlockSpec((1,) + v.shape[1:], lambda i: (i, 0, 0, 0))
    return pl.pallas_call(
        pieces_kernel,
        grid=(count,),
        in_specs=[spec(cols), spec(own), spec(other)] + [ANY] * len(after),
        out_specs=pl.BlockSpec((2, n2 // 2, rows), lambda i: (0, 0, 0)),
        out_shape=jax.ShapeDtypeStruct((2, n2 // 2, rows), jnp.float32),
        compiler_params=pltpu.CompilerParams(vmem_limit_bytes=16 * 2**20),
        cost_estimate=HINT,
        name="project_pieces",
    )(cols, own, other, *after)


def project(cols, own, other, x, y, step, *after):
    size, inner, colours, _, sites = cols[0].shape
    rows, stride = own.shape[3], own.shape[1] // inner
    spec = lambda n, stride=1, x=0, y=0: pl.BlockSpec(
        (1, step, colours, n, sites), lambda i, j: (i + x, j * stride + y, 0, 0, 0)
    )
    in_specs = [spec(c.shape[3]) for c in cols] + [spec(rows, stride, x, y)] * 2
    in_specs += [ANY] * len(after)
    out_specs = [
        pl.BlockSpec((1, step, 2, c.shape[3] // 2, rows), lambda i, j: (i, j, 0, 0, 0))
        for c in cols
    ]
    out_shape = [
        jax.ShapeDtypeStruct((size, inner, 2, c.shape[3] // 2, rows), jnp.float32) for c in cols
    ]
    return pl.pallas_call(
        functools.partial(dot_kernel, len(cols)),
        grid=(size, inner // step),
        in_specs=in_specs,
        out_specs=out_specs,
        out_shape=out_shape,
        compiler_params=pltpu.CompilerParams(vmem_limit_bytes=60 * 2**20),
        cost_estimate=HINT,
        name="project",
    )(*cols, own, other, *after)


def pick(value, index):
    return lax.dynamic_index_in_dim(value, index, 0, keepdims=False)


def share_z(slabs):
    me = lax.axis_index("z")
    got = [
        lax.ppermute(pick(slabs, (me + k) % 4), "z", [(i, (i + k) % 4) for i in range(4)])
        for k in (1, 3, 2)
    ]
    return [pick(slabs, me), *got]


def sum_z(slabs):
    got = share_z(slabs)
    return got[0] + got[1] + got[2] + got[3]


def sum_x(slabs):
    me = lax.axis_index("x")
    total = pick(slabs, me)
    for k in (1, 3, 2):
        pairs = [(i, (i + k) % 4) for i in range(4)]
        total = total + lax.ppermute(pick(slabs, (me + k) % 4), "x", pairs)
    return total


def sum_yh(part):
    me = lax.axis_index("yh")
    return pick(part, me) + swap(pick(part, 1 - me), "yh")


def local(eigvecs, solutions, source_index, source_time, dilution):
    owned, times, comps, sites = eigvecs.shape
    count = solutions.shape[1]
    nsources, spins = dilution.shape
    scale = 1.0 / math.sqrt(comps * sites * 32)
    core = lax.axis_index("c")
    group = 2 * lax.axis_index("yl") + core
    sols = solutions[0].transpose(0, 2, 1, 3)
    vecs = eigvecs.transpose(0, 2, 1, 3)

    first_part = front(sols, vecs, source_index, source_time, group)
    raw = swap(first_part, "yl")
    other = swap(vecs, "c")
    parts = ((0, 2, 0, 2), (2, 1, 0, 2), (3, 1, 0, 1), (3, 1, 1, 1))
    sent = [(RAW, count, *part) for part in parts]
    mine, *send = by_time(sols, ((0, count, 0, 4, 0, 2), *sent), mark(first_part))
    send = [rows_of(part) for part in send]
    got = [swap(send[0], "yl"), swap(hold(send[1], raw), "yl")]

    whole, late = (0, owned, 0, 4, 0, 2), (0, owned, 3, 1, 1, 1)
    own, own_late = by_time(vecs, (whole, late), mark(send[0]))
    other = by_time(other, (whole,))[0]
    own, other = rows_of(own), rows_of(other)
    lines = raw[RAW * comps] + first_part[RAW * comps]
    lines = lines + swap(lines, "c")
    raw_rows = rows_of(by_time(raw, ((0, RAW, 0, 4, 0, 2),), mark(other), lines)[0])

    def against(part, x, y, step, *after):
        out = project([part], own, other, x, y, step, *map(mark, after))[0]
        return out.reshape(out.shape[0], 4, -1, 2 * (count - RAW), 2 * owned)

    first = project([rows_of(mine), raw_rows], own, other, 0, 0, 8)

    slabs = [v.reshape(4, comps // 2, -1, sites) for v in (send[3], own_late)]
    spread = share_z(hold(jnp.concatenate(slabs, axis=2), raw, other))
    spread[1] = hold(spread[1], first[0])
    spread = jnp.stack(spread)
    cut = send[3].shape[3]
    spread_s, spread_v = spread[:, :, :cut], spread[:, :, cut:]
    spread_w = swap(spread_v, "c")

    first = [v.reshape(4, 4, 2, -1, 2 * owned) for v in first]
    first = sum_x(jnp.concatenate(first, axis=3))
    first = sum_z(hold(first, spread_v))

    got.append(swap(hold(send[2], got[0]), "yl"))
    early = against(got[0], 0, 0, 8, first, spread_w)
    early = sum_z(jnp.swapaxes(early, 0, 1)).reshape(4, -1, 2 * owned)
    mid = [against(got[1], 2, 0, 4, early)[0]]
    got.append(swap(hold(spread_s, mid[0]), "yl"))
    mid.append(against(got[2], 3, 0, 1, mid[0])[0])
    mid = sum_z(jnp.concatenate(mid, axis=1))
    last = project_pieces(got[3], spread_v, spread_w)
    last = last.reshape(1, -1, 2 * owned)
    late = sum_x(jnp.concatenate([early, mid, last]).reshape(4, 2, -1, 2 * owned))

    here = sum_yh(jnp.concatenate([first, late], axis=1))
    there = swap(here, "c")

    def assemble(sums, half):
        sums = sums[:, half * owned : (half + 1) * owned]
        view = lambda v: v.reshape(2, -1, owned)
        cut = [2 * count, 2 * (count + RAW)]
        away = [view(sums[cut[0] : cut[1]]), view(sums[cut[1] :])]
        return view(sums[: cut[0]]), jnp.concatenate(away, axis=1)

    h0, y0 = assemble(here, 0)
    h1, y1 = assemble(there, 1)
    tau = jnp.stack([h0, h1, y0, y1])
    order = jnp.stack([group, group ^ 1, group ^ 2, group ^ 3])
    spin_of = jnp.take(jnp.transpose(dilution), order, axis=0)
    mask = spin_of[:, None, :] == jnp.arange(spins, dtype=jnp.int32)[None, :, None]
    view = tau.reshape(4, 1, 2, MASS, nsources, count // (MASS * nsources), owned)
    picked = jnp.where(mask[:, :, None, None, :, None, None], view, 0.0)
    result = jnp.sum(picked, axis=0).reshape(spins, 2, count, owned) * scale
    result = result.transpose(3, 0, 2, 1).reshape(1, owned, spins * count * 2)

    chosen = lines.reshape(nsources, -1, sites)[:, :comps]
    my_spins = lax.dynamic_index_in_dim(dilution, group, 1, keepdims=False)
    spin_mask = jnp.arange(spins, dtype=jnp.int32)[None, :] == my_spins[:, None]
    sources = jnp.where(
        spin_mask[:, :, None, None], chosen[:, None, :, :], jnp.zeros((), jnp.bfloat16)
    )
    return result, sources[None]


def solution(mesh):
    split = Mesh(mesh.devices.reshape(2, 2, 4, 4, 2), ("yl", "c", "z", "x", "yh"))
    grp, lat = ("yl", "c"), ("z", "x", "yh")
    return jax.shard_map(
        local,
        mesh=split,
        in_specs=(P(grp, None, None, lat), P(grp, None, None, None, lat), P(), P(), P()),
        out_specs=(P(lat, grp, None), P(grp, None, None, None, lat)),
        check_vma=False,
    )
```

```python
import functools
import math

import jax
import jax.numpy as jnp
from jax import lax
from jax.experimental import pallas as pl
from jax.experimental.pallas import tpu as pltpu
from jax.sharding import Mesh
from jax.sharding import PartitionSpec as P

MASS = 2
RAW = 8
SWAP = [(0, 1), (1, 0)]


def swap(value, axis):
    return lax.ppermute(value, axis, SWAP)


ANY = pl.BlockSpec(memory_space=pl.ANY)
HINT = pl.CostEstimate(flops=1000, bytes_accessed=1000, transcendentals=0)


def by_time_kernel(cuts, block, *refs):
    outs = refs[-len(cuts) :]
    comps = refs[-1].shape[3]
    for k in range(comps):
        if len(block.shape) == 4:
            part = block[:, k]
        else:
            part = jnp.stack([block[n * comps + k] for n in range(block.shape[0] // comps)])
        turned = jnp.swapaxes(part, 0, 1)
        for (low, high, x, nx, y, ny), out in zip(cuts, outs):
            for i in range(nx):
                for j in range(ny):
                    out[i, 0, j, k] = turned[2 * (x + i) + y + j, low:high]


def by_time(block, cuts, *after):
    if block.ndim == 4:
        n, comps, times, sites = block.shape
        spec = pl.BlockSpec((n, comps, times // 4, sites), lambda z: (0, 0, z, 0))
    else:
        n, comps = RAW, block.shape[0] // RAW
        _, times, sites = block.shape
        spec = pl.BlockSpec((n * comps, times // 4, sites), lambda z: (0, z, 0))
    return pl.pallas_call(
        functools.partial(by_time_kernel, cuts),
        grid=(4,),
        in_specs=[spec] + [ANY] * len(after),
        out_specs=[
            pl.BlockSpec((nx, 1, ny, comps, high - low, sites), lambda z: (0, z, 0, 0, 0, 0))
            for low, high, _, nx, _, ny in cuts
        ],
        out_shape=[
            jax.ShapeDtypeStruct((nx, 4, ny, comps, high - low, sites), block.dtype)
            for low, high, _, nx, _, ny in cuts
        ],
        compiler_params=pltpu.CompilerParams(vmem_limit_bytes=(56 if n > RAW else 16) * 2**20),
        cost_estimate=HINT,
        name="by_time",
    )(block, *after)


def rows_of(block):
    x, z, yh, comps, n, sites = block.shape
    return block.reshape(x, z * yh, comps // 2, 2 * n, sites)


def mark(value):
    while value.ndim > 2:
        value = value[0]
    return value


def hold_kernel(*refs):
    pass


def hold(value, *after):
    return pl.pallas_call(
        hold_kernel,
        in_specs=[ANY] * (1 + len(after)),
        out_specs=ANY,
        out_shape=jax.ShapeDtypeStruct(value.shape, value.dtype),
        input_output_aliases={0: 0},
        cost_estimate=HINT,
        name="hold",
    )(value, *map(mark, after))


def front_kernel(owned, at, sols, vecs, out, lines, slab, held, sems):
    count, comps, rows, _ = lines.shape
    group, time = at[0], at[1]
    span = held.shape[0] // 4
    part = lambda ref, i: ref.at[pl.ds(i * span, span)]
    into = [
        pltpu.make_async_copy(part(sols, i), part(held, i), sems.at[i]) for i in range(4)
    ]
    outof = [
        pltpu.make_async_copy(part(held, i), part(out, i), sems.at[4 + i]) for i in range(4)
    ]
    first = pl.multiple_of(time // rows * rows, rows)
    picks = [
        pltpu.make_async_copy(
            vecs.at[at[2 + s] % owned, :, pl.ds(first, rows)], lines.at[s], sems.at[8 + s]
        )
        for s in range(count)
    ]
    last = pltpu.make_async_copy(slab, out.at[held.shape[0]], sems.at[8 + count])
    for copy in into + picks:
        copy.start()
    for i in range(4):
        into[i].wait()
        outof[i].start()
    row = lax.broadcasted_iota(jnp.int32, lines.shape[1:], 1)
    for s in range(count):
        picks[s].wait()
        here = jnp.where(at[2 + s] // owned == group, time % rows, -1)
        kept = jnp.sum(jnp.where(row == here, lines[s].astype(jnp.float32), 0.0), axis=1)
        slab[s] = jnp.concatenate([kept, jnp.zeros_like(kept[:2])], axis=0).astype(slab.dtype)
    last.start()
    for i in range(4):
        outof[i].wait()
    last.wait()


def front(sols, vecs, source_index, source_time, group):
    owned, comps, times, sites = vecs.shape
    count = source_index.shape[0]
    at = jnp.concatenate([group[None], source_time, source_index])
    out = pl.pallas_call(
        functools.partial(front_kernel, owned),
        in_specs=[pl.BlockSpec(memory_space=pltpu.SMEM), ANY, ANY],
        out_specs=ANY,
        out_shape=jax.ShapeDtypeStruct((RAW * comps + 1, count, times // count, sites), sols.dtype),
        scratch_shapes=[
            pltpu.VMEM((count, comps, 16, sites), sols.dtype),
            pltpu.VMEM((count, times // count, sites), sols.dtype),
            pltpu.VMEM((RAW * comps, count, times // count, sites), sols.dtype),
            pltpu.SemaphoreType.DMA((9 + count,)),
        ],
        compiler_params=pltpu.CompilerParams(vmem_limit_bytes=56 * 2**20),
        cost_estimate=HINT,
        name="front",
    )(at, sols.reshape(-1, count, times // count, sites), vecs)
    return out.reshape(RAW * comps + 1, times, sites)


def product(cols, own, other):
    return lax.dot_general(
        jnp.concatenate(cols, axis=0),
        jnp.concatenate([own, other], axis=0),
        (((1,), (1,)), ((), ())),
        preferred_element_type=jnp.float32,
    )


def real_imag(total, row, n):
    width = total.shape[1] // 4
    re, im = total[row : row + n], total[row + n : row + 2 * n]
    real, imag = [], []
    for left in (0, 2 * width):
        mid, right = left + width, left + 2 * width
        real.append(re[:, left:mid] + im[:, mid:right])
        imag.append(im[:, left:mid] - re[:, mid:right])
    return jnp.concatenate(real, axis=1), jnp.concatenate(imag, axis=1)


def dot_kernel(count, *refs):
    cols, (own, other), outs = refs[:count], refs[count : count + 2], refs[-count:]
    for at in range(own.shape[1]):
        total = None
        for colour in range(own.shape[2]):
            term = product(
                [col[0, at, colour] for col in cols], own[0, at, colour], other[0, at, colour]
            )
            total = term if total is None else total + term
        row = 0
        for col, out in zip(cols, outs):
            n = col.shape[3] // 2
            out[0, at, 0], out[0, at, 1] = real_imag(total, row, n)
            row += 2 * n


def pieces_kernel(col, own, other, out):
    total = None
    for colour in range(own.shape[1]):
        term = product([col[0, colour]], own[0, colour], other[0, colour])
        total = term if total is None else total + term
    here = pl.program_id(0)
    for part, value in enumerate(real_imag(total, 0, out.shape[1])):
        out[part] = jnp.where(here == 0, value, out[part] + value)


def project_pieces(cols, own, other, *after):
    count, _, n2, _ = cols.shape
    rows = own.shape[2]
    spec = lambda v: pl.BlockSpec((1,) + v.shape[1:], lambda i: (i, 0, 0, 0))
    return pl.pallas_call(
        pieces_kernel,
        grid=(count,),
        in_specs=[spec(cols), spec(own), spec(other)] + [ANY] * len(after),
        out_specs=pl.BlockSpec((2, n2 // 2, rows), lambda i: (0, 0, 0)),
        out_shape=jax.ShapeDtypeStruct((2, n2 // 2, rows), jnp.float32),
        compiler_params=pltpu.CompilerParams(vmem_limit_bytes=16 * 2**20),
        cost_estimate=HINT,
        name="project_pieces",
    )(cols, own, other, *after)


def project(cols, own, other, x, y, step, *after):
    size, inner, colours, _, sites = cols[0].shape
    rows, stride = own.shape[3], own.shape[1] // inner
    spec = lambda n, stride=1, x=0, y=0: pl.BlockSpec(
        (1, step, colours, n, sites), lambda i, j: (i + x, j * stride + y, 0, 0, 0)
    )
    in_specs = [spec(c.shape[3]) for c in cols] + [spec(rows, stride, x, y)] * 2
    in_specs += [ANY] * len(after)
    out_specs = [
        pl.BlockSpec((1, step, 2, c.shape[3] // 2, rows), lambda i, j: (i, j, 0, 0, 0))
        for c in cols
    ]
    out_shape = [
        jax.ShapeDtypeStruct((size, inner, 2, c.shape[3] // 2, rows), jnp.float32) for c in cols
    ]
    return pl.pallas_call(
        functools.partial(dot_kernel, len(cols)),
        grid=(size, inner // step),
        in_specs=in_specs,
        out_specs=out_specs,
        out_shape=out_shape,
        compiler_params=pltpu.CompilerParams(vmem_limit_bytes=60 * 2**20),
        cost_estimate=HINT,
        name="project",
    )(*cols, own, other, *after)


def pick(value, index):
    return lax.dynamic_index_in_dim(value, index, 0, keepdims=False)


def share_z(slabs):
    me = lax.axis_index("z")
    got = [
        lax.ppermute(pick(slabs, (me + k) % 4), "z", [(i, (i + k) % 4) for i in range(4)])
        for k in (1, 3, 2)
    ]
    return [pick(slabs, me), *got]


def sum_z(slabs):
    got = share_z(slabs)
    return got[0] + got[1] + got[2] + got[3]


def sum_x(slabs):
    me = lax.axis_index("x")
    total = pick(slabs, me)
    for k in (1, 3, 2):
        pairs = [(i, (i + k) % 4) for i in range(4)]
        total = total + lax.ppermute(pick(slabs, (me + k) % 4), "x", pairs)
    return total


def sum_yh(part):
    me = lax.axis_index("yh")
    return pick(part, me) + swap(pick(part, 1 - me), "yh")


def local(eigvecs, solutions, source_index, source_time, dilution):
    owned, times, comps, sites = eigvecs.shape
    count = solutions.shape[1]
    nsources, spins = dilution.shape
    scale = 1.0 / math.sqrt(comps * sites * 32)
    core = lax.axis_index("c")
    group = 2 * lax.axis_index("yl") + core
    sols = solutions[0].transpose(0, 2, 1, 3)
    vecs = eigvecs.transpose(0, 2, 1, 3)

    first_part = front(sols, vecs, source_index, source_time, group)
    raw = swap(first_part, "yl")
    other = swap(vecs, "c")
    parts = ((0, 3, 0, 2), (3, 1, 0, 1), (3, 1, 1, 1))
    sent = [(RAW, count, *part) for part in parts]
    mine, *send = by_time(sols, ((0, count, 0, 4, 0, 2), *sent), first_part)
    send = [rows_of(part) for part in send]
    got = [swap(send[0], "yl"), swap(hold(send[1], raw), "yl")]

    whole, late = (0, owned, 0, 4, 0, 2), (0, owned, 3, 1, 1, 1)
    own, own_late = by_time(vecs, (whole, late), send[0])
    other = by_time(other, (whole,))[0]
    own, other = rows_of(own), rows_of(other)
    lines = raw[RAW * comps] + first_part[RAW * comps]
    lines = lines + swap(lines, "c")
    raw_rows = rows_of(by_time(raw, ((0, RAW, 0, 4, 0, 2),), mark(other), lines)[0])

    def against(part, x, y, step, *after):
        out = project([part], own, other, x, y, step, *map(mark, after))[0]
        return out.reshape(out.shape[0], 4, -1, 2 * (count - RAW), 2 * owned)

    first = project([rows_of(mine), raw_rows], own, other, 0, 0, 8)

    slabs = [v.reshape(4, comps // 2, -1, sites) for v in (send[2], own_late)]
    spread = share_z(jnp.concatenate(slabs, axis=2))
    spread[1] = hold(spread[1], first[0])
    spread = jnp.stack(spread)
    cut = send[2].shape[3]
    spread_s, spread_v = spread[:, :, :cut], spread[:, :, cut:]
    spread_w = swap(spread_v, "c")

    first = [v.reshape(4, 4, 2, -1, 2 * owned) for v in first]
    first = sum_x(jnp.concatenate(first, axis=3))
    first = sum_z(hold(first, spread_v, spread_w))

    late = [against(got[0], 0, 0, 8, first)]
    got.append(swap(hold(spread_s, late[0]), "yl"))
    late.append(against(got[1], 3, 0, 1, late[0]))
    late = [jnp.swapaxes(v, 0, 1).reshape(4, -1, *v.shape[3:]) for v in late]
    late = sum_z(jnp.concatenate(late, axis=1))
    last = project_pieces(got[2], spread_v, spread_w)
    last = last.reshape(1, -1, 2 * owned)
    late = sum_x(jnp.concatenate([late, last]).reshape(4, 2, -1, 2 * owned))

    here = sum_yh(jnp.concatenate([first, late], axis=1))
    there = swap(here, "c")

    def assemble(sums, half):
        sums = sums[:, half * owned : (half + 1) * owned]
        view = lambda v: v.reshape(2, -1, owned)
        cut = [2 * count, 2 * (count + RAW)]
        away = [view(sums[cut[0] : cut[1]]), view(sums[cut[1] :])]
        return view(sums[: cut[0]]), jnp.concatenate(away, axis=1)

    h0, y0 = assemble(here, 0)
    h1, y1 = assemble(there, 1)
    tau = jnp.stack([h0, h1, y0, y1])
    order = jnp.stack([group, group ^ 1, group ^ 2, group ^ 3])
    spin_of = jnp.take(jnp.transpose(dilution), order, axis=0)
    mask = spin_of[:, None, :] == jnp.arange(spins, dtype=jnp.int32)[None, :, None]
    view = tau.reshape(4, 1, 2, MASS, nsources, count // (MASS * nsources), owned)
    picked = jnp.where(mask[:, :, None, None, :, None, None], view, 0.0)
    result = jnp.sum(picked, axis=0).reshape(spins, 2, count, owned) * scale
    result = result.transpose(3, 0, 2, 1).reshape(1, owned, spins * count * 2)

    chosen = lines.reshape(nsources, -1, sites)[:, :comps]
    my_spins = lax.dynamic_index_in_dim(dilution, group, 1, keepdims=False)
    spin_mask = jnp.arange(spins, dtype=jnp.int32)[None, :] == my_spins[:, None]
    sources = jnp.where(
        spin_mask[:, :, None, None], chosen[:, None, :, :], jnp.zeros((), jnp.bfloat16)
    )
    return result, sources[None]


def solution(mesh):
    split = Mesh(mesh.devices.reshape(2, 2, 4, 4, 2), ("yl", "c", "z", "x", "yh"))
    grp, lat = ("yl", "c"), ("z", "x", "yh")
    return jax.shard_map(
        local,
        mesh=split,
        in_specs=(P(grp, None, None, lat), P(grp, None, None, None, lat), P(), P(), P()),
        out_specs=(P(lat, grp, None), P(grp, None, None, None, lat)),
        check_vma=False,
    )
```

```python
import functools
import math

import jax
import jax.numpy as jnp
from jax import lax
from jax.experimental import pallas as pl
from jax.experimental.pallas import tpu as pltpu
from jax.sharding import Mesh
from jax.sharding import PartitionSpec as P

MASS = 2
RAW = 8
SWAP = [(0, 1), (1, 0)]


def swap(value, axis):
    return lax.ppermute(value, axis, SWAP)


ANY = pl.BlockSpec(memory_space=pl.ANY)
HINT = pl.CostEstimate(flops=1000, bytes_accessed=1000, transcendentals=0)


def by_time_kernel(cuts, block, *refs):
    outs = refs[-len(cuts) :]
    comps = refs[-1].shape[3]
    for k in range(comps):
        if len(block.shape) == 4:
            part = block[:, k]
        else:
            part = jnp.stack([block[n * comps + k] for n in range(block.shape[0] // comps)])
        turned = jnp.swapaxes(part, 0, 1)
        for (low, high, x, nx, y, ny), out in zip(cuts, outs):
            for i in range(nx):
                for j in range(ny):
                    out[i, 0, j, k] = turned[2 * (x + i) + y + j, low:high]


def by_time(block, cuts, *after):
    if block.ndim == 4:
        n, comps, times, sites = block.shape
        spec = pl.BlockSpec((n, comps, times // 4, sites), lambda z: (0, 0, z, 0))
    else:
        n, comps = RAW, block.shape[0] // RAW
        _, times, sites = block.shape
        spec = pl.BlockSpec((n * comps, times // 4, sites), lambda z: (0, z, 0))
    return pl.pallas_call(
        functools.partial(by_time_kernel, cuts),
        grid=(4,),
        in_specs=[spec] + [ANY] * len(after),
        out_specs=[
            pl.BlockSpec((nx, 1, ny, comps, high - low, sites), lambda z: (0, z, 0, 0, 0, 0))
            for low, high, _, nx, _, ny in cuts
        ],
        out_shape=[
            jax.ShapeDtypeStruct((nx, 4, ny, comps, high - low, sites), block.dtype)
            for low, high, _, nx, _, ny in cuts
        ],
        compiler_params=pltpu.CompilerParams(vmem_limit_bytes=(56 if n > RAW else 16) * 2**20),
        cost_estimate=HINT,
        name="by_time",
    )(block, *after)


def rows_of(block):
    x, z, yh, comps, n, sites = block.shape
    return block.reshape(x, z * yh, comps // 2, 2 * n, sites)


def mark(value):
    while value.ndim > 2:
        value = value[0]
    return value


def hold_kernel(*refs):
    pass


def hold(value, *after):
    return pl.pallas_call(
        hold_kernel,
        in_specs=[ANY] * (1 + len(after)),
        out_specs=ANY,
        out_shape=jax.ShapeDtypeStruct(value.shape, value.dtype),
        input_output_aliases={0: 0},
        cost_estimate=HINT,
        name="hold",
    )(value, *after)


def front_kernel(owned, index, when, sols, vecs, out, lines, slab, held, sems):
    count, comps, rows, _ = lines.shape
    group, time = 2 * lax.axis_index("yl") + lax.axis_index("c"), when[0]
    span = held.shape[0] // 4
    part = lambda ref, i: ref.at[pl.ds(i * span, span)]
    into = [
        pltpu.make_async_copy(part(sols, i), part(held, i), sems.at[i]) for i in range(4)
    ]
    outof = [
        pltpu.make_async_copy(part(held, i), part(out, i), sems.at[4 + i]) for i in range(4)
    ]
    first = pl.multiple_of(time // rows * rows, rows)
    picks = [
        pltpu.make_async_copy(
            vecs.at[index[s] % owned, :, pl.ds(first, rows)], lines.at[s], sems.at[8 + s]
        )
        for s in range(count)
    ]
    last = pltpu.make_async_copy(slab, out.at[held.shape[0]], sems.at[8 + count])
    for copy in into + picks:
        copy.start()
    for i in range(4):
        into[i].wait()
        outof[i].start()
    row = lax.broadcasted_iota(jnp.int32, lines.shape[1:], 1)
    for s in range(count):
        picks[s].wait()
        here = jnp.where(index[s] // owned == group, time % rows, -1)
        kept = jnp.sum(jnp.where(row == here, lines[s].astype(jnp.float32), 0.0), axis=1)
        slab[s] = jnp.concatenate([kept, jnp.zeros_like(kept[:2])], axis=0).astype(slab.dtype)
    last.start()
    for i in range(4):
        outof[i].wait()
    last.wait()


def front(sols, vecs, source_index, source_time):
    owned, comps, times, sites = vecs.shape
    count = source_index.shape[0]
    out = pl.pallas_call(
        functools.partial(front_kernel, owned),
        in_specs=[pl.BlockSpec(memory_space=pltpu.SMEM)] * 2 + [ANY] * 2,
        out_specs=ANY,
        out_shape=jax.ShapeDtypeStruct((RAW * comps + 1, count, times // count, sites), sols.dtype),
        scratch_shapes=[
            pltpu.VMEM((count, comps, 16, sites), sols.dtype),
            pltpu.VMEM((count, times // count, sites), sols.dtype),
            pltpu.VMEM((RAW * comps, count, times // count, sites), sols.dtype),
            pltpu.SemaphoreType.DMA((9 + count,)),
        ],
        compiler_params=pltpu.CompilerParams(vmem_limit_bytes=56 * 2**20),
        cost_estimate=HINT,
        name="front",
    )(source_index, source_time, sols.reshape(-1, count, times // count, sites), vecs)
    return out.reshape(RAW * comps + 1, times, sites)


def product(cols, own, other):
    return lax.dot_general(
        jnp.concatenate(cols, axis=0),
        jnp.concatenate([own, other], axis=0),
        (((1,), (1,)), ((), ())),
        preferred_element_type=jnp.float32,
    )


def real_imag(total, row, n):
    width = total.shape[1] // 4
    re, im = total[row : row + n], total[row + n : row + 2 * n]
    real, imag = [], []
    for left in (0, 2 * width):
        mid, right = left + width, left + 2 * width
        real.append(re[:, left:mid] + im[:, mid:right])
        imag.append(im[:, left:mid] - re[:, mid:right])
    return jnp.concatenate(real, axis=1), jnp.concatenate(imag, axis=1)


def dot_kernel(count, *refs):
    cols, (own, other), outs = refs[:count], refs[count : count + 2], refs[-count:]
    for at in range(own.shape[1]):
        total = None
        for colour in range(own.shape[2]):
            term = product(
                [col[0, at, colour] for col in cols], own[0, at, colour], other[0, at, colour]
            )
            total = term if total is None else total + term
        row = 0
        for col, out in zip(cols, outs):
            n = col.shape[3] // 2
            out[0, at, 0], out[0, at, 1] = real_imag(total, row, n)
            row += 2 * n


def pieces_kernel(col, own, other, out):
    total = None
    for colour in range(own.shape[1]):
        term = product([col[0, colour]], own[0, colour], other[0, colour])
        total = term if total is None else total + term
    here = pl.program_id(0)
    for part, value in enumerate(real_imag(total, 0, out.shape[1])):
        out[part] = jnp.where(here == 0, value, out[part] + value)


def project_pieces(cols, own, other, *after):
    count, _, n2, _ = cols.shape
    rows = own.shape[2]
    spec = lambda v: pl.BlockSpec((1,) + v.shape[1:], lambda i: (i, 0, 0, 0))
    return pl.pallas_call(
        pieces_kernel,
        grid=(count,),
        in_specs=[spec(cols), spec(own), spec(other)] + [ANY] * len(after),
        out_specs=pl.BlockSpec((2, n2 // 2, rows), lambda i: (0, 0, 0)),
        out_shape=jax.ShapeDtypeStruct((2, n2 // 2, rows), jnp.float32),
        compiler_params=pltpu.CompilerParams(vmem_limit_bytes=16 * 2**20),
        cost_estimate=HINT,
        name="project_pieces",
    )(cols, own, other, *after)


def project(cols, own, other, x, y, step, *after):
    size, inner, colours, _, sites = cols[0].shape
    rows, stride = own.shape[3], own.shape[1] // inner
    spec = lambda n, stride=1, x=0, y=0: pl.BlockSpec(
        (1, step, colours, n, sites), lambda i, j: (i + x, j * stride + y, 0, 0, 0)
    )
    in_specs = [spec(c.shape[3]) for c in cols] + [spec(rows, stride, x, y)] * 2
    in_specs += [ANY] * len(after)
    out_specs = [
        pl.BlockSpec((1, step, 2, c.shape[3] // 2, rows), lambda i, j: (i, j, 0, 0, 0))
        for c in cols
    ]
    out_shape = [
        jax.ShapeDtypeStruct((size, inner, 2, c.shape[3] // 2, rows), jnp.float32) for c in cols
    ]
    return pl.pallas_call(
        functools.partial(dot_kernel, len(cols)),
        grid=(size, inner // step),
        in_specs=in_specs,
        out_specs=out_specs,
        out_shape=out_shape,
        compiler_params=pltpu.CompilerParams(vmem_limit_bytes=60 * 2**20),
        cost_estimate=HINT,
        name="project",
    )(*cols, own, other, *after)


def pick(value, index):
    return lax.dynamic_index_in_dim(value, index, 0, keepdims=False)


def share_z(slabs):
    me = lax.axis_index("z")
    got = [
        lax.ppermute(pick(slabs, (me + k) % 4), "z", [(i, (i + k) % 4) for i in range(4)])
        for k in (1, 3, 2)
    ]
    return [pick(slabs, me), *got]


def sum_z(slabs):
    got = share_z(slabs)
    return got[0] + got[1] + got[2] + got[3]


def sum_x(slabs):
    me = lax.axis_index("x")
    total = pick(slabs, me)
    for k in (1, 3, 2):
        pairs = [(i, (i + k) % 4) for i in range(4)]
        total = total + lax.ppermute(pick(slabs, (me + k) % 4), "x", pairs)
    return total


def sum_yh(part):
    me = lax.axis_index("yh")
    return pick(part, me) + swap(pick(part, 1 - me), "yh")


def local(eigvecs, solutions, source_index, source_time, dilution):
    owned, times, comps, sites = eigvecs.shape
    count = solutions.shape[1]
    nsources, spins = dilution.shape
    scale = 1.0 / math.sqrt(comps * sites * 32)
    core = lax.axis_index("c")
    group = 2 * lax.axis_index("yl") + core
    sols = solutions[0].transpose(0, 2, 1, 3)
    vecs = eigvecs.transpose(0, 2, 1, 3)

    first_part = front(sols, vecs, source_index, source_time)
    raw = swap(first_part, "yl")
    other = swap(vecs, "c")
    parts = ((0, 3, 0, 2), (3, 1, 0, 1), (3, 1, 1, 1))
    sent = [(RAW, count, *part) for part in parts]
    mine, *send = by_time(sols, ((0, count, 0, 4, 0, 2), *sent), first_part)
    send = [rows_of(part) for part in send]
    got = [swap(send[0], "yl"), swap(hold(send[1], mark(raw)), "yl")]

    whole, late = (0, owned, 0, 4, 0, 2), (0, owned, 3, 1, 1, 1)
    own, own_late = by_time(vecs, (whole, late), send[0])
    other = by_time(other, (whole,))[0]
    own, other = rows_of(own), rows_of(other)
    lines = raw[RAW * comps] + first_part[RAW * comps]
    lines = lines + swap(lines, "c")
    raw_rows = rows_of(by_time(raw, ((0, RAW, 0, 4, 0, 2),), lines)[0])

    def against(part, x, y, step, *after):
        out = project([part], own, other, x, y, step, *after)[0]
        return out.reshape(out.shape[0], 4, -1, 2 * (count - RAW), 2 * owned)

    first = project([rows_of(mine), raw_rows], own, other, 0, 0, 8)

    slabs = [v.reshape(4, comps // 2, -1, sites) for v in (send[2], own_late)]
    spread = share_z(hold(jnp.concatenate(slabs, axis=2), mark(other)))
    spread[1] = hold(spread[1], mark(first[0]))
    spread = jnp.stack(spread)
    cut = send[2].shape[3]
    spread_s, spread_v = spread[:, :, :cut], spread[:, :, cut:]
    spread_w = swap(spread_v, "c")

    first = [v.reshape(4, 4, 2, -1, 2 * owned) for v in first]
    first = sum_x(jnp.concatenate(first, axis=3))
    late = [against(got[0], 0, 0, 8, mark(first), mark(spread_w))]
    got.append(swap(hold(spread_s, mark(first)), "yl"))
    late.append(against(got[1], 3, 0, 1, late[0]))
    last = project_pieces(got[2], spread_v, spread_w).reshape(1, -1, 2 * owned)
    late = [jnp.swapaxes(v, 0, 1).reshape(4, -1, 2 * owned) for v in late]
    late = share_z(jnp.concatenate([first.reshape(4, -1, 2 * owned), *late], axis=1))
    late = late[0] + late[1] + late[2] + hold(late[3], last)
    cut = 4 * (count + RAW)
    first = late[:cut].reshape(2, -1, 2 * owned)
    late = late[cut:].reshape(7, -1, 2 * owned)
    late = sum_x(jnp.concatenate([late, last]).reshape(4, 2, -1, 2 * owned))

    here = sum_yh(jnp.concatenate([first, late], axis=1))
    there = swap(here, "c")

    def assemble(sums, half):
        sums = sums[:, half * owned : (half + 1) * owned]
        view = lambda v: v.reshape(2, -1, owned)
        cut = [2 * count, 2 * (count + RAW)]
        away = [view(sums[cut[0] : cut[1]]), view(sums[cut[1] :])]
        return view(sums[: cut[0]]), jnp.concatenate(away, axis=1)

    h0, y0 = assemble(here, 0)
    h1, y1 = assemble(there, 1)
    tau = jnp.stack([h0, h1, y0, y1])
    order = jnp.stack([group, group ^ 1, group ^ 2, group ^ 3])
    spin_of = jnp.take(jnp.transpose(dilution), order, axis=0)
    mask = spin_of[:, None, :] == jnp.arange(spins, dtype=jnp.int32)[None, :, None]
    view = tau.reshape(4, 1, 2, MASS, nsources, count // (MASS * nsources), owned)
    picked = jnp.where(mask[:, :, None, None, :, None, None], view, 0.0)
    result = jnp.sum(picked, axis=0).reshape(spins, 2, count, owned) * scale
    result = result.transpose(3, 0, 2, 1).reshape(1, owned, spins * count * 2)

    chosen = lines.reshape(nsources, -1, sites)[:, :comps]
    my_spins = lax.dynamic_index_in_dim(dilution, group, 1, keepdims=False)
    spin_mask = jnp.arange(spins, dtype=jnp.int32)[None, :] == my_spins[:, None]
    sources = jnp.where(
        spin_mask[:, :, None, None], chosen[:, None, :, :], jnp.zeros((), jnp.bfloat16)
    )
    return result, sources[None]


def solution(mesh):
    split = Mesh(mesh.devices.reshape(2, 2, 4, 4, 2), ("yl", "c", "z", "x", "yh"))
    grp, lat = ("yl", "c"), ("z", "x", "yh")
    return jax.shard_map(
        local,
        mesh=split,
        in_specs=(P(grp, None, None, lat), P(grp, None, None, None, lat), P(), P(), P()),
        out_specs=(P(lat, grp, None), P(grp, None, None, None, lat)),
        check_vma=False,
    )
```

```python
import functools
import math

import jax
import jax.numpy as jnp
from jax import lax
from jax.experimental import pallas as pl
from jax.experimental.pallas import tpu as pltpu
from jax.sharding import Mesh
from jax.sharding import PartitionSpec as P

MASS = 2
SWAP = [(0, 1), (1, 0)]


def swap(value, axis):
    return lax.ppermute(value, axis, SWAP)


ANY = pl.BlockSpec(memory_space=pl.ANY)
HINT = pl.CostEstimate(flops=1000, bytes_accessed=1000, transcendentals=0)


def by_time_kernel(cuts, block, *refs):
    outs = refs[-len(cuts) :]
    for k in range(block.shape[1]):
        turned = jnp.swapaxes(block[:, k], 0, 1)
        for (low, high, x, nx, y, ny), out in zip(cuts, outs):
            for i in range(nx):
                for j in range(ny):
                    out[i, 0, j, k] = turned[2 * (x + i) + y + j, low:high]


def by_time(block, cuts, *after):
    n, comps, times, sites = block.shape
    spec = pl.BlockSpec((n, comps, times // 4, sites), lambda z: (0, 0, z, 0))
    return pl.pallas_call(
        functools.partial(by_time_kernel, cuts),
        grid=(4,),
        in_specs=[spec] + [ANY] * len(after),
        out_specs=[
            pl.BlockSpec((nx, 1, ny, comps, high - low, sites), lambda z: (0, z, 0, 0, 0, 0))
            for low, high, _, nx, _, ny in cuts
        ],
        out_shape=[
            jax.ShapeDtypeStruct((nx, 4, ny, comps, high - low, sites), block.dtype)
            for low, high, _, nx, _, ny in cuts
        ],
        compiler_params=pltpu.CompilerParams(vmem_limit_bytes=56 * 2**20),
        cost_estimate=HINT,
        name="by_time",
    )(block, *after)


def rows_of(block):
    x, z, yh, comps, n, sites = block.shape
    return block.reshape(x, z * yh, comps // 2, 2 * n, sites)


def mark(value):
    while value.ndim > 2:
        value = value[0]
    return value


def hold_kernel(*refs):
    pass


def hold(value, *after):
    return pl.pallas_call(
        hold_kernel,
        in_specs=[ANY] * (1 + len(after)),
        out_specs=ANY,
        out_shape=jax.ShapeDtypeStruct(value.shape, value.dtype),
        input_output_aliases={0: 0},
        cost_estimate=HINT,
        name="hold",
    )(value, *after)


def choose_kernel(owned, index, when, vecs, out, lines, sems):
    count, comps, rows, _ = lines.shape
    group, time = 2 * lax.axis_index("yl") + lax.axis_index("c"), when[0]
    first = pl.multiple_of(time // rows * rows, rows)
    picks = [
        pltpu.make_async_copy(
            vecs.at[index[s] % owned, :, pl.ds(first, rows)], lines.at[s], sems.at[s]
        )
        for s in range(count)
    ]
    for copy in picks:
        copy.start()
    row = lax.broadcasted_iota(jnp.int32, lines.shape[1:], 1)
    for s in range(count):
        picks[s].wait()
        here = jnp.where(index[s] // owned == group, time % rows, -1)
        kept = jnp.sum(jnp.where(row == here, lines[s].astype(jnp.float32), 0.0), axis=1)
        out[s] = jnp.concatenate([kept, jnp.zeros_like(kept[:2])], axis=0).astype(out.dtype)


def choose(vecs, source_index, source_time, after):
    owned, comps, times, sites = vecs.shape
    count = source_index.shape[0]
    kernel = functools.partial(choose_kernel, owned)
    return pl.pallas_call(
        lambda index, when, vecs, after, *refs: kernel(index, when, vecs, *refs),
        in_specs=[pl.BlockSpec(memory_space=pltpu.SMEM)] * 2 + [ANY] * 2,
        out_specs=pl.BlockSpec(memory_space=pltpu.VMEM),
        out_shape=jax.ShapeDtypeStruct((count, 8, sites), vecs.dtype),
        scratch_shapes=[
            pltpu.VMEM((count, comps, 16, sites), vecs.dtype),
            pltpu.SemaphoreType.DMA((count,)),
        ],
        compiler_params=pltpu.CompilerParams(vmem_limit_bytes=60 * 2**20),
        cost_estimate=HINT,
        name="choose",
    )(source_index, source_time, vecs, after)


def product(cols, own, other):
    return lax.dot_general(
        jnp.concatenate(cols, axis=0),
        jnp.concatenate([own, other], axis=0),
        (((1,), (1,)), ((), ())),
        preferred_element_type=jnp.float32,
    )


def real_imag(total, row, n):
    width = total.shape[1] // 4
    re, im = total[row : row + n], total[row + n : row + 2 * n]
    real, imag = [], []
    for left in (0, 2 * width):
        mid, right = left + width, left + 2 * width
        real.append(re[:, left:mid] + im[:, mid:right])
        imag.append(im[:, left:mid] - re[:, mid:right])
    return jnp.concatenate(real, axis=1), jnp.concatenate(imag, axis=1)


def dot_kernel(count, *refs):
    cols, (own, other), outs = refs[:count], refs[count : count + 2], refs[-count:]
    for at in range(own.shape[1]):
        total = None
        for colour in range(own.shape[2]):
            term = product(
                [col[0, at, colour] for col in cols], own[0, at, colour], other[0, at, colour]
            )
            total = term if total is None else total + term
        row = 0
        for col, out in zip(cols, outs):
            n = col.shape[3] // 2
            out[0, at, 0], out[0, at, 1] = real_imag(total, row, n)
            row += 2 * n


def pieces_kernel(col, own, other, *refs):
    total, out = None, refs[-1]
    for colour in range(own.shape[2]):
        pair = [col[2 * colour], col[2 * colour + 1]]
        term = product(pair, own[0, 0, colour], other[0, 0, colour])
        total = term if total is None else total + term
    here = pl.program_id(0)
    for part, value in enumerate(real_imag(total, 0, out.shape[1])):
        out[part] = jnp.where(here == 0, value, out[part] + value)


def project_pieces(cols, own, other, y, *after):
    count, _, colours, rows, sites = own.shape
    n = cols.shape[1]
    vecs = pl.BlockSpec((1, 1, colours, rows, sites), lambda i: (i, y, 0, 0, 0))
    return pl.pallas_call(
        pieces_kernel,
        grid=(count,),
        in_specs=[pl.BlockSpec((2 * colours, n, sites), lambda i: (i, 0, 0)), vecs, vecs]
        + [ANY] * len(after),
        out_specs=pl.BlockSpec((2, n, rows), lambda i: (0, 0, 0)),
        out_shape=jax.ShapeDtypeStruct((2, n, rows), jnp.float32),
        compiler_params=pltpu.CompilerParams(vmem_limit_bytes=16 * 2**20),
        cost_estimate=HINT,
        name="project_pieces",
    )(cols, own, other, *after)


def project(cols, own, other, x, y, step, *after):
    size, inner, colours, _, sites = cols[0].shape
    rows, stride = own.shape[3], own.shape[1] // inner
    spec = lambda n, stride=1, x=0, y=0: pl.BlockSpec(
        (1, step, colours, n, sites), lambda i, j: (i + x, j * stride + y, 0, 0, 0)
    )
    in_specs = [spec(c.shape[3]) for c in cols] + [spec(rows, stride, x, y)] * 2
    in_specs += [ANY] * len(after)
    out_specs = [
        pl.BlockSpec((1, step, 2, c.shape[3] // 2, rows), lambda i, j: (i, j, 0, 0, 0))
        for c in cols
    ]
    out_shape = [
        jax.ShapeDtypeStruct((size, inner, 2, c.shape[3] // 2, rows), jnp.float32) for c in cols
    ]
    return pl.pallas_call(
        functools.partial(dot_kernel, len(cols)),
        grid=(size, inner // step),
        in_specs=in_specs,
        out_specs=out_specs,
        out_shape=out_shape,
        compiler_params=pltpu.CompilerParams(vmem_limit_bytes=60 * 2**20),
        cost_estimate=HINT,
        name="project",
    )(*cols, own, other, *after)


def pick(value, index):
    return lax.dynamic_index_in_dim(value, index, 0, keepdims=False)


def share_z(slabs):
    me = lax.axis_index("z")
    got = [
        lax.ppermute(pick(slabs, (me + k) % 4), "z", [(i, (i + k) % 4) for i in range(4)])
        for k in (1, 3, 2)
    ]
    return [pick(slabs, me), *got]


def sum_z(slabs):
    got = share_z(slabs)
    return got[0] + got[1] + got[2] + got[3]


def sum_x(slabs):
    me = lax.axis_index("x")
    total = pick(slabs, me)
    for k in (1, 3, 2):
        pairs = [(i, (i + k) % 4) for i in range(4)]
        total = total + lax.ppermute(pick(slabs, (me + k) % 4), "x", pairs)
    return total


def sum_yh(part):
    me = lax.axis_index("yh")
    return pick(part, me) + swap(pick(part, 1 - me), "yh")


def local(eigvecs, solutions, source_index, source_time, dilution):
    owned, times, comps, sites = eigvecs.shape
    count = solutions.shape[1]
    nsources, spins = dilution.shape
    scale = 1.0 / math.sqrt(comps * sites * 32)
    core = lax.axis_index("c")
    group = 2 * lax.axis_index("yl") + core
    sols = solutions[0].transpose(0, 2, 1, 3)
    vecs = eigvecs.transpose(0, 2, 1, 3)

    other = swap(vecs, "c")
    mine = by_time(sols, ((0, count, 0, 3, 0, 2), (0, count, 3, 1, 0, 2)))
    mine = [rows_of(part) for part in mine]
    got = swap(mine[0], "yl")

    whole, late = (0, owned, 0, 4, 0, 2), (0, owned, 3, 1, 0, 2)
    own, own_late = by_time(vecs, (whole, late), mine[0])
    other = by_time(other, (whole,))[0]
    own, other = rows_of(own), rows_of(other)
    lines = choose(vecs, source_index, source_time, mark(other)).reshape(1, -1, sites)

    def against(part, x, *after):
        out = project([part], own, other, x, 0, 8, *after)[0]
        return out.reshape(out.shape[0], 4, 2, 2 * count, 2 * owned)

    slabs = [v.reshape(4, 2, comps // 2, -1, sites) for v in (mine[1], own_late)]
    spread = share_z(hold(jnp.concatenate(slabs, axis=3), mark(other)))
    first = [against(mine[0], 0), against(mine[1], 3)]
    spread[1] = hold(spread[1], mark(first[0]), mark(first[1]))
    spread = jnp.stack(spread)
    cut = 2 * count
    spread_s, spread_v = spread[:, :, :, :cut], spread[:, :, :, cut:]
    spread_w = swap(spread_v, "c")
    spread_s = [spread_s[:, y].reshape(-1, count, sites) for y in range(2)]

    first = sum_x(jnp.concatenate(first))
    got_a = swap(hold(jnp.concatenate([spread_s[0], lines]), mark(first)), "yl")
    late = against(got, 0)
    got_b = swap(hold(spread_s[1], mark(late)), "yl")
    last = [project_pieces(got_a, spread_v, spread_w, 0)]
    last.append(project_pieces(got_b, spread_v, spread_w, 1, last[0]))
    late = jnp.swapaxes(late, 0, 1).reshape(4, -1, 2 * owned)
    late = share_z(jnp.concatenate([first.reshape(4, -1, 2 * owned), late], axis=1))
    late = late[0] + late[1] + late[2] + hold(late[3], last[0])
    cut = 4 * count
    first = late[:cut].reshape(2, -1, 2 * owned)
    late = late[cut:].reshape(6, -1, 2 * owned)
    late = jnp.concatenate([late, *(v.reshape(1, -1, 2 * owned) for v in last)])
    late = sum_x(late.reshape(4, 2, -1, 2 * owned))

    here = sum_yh(jnp.concatenate([first, late], axis=1))
    there = swap(here, "c")

    lines = lines[0] + got_a[-1]
    lines = lines + swap(lines, "c")

    def assemble(sums, half):
        sums = sums[:, half * owned : (half + 1) * owned].reshape(2, 2, count, owned)
        return sums[0], sums[1]

    h0, y0 = assemble(here, 0)
    h1, y1 = assemble(there, 1)
    tau = jnp.stack([h0, h1, y0, y1])
    order = jnp.stack([group, group ^ 1, group ^ 2, group ^ 3])
    spin_of = jnp.take(jnp.transpose(dilution), order, axis=0)
    mask = spin_of[:, None, :] == jnp.arange(spins, dtype=jnp.int32)[None, :, None]
    view = tau.reshape(4, 1, 2, MASS, nsources, count // (MASS * nsources), owned)
    picked = jnp.where(mask[:, :, None, None, :, None, None], view, 0.0)
    result = jnp.sum(picked, axis=0).reshape(spins, 2, count, owned) * scale
    result = result.transpose(3, 0, 2, 1).reshape(1, owned, spins * count * 2)

    chosen = lines.reshape(nsources, -1, sites)[:, :comps]
    my_spins = lax.dynamic_index_in_dim(dilution, group, 1, keepdims=False)
    spin_mask = jnp.arange(spins, dtype=jnp.int32)[None, :] == my_spins[:, None]
    sources = jnp.where(
        spin_mask[:, :, None, None], chosen[:, None, :, :], jnp.zeros((), jnp.bfloat16)
    )
    return result, sources[None]


def solution(mesh):
    split = Mesh(mesh.devices.reshape(2, 2, 4, 4, 2), ("yl", "c", "z", "x", "yh"))
    grp, lat = ("yl", "c"), ("z", "x", "yh")
    return jax.shard_map(
        local,
        mesh=split,
        in_specs=(P(grp, None, None, lat), P(grp, None, None, None, lat), P(), P(), P()),
        out_specs=(P(lat, grp, None), P(grp, None, None, None, lat)),
        check_vma=False,
    )
```

```python
import functools
import math

import jax
import jax.numpy as jnp
from jax import lax
from jax.experimental import pallas as pl
from jax.experimental.pallas import tpu as pltpu
from jax.sharding import Mesh
from jax.sharding import PartitionSpec as P

MASS = 2
SWAP = [(0, 1), (1, 0)]


def swap(value, axis):
    return lax.ppermute(value, axis, SWAP)


ANY = pl.BlockSpec(memory_space=pl.ANY)
HINT = pl.CostEstimate(flops=1000, bytes_accessed=1000, transcendentals=0)


def by_time_kernel(cuts, block, *refs):
    outs = refs[-len(cuts) :]
    for k in range(block.shape[1]):
        turned = jnp.swapaxes(block[:, k], 0, 1)
        for (low, high, x, nx, y, ny), out in zip(cuts, outs):
            for i in range(nx):
                for j in range(ny):
                    out[i, 0, j, k] = turned[2 * (x + i) + y + j, low:high]


def by_time(block, cuts, *after):
    n, comps, times, sites = block.shape
    spec = pl.BlockSpec((n, comps, times // 4, sites), lambda z: (0, 0, z, 0))
    return pl.pallas_call(
        functools.partial(by_time_kernel, cuts),
        grid=(4,),
        in_specs=[spec] + [ANY] * len(after),
        out_specs=[
            pl.BlockSpec((nx, 1, ny, comps, high - low, sites), lambda z: (0, z, 0, 0, 0, 0))
            for low, high, _, nx, _, ny in cuts
        ],
        out_shape=[
            jax.ShapeDtypeStruct((nx, 4, ny, comps, high - low, sites), block.dtype)
            for low, high, _, nx, _, ny in cuts
        ],
        compiler_params=pltpu.CompilerParams(vmem_limit_bytes=56 * 2**20),
        cost_estimate=HINT,
        name="by_time",
    )(block, *after)


def rows_of(block):
    x, z, yh, comps, n, sites = block.shape
    return block.reshape(x, z * yh, comps // 2, 2 * n, sites)


def mark(value):
    while value.ndim > 2:
        value = value[0]
    return value


def hold_kernel(*refs):
    pass


def hold(value, *after):
    return pl.pallas_call(
        hold_kernel,
        in_specs=[ANY] * (1 + len(after)),
        out_specs=ANY,
        out_shape=jax.ShapeDtypeStruct(value.shape, value.dtype),
        input_output_aliases={0: 0},
        cost_estimate=HINT,
        name="hold",
    )(value, *after)


def choose_kernel(owned, index, when, vecs, out, lines, sems):
    count, comps, rows, _ = lines.shape
    group, time = 2 * lax.axis_index("yl") + lax.axis_index("c"), when[0]
    first = pl.multiple_of(time // rows * rows, rows)
    picks = [
        pltpu.make_async_copy(
            vecs.at[index[s] % owned, :, pl.ds(first, rows)], lines.at[s], sems.at[s]
        )
        for s in range(count)
    ]
    for copy in picks:
        copy.start()
    row = lax.broadcasted_iota(jnp.int32, lines.shape[1:], 1)
    for s in range(count):
        picks[s].wait()
        here = jnp.where(index[s] // owned == group, time % rows, -1)
        kept = jnp.sum(jnp.where(row == here, lines[s].astype(jnp.float32), 0.0), axis=1)
        out[s] = jnp.concatenate([kept, jnp.zeros_like(kept[:2])], axis=0).astype(out.dtype)


def choose(vecs, source_index, source_time, after):
    owned, comps, times, sites = vecs.shape
    count = source_index.shape[0]
    kernel = functools.partial(choose_kernel, owned)
    return pl.pallas_call(
        lambda index, when, vecs, after, *refs: kernel(index, when, vecs, *refs),
        in_specs=[pl.BlockSpec(memory_space=pltpu.SMEM)] * 2 + [ANY] * 2,
        out_specs=pl.BlockSpec(memory_space=pltpu.VMEM),
        out_shape=jax.ShapeDtypeStruct((count, 8, sites), vecs.dtype),
        scratch_shapes=[
            pltpu.VMEM((count, comps, 16, sites), vecs.dtype),
            pltpu.SemaphoreType.DMA((count,)),
        ],
        compiler_params=pltpu.CompilerParams(vmem_limit_bytes=60 * 2**20),
        cost_estimate=HINT,
        name="choose",
    )(source_index, source_time, vecs, after)


def product(cols, own, other):
    return lax.dot_general(
        jnp.concatenate(cols, axis=0),
        jnp.concatenate([own, other], axis=0),
        (((1,), (1,)), ((), ())),
        preferred_element_type=jnp.float32,
    )


def real_imag(total, row, n):
    width = total.shape[1] // 4
    re, im = total[row : row + n], total[row + n : row + 2 * n]
    real, imag = [], []
    for left in (0, 2 * width):
        mid, right = left + width, left + 2 * width
        real.append(re[:, left:mid] + im[:, mid:right])
        imag.append(im[:, left:mid] - re[:, mid:right])
    return jnp.concatenate(real, axis=1), jnp.concatenate(imag, axis=1)


def dot_kernel(count, *refs):
    cols, (own, other), outs = refs[:count], refs[count : count + 2], refs[-count:]
    for at in range(own.shape[1]):
        total = None
        for colour in range(own.shape[2]):
            term = product(
                [col[0, at, colour] for col in cols], own[0, at, colour], other[0, at, colour]
            )
            total = term if total is None else total + term
        row = 0
        for col, out in zip(cols, outs):
            n = col.shape[3] // 2
            out[0, at, 0], out[0, at, 1] = real_imag(total, row, n)
            row += 2 * n


def pieces_kernel(col, own, other, *refs):
    total, out = None, refs[-1]
    for colour in range(own.shape[2]):
        pair = [col[2 * colour], col[2 * colour + 1]]
        term = product(pair, own[0, 0, colour], other[0, 0, colour])
        total = term if total is None else total + term
    here = pl.program_id(0)
    for part, value in enumerate(real_imag(total, 0, out.shape[1])):
        out[part] = jnp.where(here == 0, value, out[part] + value)


def project_pieces(cols, own, other, y, *after):
    count, _, colours, rows, sites = own.shape
    n = cols.shape[1]
    vecs = pl.BlockSpec((1, 1, colours, rows, sites), lambda i: (i, y, 0, 0, 0))
    return pl.pallas_call(
        pieces_kernel,
        grid=(count,),
        in_specs=[pl.BlockSpec((2 * colours, n, sites), lambda i: (i, 0, 0)), vecs, vecs]
        + [ANY] * len(after),
        out_specs=pl.BlockSpec((2, n, rows), lambda i: (0, 0, 0)),
        out_shape=jax.ShapeDtypeStruct((2, n, rows), jnp.float32),
        compiler_params=pltpu.CompilerParams(vmem_limit_bytes=16 * 2**20),
        cost_estimate=HINT,
        name="project_pieces",
    )(cols, own, other, *after)


def project(cols, own, other, x, y, step, *after):
    size, inner, colours, _, sites = cols[0].shape
    rows, stride = own.shape[3], own.shape[1] // inner
    spec = lambda n, stride=1, x=0, y=0: pl.BlockSpec(
        (1, step, colours, n, sites), lambda i, j: (i + x, j * stride + y, 0, 0, 0)
    )
    in_specs = [spec(c.shape[3]) for c in cols] + [spec(rows, stride, x, y)] * 2
    in_specs += [ANY] * len(after)
    out_specs = [
        pl.BlockSpec((1, step, 2, c.shape[3] // 2, rows), lambda i, j: (i, j, 0, 0, 0))
        for c in cols
    ]
    out_shape = [
        jax.ShapeDtypeStruct((size, inner, 2, c.shape[3] // 2, rows), jnp.float32) for c in cols
    ]
    return pl.pallas_call(
        functools.partial(dot_kernel, len(cols)),
        grid=(size, inner // step),
        in_specs=in_specs,
        out_specs=out_specs,
        out_shape=out_shape,
        compiler_params=pltpu.CompilerParams(vmem_limit_bytes=60 * 2**20),
        cost_estimate=HINT,
        name="project",
    )(*cols, own, other, *after)


def pick(value, index):
    return lax.dynamic_index_in_dim(value, index, 0, keepdims=False)


def share_z(slabs):
    me = lax.axis_index("z")
    got = [
        lax.ppermute(pick(slabs, (me + k) % 4), "z", [(i, (i + k) % 4) for i in range(4)])
        for k in (1, 3, 2)
    ]
    return [pick(slabs, me), *got]


def sum_z(slabs):
    got = share_z(slabs)
    return got[0] + got[1] + got[2] + got[3]


def sum_x(slabs):
    me = lax.axis_index("x")
    total = pick(slabs, me)
    for k in (1, 3, 2):
        pairs = [(i, (i + k) % 4) for i in range(4)]
        total = total + lax.ppermute(pick(slabs, (me + k) % 4), "x", pairs)
    return total


def sum_yh(part):
    me = lax.axis_index("yh")
    return pick(part, me) + swap(pick(part, 1 - me), "yh")


def local(eigvecs, solutions, source_index, source_time, dilution):
    owned, times, comps, sites = eigvecs.shape
    count = solutions.shape[1]
    nsources, spins = dilution.shape
    scale = 1.0 / math.sqrt(comps * sites * 32)
    core = lax.axis_index("c")
    group = 2 * lax.axis_index("yl") + core
    sols = solutions[0].transpose(0, 2, 1, 3)
    vecs = eigvecs.transpose(0, 2, 1, 3)

    other = swap(vecs, "c")
    mine = by_time(sols, ((0, count, 0, 3, 0, 2), (0, count, 3, 1, 0, 2)))
    mine = [rows_of(part) for part in mine]
    got = swap(mine[0], "yl")

    whole, late = (0, owned, 0, 4, 0, 2), (0, owned, 3, 1, 0, 2)
    own, own_late = by_time(vecs, (whole, late), mine[0])
    other = by_time(other, (whole,))[0]
    own, other = rows_of(own), rows_of(other)
    lines = choose(vecs, source_index, source_time, mark(other)).reshape(1, -1, sites)

    def against(part, x, *after):
        out = project([part], own, other, x, 0, 8, *after)[0]
        return out.reshape(out.shape[0], 4, 2, 2 * count, 2 * owned)

    slabs = [v.reshape(4, 2, comps // 2, -1, sites) for v in (mine[1], own_late)]
    spread = share_z(jnp.concatenate(slabs, axis=3))
    first = [against(mine[0], 0), against(mine[1], 3)]
    spread[1] = hold(spread[1], mark(first[0]), mark(first[1]))
    spread = jnp.stack(spread)
    cut = 2 * count
    spread_s, spread_v = spread[:, :, :, :cut], spread[:, :, :, cut:]
    spread_w = swap(spread_v, "c")
    spread_s = [spread_s[:, y].reshape(-1, count, sites) for y in range(2)]

    first = sum_x(jnp.concatenate(first))
    got_a = swap(hold(jnp.concatenate([spread_s[0], lines]), mark(first)), "yl")
    late = against(got, 0)
    got_b = swap(hold(spread_s[1], mark(late)), "yl")
    last = [project_pieces(got_a, spread_v, spread_w, 0)]
    last.append(project_pieces(got_b, spread_v, spread_w, 1, last[0]))
    late = jnp.swapaxes(late, 0, 1).reshape(4, -1, 2 * owned)
    late = share_z(jnp.concatenate([first.reshape(4, -1, 2 * owned), late], axis=1))
    late = late[0] + late[1] + late[2] + hold(late[3], last[0])
    cut = 4 * count
    first = late[:cut].reshape(2, -1, 2 * owned)
    late = late[cut:].reshape(6, -1, 2 * owned)
    late = jnp.concatenate([late, *(v.reshape(1, -1, 2 * owned) for v in last)])
    late = sum_x(late.reshape(4, 2, -1, 2 * owned))

    here = sum_yh(jnp.concatenate([first, late], axis=1))
    there = swap(here, "c")

    lines = lines[0] + got_a[-1]
    lines = lines + swap(lines, "c")

    def assemble(sums, half):
        sums = sums[:, half * owned : (half + 1) * owned].reshape(2, 2, count, owned)
        return sums[0], sums[1]

    h0, y0 = assemble(here, 0)
    h1, y1 = assemble(there, 1)
    tau = jnp.stack([h0, h1, y0, y1])
    order = jnp.stack([group, group ^ 1, group ^ 2, group ^ 3])
    spin_of = jnp.take(jnp.transpose(dilution), order, axis=0)
    mask = spin_of[:, None, :] == jnp.arange(spins, dtype=jnp.int32)[None, :, None]
    view = tau.reshape(4, 1, 2, MASS, nsources, count // (MASS * nsources), owned)
    picked = jnp.where(mask[:, :, None, None, :, None, None], view, 0.0)
    result = jnp.sum(picked, axis=0).reshape(spins, 2, count, owned) * scale
    result = result.transpose(3, 0, 2, 1).reshape(1, owned, spins * count * 2)

    chosen = lines.reshape(nsources, -1, sites)[:, :comps]
    my_spins = lax.dynamic_index_in_dim(dilution, group, 1, keepdims=False)
    spin_mask = jnp.arange(spins, dtype=jnp.int32)[None, :] == my_spins[:, None]
    sources = jnp.where(
        spin_mask[:, :, None, None], chosen[:, None, :, :], jnp.zeros((), jnp.bfloat16)
    )
    return result, sources[None]


def solution(mesh):
    split = Mesh(mesh.devices.reshape(2, 2, 4, 4, 2), ("yl", "c", "z", "x", "yh"))
    grp, lat = ("yl", "c"), ("z", "x", "yh")
    return jax.shard_map(
        local,
        mesh=split,
        in_specs=(P(grp, None, None, lat), P(grp, None, None, None, lat), P(), P(), P()),
        out_specs=(P(lat, grp, None), P(grp, None, None, None, lat)),
        check_vma=False,
    )
```

```python
import functools
import math

import jax
import jax.numpy as jnp
from jax import lax
from jax.experimental import pallas as pl
from jax.experimental.pallas import tpu as pltpu
from jax.sharding import Mesh
from jax.sharding import PartitionSpec as P

MASS = 2
SWAP = [(0, 1), (1, 0)]


def swap(value, axis):
    return lax.ppermute(value, axis, SWAP)


ANY = pl.BlockSpec(memory_space=pl.ANY)
HINT = pl.CostEstimate(flops=1000, bytes_accessed=1000, transcendentals=0)


def by_time_kernel(cuts, block, *refs):
    outs, (given, turned, sems) = refs[-len(cuts) - 3 : -3], refs[-3:]
    pairs, comps = given.shape[0], given.shape[2]
    copies = [
        pltpu.make_async_copy(block.at[:, :, pl.ds(16 * i, 16)], given.at[i], sems.at[i])
        for i in range(pairs)
    ]
    for copy in copies:
        copy.start()
    sent = []
    for z in range(2 * pairs):
        if z % 2 == 0:
            copies[z // 2].wait()
        for k in range(comps):
            eight = pl.ds(8 * (z % 2), 8)
            turned[z, :, k] = jnp.swapaxes(given[z // 2, :, k, eight], 0, 1)
        for (low, high, x, nx, y, ny), out in zip(cuts, outs):
            for i in range(nx):
                at = len(sent)
                source = turned.at[z, pl.ds(2 * (x + i) + y, ny), :, pl.ds(low, high - low)]
                sent.append(pltpu.make_async_copy(source, out.at[i, z], sems.at[pairs + at]))
                sent[at].start()
    for copy in sent:
        copy.wait()


def by_time(block, cuts, *after):
    n, comps, times, sites = block.shape
    return pl.pallas_call(
        functools.partial(by_time_kernel, cuts),
        in_specs=[ANY] * (1 + len(after)),
        out_specs=[ANY] * len(cuts),
        out_shape=[
            jax.ShapeDtypeStruct((nx, 4, ny, comps, high - low, sites), block.dtype)
            for low, high, _, nx, _, ny in cuts
        ],
        scratch_shapes=[
            pltpu.VMEM((times // 16, n, comps, 16, sites), block.dtype),
            pltpu.VMEM((times // 8, 8, comps, n, sites), block.dtype),
            pltpu.SemaphoreType.DMA((times // 16 + sum(4 * cut[3] for cut in cuts),)),
        ],
        compiler_params=pltpu.CompilerParams(vmem_limit_bytes=56 * 2**20),
        cost_estimate=HINT,
        name="by_time",
    )(block, *after)


def rows_of(block):
    x, z, yh, comps, n, sites = block.shape
    return block.reshape(x, z * yh, comps // 2, 2 * n, sites)


def mark(value):
    while value.ndim > 2:
        value = value[0]
    return value


def hold_kernel(*refs):
    pass


def hold(value, *after):
    return pl.pallas_call(
        hold_kernel,
        in_specs=[ANY] * (1 + len(after)),
        out_specs=ANY,
        out_shape=jax.ShapeDtypeStruct(value.shape, value.dtype),
        input_output_aliases={0: 0},
        cost_estimate=HINT,
        name="hold",
    )(value, *after)


def choose_kernel(owned, index, when, vecs, out, lines, sems):
    count, comps, rows, _ = lines.shape
    group, time = 2 * lax.axis_index("yl") + lax.axis_index("c"), when[0]
    first = pl.multiple_of(time // rows * rows, rows)
    picks = [
        pltpu.make_async_copy(
            vecs.at[index[s] % owned, :, pl.ds(first, rows)], lines.at[s], sems.at[s]
        )
        for s in range(count)
    ]
    for copy in picks:
        copy.start()
    row = lax.broadcasted_iota(jnp.int32, lines.shape[1:], 1)
    for s in range(count):
        picks[s].wait()
        here = jnp.where(index[s] // owned == group, time % rows, -1)
        kept = jnp.sum(jnp.where(row == here, lines[s].astype(jnp.float32), 0.0), axis=1)
        out[s] = jnp.concatenate([kept, jnp.zeros_like(kept[:2])], axis=0).astype(out.dtype)


def choose(vecs, source_index, source_time, after):
    owned, comps, times, sites = vecs.shape
    count = source_index.shape[0]
    kernel = functools.partial(choose_kernel, owned)
    return pl.pallas_call(
        lambda index, when, vecs, after, *refs: kernel(index, when, vecs, *refs),
        in_specs=[pl.BlockSpec(memory_space=pltpu.SMEM)] * 2 + [ANY] * 2,
        out_specs=pl.BlockSpec(memory_space=pltpu.VMEM),
        out_shape=jax.ShapeDtypeStruct((count, 8, sites), vecs.dtype),
        scratch_shapes=[
            pltpu.VMEM((count, comps, 16, sites), vecs.dtype),
            pltpu.SemaphoreType.DMA((count,)),
        ],
        compiler_params=pltpu.CompilerParams(vmem_limit_bytes=60 * 2**20),
        cost_estimate=HINT,
        name="choose",
    )(source_index, source_time, vecs, after)


def product(cols, own, other):
    return lax.dot_general(
        jnp.concatenate(cols, axis=0),
        jnp.concatenate([own, other], axis=0),
        (((1,), (1,)), ((), ())),
        preferred_element_type=jnp.float32,
    )


def real_imag(total, row, n):
    width = total.shape[1] // 4
    re, im = total[row : row + n], total[row + n : row + 2 * n]
    real, imag = [], []
    for left in (0, 2 * width):
        mid, right = left + width, left + 2 * width
        real.append(re[:, left:mid] + im[:, mid:right])
        imag.append(im[:, left:mid] - re[:, mid:right])
    return jnp.concatenate(real, axis=1), jnp.concatenate(imag, axis=1)


def dot_kernel(count, *refs):
    cols, (own, other), out = refs[:count], refs[count : count + 2], refs[-1]
    for at in range(own.shape[1]):
        total = None
        for colour in range(own.shape[2]):
            term = product(
                [col[0, at, colour] for col in cols], own[0, at, colour], other[0, at, colour]
            )
            total = term if total is None else total + term
        row = 0
        for col in cols:
            n = col.shape[3] // 2
            real, imag = real_imag(total, 2 * row, n)
            out[0, at, 0, row : row + n], out[0, at, 1, row : row + n] = real, imag
            row += n


def pieces_kernel(y, col, own, other, *refs):
    total, out = None, refs[-1]
    for block in range(own.shape[0]):
        for colour in range(own.shape[2]):
            at = 2 * (block * own.shape[2] + colour)
            term = product([col[at], col[at + 1]], own[block, y, colour], other[block, y, colour])
            total = term if total is None else total + term
    out[0], out[1] = real_imag(total, 0, out.shape[1])


def project_pieces(cols, own, other, y, *after):
    whole = pl.BlockSpec(memory_space=pltpu.VMEM)
    return pl.pallas_call(
        functools.partial(pieces_kernel, y),
        in_specs=[whole] * 3 + [ANY] * len(after),
        out_specs=whole,
        out_shape=jax.ShapeDtypeStruct((2, cols.shape[1], own.shape[3]), jnp.float32),
        compiler_params=pltpu.CompilerParams(vmem_limit_bytes=24 * 2**20),
        cost_estimate=HINT,
        name="project_pieces",
    )(cols, own, other, *after)


def project(cols, own, other, x, y, step, *after):
    size, inner, colours, _, sites = cols[0].shape
    rows, stride = own.shape[3], own.shape[1] // inner
    spec = lambda n, stride=1, x=0, y=0: pl.BlockSpec(
        (1, step, colours, n, sites), lambda i, j: (i + x, j * stride + y, 0, 0, 0)
    )
    in_specs = [spec(c.shape[3]) for c in cols] + [spec(rows, stride, x, y)] * 2
    in_specs += [ANY] * len(after)
    total = sum(c.shape[3] for c in cols) // 2
    out_specs = pl.BlockSpec((1, step, 2, total, rows), lambda i, j: (i, j, 0, 0, 0))
    out_shape = jax.ShapeDtypeStruct((size, inner, 2, total, rows), jnp.float32)
    return pl.pallas_call(
        functools.partial(dot_kernel, len(cols)),
        grid=(size, inner // step),
        in_specs=in_specs,
        out_specs=out_specs,
        out_shape=out_shape,
        compiler_params=pltpu.CompilerParams(vmem_limit_bytes=60 * 2**20),
        cost_estimate=HINT,
        name="project",
    )(*cols, own, other, *after)


def pick(value, index):
    return lax.dynamic_index_in_dim(value, index, 0, keepdims=False)


def share_z(slabs):
    me = lax.axis_index("z")
    got = [
        lax.ppermute(pick(slabs, (me + k) % 4), "z", [(i, (i + k) % 4) for i in range(4)])
        for k in (1, 3, 2)
    ]
    return [pick(slabs, me), *got]


def sum_z(slabs):
    got = share_z(slabs)
    return got[0] + got[1] + got[2] + got[3]


def sum_x(slabs):
    me = lax.axis_index("x")
    total = pick(slabs, me)
    for k in (1, 3, 2):
        pairs = [(i, (i + k) % 4) for i in range(4)]
        total = total + lax.ppermute(pick(slabs, (me + k) % 4), "x", pairs)
    return total


def sum_yh(part):
    me = lax.axis_index("yh")
    return pick(part, me) + swap(pick(part, 1 - me), "yh")


def local(eigvecs, solutions, source_index, source_time, dilution):
    owned, times, comps, sites = eigvecs.shape
    count = solutions.shape[1]
    nsources, spins = dilution.shape
    scale = 1.0 / math.sqrt(comps * sites * 32)
    core = lax.axis_index("c")
    group = 2 * lax.axis_index("yl") + core
    sols = solutions[0].transpose(0, 2, 1, 3)
    vecs = eigvecs.transpose(0, 2, 1, 3)

    other = swap(vecs, "c")
    mine = by_time(sols, ((0, count, 0, 3, 0, 2), (0, count, 3, 1, 0, 2)))
    mine = [rows_of(part) for part in mine]
    got = swap(mine[0], "yl")

    whole, late = (0, owned, 0, 4, 0, 2), (0, owned, 3, 1, 0, 2)
    own, own_late = by_time(vecs, (whole, late), mine[0])
    other = by_time(other, (whole,))[0]
    own, other = rows_of(own), rows_of(other)
    lines = choose(vecs, source_index, source_time, mark(other)).reshape(1, -1, sites)

    def against(parts, x, *after):
        out = project(parts, own, other, x, 0, 8, *after)
        return out.reshape(out.shape[0], 4, 2, 2 * count, 2 * owned)

    slabs = [v.reshape(4, 2, comps // 2, -1, sites) for v in (mine[1], own_late)]
    spread = share_z(jnp.concatenate(slabs, axis=3))
    first = [against(mine[:1], 0), against(mine[1:], 3)]
    spread[1] = hold(spread[1], mark(first[0]), mark(first[1]))
    spread = jnp.stack(spread)
    cut = 2 * count
    spread_s, spread_v = spread[:, :, :, :cut], spread[:, :, :, cut:]
    spread_w = swap(spread_v, "c")
    spread_s = [spread_s[:, y].reshape(-1, count, sites) for y in range(2)]

    first = sum_x(jnp.concatenate(first))
    got_a = swap(hold(jnp.concatenate([spread_s[0], lines]), mark(first)), "yl")
    late = against([got], 0)
    got_b = swap(hold(spread_s[1], mark(late)), "yl")
    last = [project_pieces(got_a, spread_v, spread_w, 0)]
    last.append(project_pieces(got_b, spread_v, spread_w, 1, last[0]))
    late = jnp.swapaxes(late, 0, 1).reshape(4, -1, 2 * owned)
    late = share_z(jnp.concatenate([first.reshape(4, -1, 2 * owned), late], axis=1))
    late = late[0] + late[1] + late[2] + hold(late[3], last[0])
    cut = 4 * count
    first = late[:cut].reshape(2, -1, 2 * owned)
    late = late[cut:].reshape(6, -1, 2 * owned)
    late = jnp.concatenate([late, *(v.reshape(1, -1, 2 * owned) for v in last)])
    late = sum_x(late.reshape(4, 2, -1, 2 * owned))

    here = sum_yh(jnp.concatenate([first, late], axis=1))
    there = swap(here, "c")

    lines = lines[0] + got_a[-1]
    lines = lines + swap(lines, "c")

    def assemble(sums, half):
        sums = sums[:, half * owned : (half + 1) * owned].reshape(2, 2, count, owned)
        return sums[0], sums[1]

    h0, y0 = assemble(here, 0)
    h1, y1 = assemble(there, 1)
    tau = jnp.stack([h0, h1, y0, y1])
    order = jnp.stack([group, group ^ 1, group ^ 2, group ^ 3])
    spin_of = jnp.take(jnp.transpose(dilution), order, axis=0)
    mask = spin_of[:, None, :] == jnp.arange(spins, dtype=jnp.int32)[None, :, None]
    view = tau.reshape(4, 1, 2, MASS, nsources, count // (MASS * nsources), owned)
    picked = jnp.where(mask[:, :, None, None, :, None, None], view, 0.0)
    result = jnp.sum(picked, axis=0).reshape(spins, 2, count, owned) * scale
    result = result.transpose(3, 0, 2, 1).reshape(1, owned, spins * count * 2)

    chosen = lines.reshape(nsources, -1, sites)[:, :comps]
    my_spins = lax.dynamic_index_in_dim(dilution, group, 1, keepdims=False)
    spin_mask = jnp.arange(spins, dtype=jnp.int32)[None, :] == my_spins[:, None]
    sources = jnp.where(
        spin_mask[:, :, None, None], chosen[:, None, :, :], jnp.zeros((), jnp.bfloat16)
    )
    return result, sources[None]


def solution(mesh):
    split = Mesh(mesh.devices.reshape(2, 2, 4, 4, 2), ("yl", "c", "z", "x", "yh"))
    grp, lat = ("yl", "c"), ("z", "x", "yh")
    return jax.shard_map(
        local,
        mesh=split,
        in_specs=(P(grp, None, None, lat), P(grp, None, None, None, lat), P(), P(), P()),
        out_specs=(P(lat, grp, None), P(grp, None, None, None, lat)),
        check_vma=False,
    )
```

```python
import functools
import math

import jax
import jax.numpy as jnp
from jax import lax
from jax.experimental import pallas as pl
from jax.experimental.pallas import tpu as pltpu
from jax.sharding import Mesh
from jax.sharding import PartitionSpec as P

MASS = 2
SWAP = [(0, 1), (1, 0)]


def swap(value, axis):
    return lax.ppermute(value, axis, SWAP)


ANY = pl.BlockSpec(memory_space=pl.ANY)
HINT = pl.CostEstimate(flops=1000, bytes_accessed=1000, transcendentals=0)


def by_time_kernel(cuts, block, *refs):
    outs, (given, turned, sems) = refs[-len(cuts) - 3 : -3], refs[-3:]
    pairs, comps = given.shape[0], given.shape[2]
    copies = [
        pltpu.make_async_copy(block.at[:, :, pl.ds(16 * i, 16)], given.at[i], sems.at[i])
        for i in range(pairs)
    ]
    for copy in copies:
        copy.start()
    sent = []
    for z in range(2 * pairs):
        if z % 2 == 0:
            copies[z // 2].wait()
        for k in range(comps):
            eight = pl.ds(8 * (z % 2), 8)
            turned[z, :, k] = jnp.swapaxes(given[z // 2, :, k, eight], 0, 1)
        for (low, high, x, nx, y, ny), out in zip(cuts, outs):
            for i in range(nx):
                at = len(sent)
                source = turned.at[z, pl.ds(2 * (x + i) + y, ny), :, pl.ds(low, high - low)]
                sent.append(pltpu.make_async_copy(source, out.at[i, z], sems.at[pairs + at]))
                sent[at].start()
    for copy in sent:
        copy.wait()


def by_time(block, cuts, *after):
    n, comps, times, sites = block.shape
    return pl.pallas_call(
        functools.partial(by_time_kernel, cuts),
        in_specs=[ANY] * (1 + len(after)),
        out_specs=[ANY] * len(cuts),
        out_shape=[
            jax.ShapeDtypeStruct((nx, 4, ny, comps, high - low, sites), block.dtype)
            for low, high, _, nx, _, ny in cuts
        ],
        scratch_shapes=[
            pltpu.VMEM((times // 16, n, comps, 16, sites), block.dtype),
            pltpu.VMEM((times // 8, 8, comps, n, sites), block.dtype),
            pltpu.SemaphoreType.DMA((times // 16 + sum(4 * cut[3] for cut in cuts),)),
        ],
        compiler_params=pltpu.CompilerParams(vmem_limit_bytes=56 * 2**20),
        cost_estimate=HINT,
        name="by_time",
    )(block, *after)


def rows_of(block):
    x, z, yh, comps, n, sites = block.shape
    return block.reshape(x, z * yh, comps // 2, 2 * n, sites)


def mark(value):
    while value.ndim > 2:
        value = value[0]
    return value


def hold_kernel(*refs):
    pass


def hold(value, *after):
    return pl.pallas_call(
        hold_kernel,
        in_specs=[ANY] * (1 + len(after)),
        out_specs=ANY,
        out_shape=jax.ShapeDtypeStruct(value.shape, value.dtype),
        input_output_aliases={0: 0},
        cost_estimate=HINT,
        name="hold",
    )(value, *after)


def choose_kernel(owned, index, when, vecs, out, lines, sems):
    count, comps, rows, _ = lines.shape
    group, time = 2 * lax.axis_index("yl") + lax.axis_index("c"), when[0]
    first = pl.multiple_of(time // rows * rows, rows)
    picks = [
        pltpu.make_async_copy(
            vecs.at[index[s] % owned, :, pl.ds(first, rows)], lines.at[s], sems.at[s]
        )
        for s in range(count)
    ]
    for copy in picks:
        copy.start()
    row = lax.broadcasted_iota(jnp.int32, lines.shape[1:], 1)
    for s in range(count):
        picks[s].wait()
        here = jnp.where(index[s] // owned == group, time % rows, -1)
        kept = jnp.sum(jnp.where(row == here, lines[s].astype(jnp.float32), 0.0), axis=1)
        out[s] = jnp.concatenate([kept, jnp.zeros_like(kept[:2])], axis=0).astype(out.dtype)


def choose(vecs, source_index, source_time, after):
    owned, comps, times, sites = vecs.shape
    count = source_index.shape[0]
    kernel = functools.partial(choose_kernel, owned)
    return pl.pallas_call(
        lambda index, when, vecs, after, *refs: kernel(index, when, vecs, *refs),
        in_specs=[pl.BlockSpec(memory_space=pltpu.SMEM)] * 2 + [ANY] * 2,
        out_specs=pl.BlockSpec(memory_space=pltpu.VMEM),
        out_shape=jax.ShapeDtypeStruct((count, 8, sites), vecs.dtype),
        scratch_shapes=[
            pltpu.VMEM((count, comps, 16, sites), vecs.dtype),
            pltpu.SemaphoreType.DMA((count,)),
        ],
        compiler_params=pltpu.CompilerParams(vmem_limit_bytes=60 * 2**20),
        cost_estimate=HINT,
        name="choose",
    )(source_index, source_time, vecs, after)


def product(cols, own, other):
    return lax.dot_general(
        jnp.concatenate(cols, axis=0),
        jnp.concatenate([own, other], axis=0),
        (((1,), (1,)), ((), ())),
        preferred_element_type=jnp.float32,
    )


def real_imag(total, row, n):
    width = total.shape[1] // 4
    re, im = total[row : row + n], total[row + n : row + 2 * n]
    real, imag = [], []
    for left in (0, 2 * width):
        mid, right = left + width, left + 2 * width
        real.append(re[:, left:mid] + im[:, mid:right])
        imag.append(im[:, left:mid] - re[:, mid:right])
    return jnp.concatenate(real, axis=1), jnp.concatenate(imag, axis=1)


def dot_kernel(count, *refs):
    cols, (own, other), out = refs[:count], refs[count : count + 2], refs[-1]
    for at in range(own.shape[1]):
        total = None
        for colour in range(own.shape[2]):
            term = product(
                [col[0, at, colour] for col in cols], own[0, at, colour], other[0, at, colour]
            )
            total = term if total is None else total + term
        row = 0
        for col in cols:
            n = col.shape[3] // 2
            real, imag = real_imag(total, 2 * row, n)
            out[0, at, 0, row : row + n], out[0, at, 1, row : row + n] = real, imag
            row += n


def pieces_kernel(col, own, other, *refs):
    total, out = None, refs[-1]
    for block in range(own.shape[0]):
        for colour in range(own.shape[2]):
            at = 2 * (block * own.shape[2] + colour)
            term = product([col[at], col[at + 1]], own[block, 0, colour], other[block, 0, colour])
            total = term if total is None else total + term
    out[0], out[1] = real_imag(total, 0, out.shape[1])


def project_pieces(cols, own, other, y, *after):
    count, _, *rest = own.shape
    vecs = pl.BlockSpec((count, 1, *rest), lambda i: (0, y, 0, 0, 0))
    rows = pl.BlockSpec((2 * count * rest[0], *cols.shape[1:]), lambda i: (0, 0, 0))
    return pl.pallas_call(
        pieces_kernel,
        grid=(1,),
        in_specs=[rows, vecs, vecs] + [ANY] * len(after),
        out_specs=pl.BlockSpec((2, cols.shape[1], own.shape[3]), lambda i: (0, 0, 0)),
        out_shape=jax.ShapeDtypeStruct((2, cols.shape[1], own.shape[3]), jnp.float32),
        compiler_params=pltpu.CompilerParams(vmem_limit_bytes=24 * 2**20),
        cost_estimate=HINT,
        name="project_pieces",
    )(cols, own, other, *after)


def project(cols, own, other, x, y, step, *after):
    size, inner, colours, _, sites = cols[0].shape
    rows, stride = own.shape[3], own.shape[1] // inner
    spec = lambda n, stride=1, x=0, y=0: pl.BlockSpec(
        (1, step, colours, n, sites), lambda i, j: (i + x, j * stride + y, 0, 0, 0)
    )
    in_specs = [spec(c.shape[3]) for c in cols] + [spec(rows, stride, x, y)] * 2
    in_specs += [ANY] * len(after)
    total = sum(c.shape[3] for c in cols) // 2
    out_specs = pl.BlockSpec((1, step, 2, total, rows), lambda i, j: (i, j, 0, 0, 0))
    out_shape = jax.ShapeDtypeStruct((size, inner, 2, total, rows), jnp.float32)
    return pl.pallas_call(
        functools.partial(dot_kernel, len(cols)),
        grid=(size, inner // step),
        in_specs=in_specs,
        out_specs=out_specs,
        out_shape=out_shape,
        compiler_params=pltpu.CompilerParams(vmem_limit_bytes=60 * 2**20),
        cost_estimate=HINT,
        name="project",
    )(*cols, own, other, *after)


def pick(value, index):
    return lax.dynamic_index_in_dim(value, index, 0, keepdims=False)


def share_z(slabs):
    me = lax.axis_index("z")
    got = [
        lax.ppermute(pick(slabs, (me + k) % 4), "z", [(i, (i + k) % 4) for i in range(4)])
        for k in (1, 3, 2)
    ]
    return [pick(slabs, me), *got]


def sum_z(slabs):
    got = share_z(slabs)
    return got[0] + got[1] + got[2] + got[3]


def sum_x(slabs):
    me = lax.axis_index("x")
    total = pick(slabs, me)
    for k in (1, 3, 2):
        pairs = [(i, (i + k) % 4) for i in range(4)]
        total = total + lax.ppermute(pick(slabs, (me + k) % 4), "x", pairs)
    return total


def sum_yh(part):
    me = lax.axis_index("yh")
    return pick(part, me) + swap(pick(part, 1 - me), "yh")


def local(eigvecs, solutions, source_index, source_time, dilution):
    owned, times, comps, sites = eigvecs.shape
    count = solutions.shape[1]
    nsources, spins = dilution.shape
    scale = 1.0 / math.sqrt(comps * sites * 32)
    core = lax.axis_index("c")
    group = 2 * lax.axis_index("yl") + core
    sols = solutions[0].transpose(0, 2, 1, 3)
    vecs = eigvecs.transpose(0, 2, 1, 3)

    other = swap(vecs, "c")
    mine = by_time(sols, ((0, count, 0, 3, 0, 2), (0, count, 3, 1, 0, 2)))
    mine = [rows_of(part) for part in mine]
    got = swap(mine[0], "yl")

    whole, late = (0, owned, 0, 4, 0, 2), (0, owned, 3, 1, 0, 2)
    own, own_late = by_time(vecs, (whole, late), mine[0])
    other = by_time(other, (whole,))[0]
    own, other = rows_of(own), rows_of(other)
    lines = choose(vecs, source_index, source_time, mark(other)).reshape(1, -1, sites)

    def against(parts, x, *after):
        out = project(parts, own, other, x, 0, 8, *after)
        return out.reshape(out.shape[0], 4, 2, 2 * count, 2 * owned)

    slabs = [v.reshape(4, 2, comps // 2, -1, sites) for v in (mine[1], own_late)]
    spread = share_z(jnp.concatenate(slabs, axis=3))
    first = [against(mine[:1], 0), against(mine[1:], 3)]
    spread[1] = hold(spread[1], mark(first[0]), mark(first[1]))
    spread = jnp.stack(spread)
    cut = 2 * count
    spread_s, spread_v = spread[:, :, :, :cut], spread[:, :, :, cut:]
    spread_w = swap(spread_v, "c")
    spread_s = [spread_s[:, y].reshape(-1, count, sites) for y in range(2)]

    first = sum_x(jnp.concatenate(first))
    got_a = swap(hold(jnp.concatenate([spread_s[0], lines]), mark(first)), "yl")
    late = against([got], 0)
    got_b = swap(hold(spread_s[1], mark(late)), "yl")
    last = [project_pieces(got_a, spread_v, spread_w, 0)]
    last.append(project_pieces(got_b, spread_v, spread_w, 1, last[0]))
    late = jnp.swapaxes(late, 0, 1).reshape(4, -1, 2 * owned)
    late = share_z(jnp.concatenate([first.reshape(4, -1, 2 * owned), late], axis=1))
    late = late[0] + late[1] + late[2] + hold(late[3], last[0])
    cut = 4 * count
    first = late[:cut].reshape(2, -1, 2 * owned)
    late = late[cut:].reshape(6, -1, 2 * owned)
    late = jnp.concatenate([late, *(v.reshape(1, -1, 2 * owned) for v in last)])
    late = sum_x(late.reshape(4, 2, -1, 2 * owned))

    here = sum_yh(jnp.concatenate([first, late], axis=1))
    there = swap(here, "c")

    lines = lines[0] + got_a[-1]
    lines = lines + swap(lines, "c")

    def assemble(sums, half):
        sums = sums[:, half * owned : (half + 1) * owned].reshape(2, 2, count, owned)
        return sums[0], sums[1]

    h0, y0 = assemble(here, 0)
    h1, y1 = assemble(there, 1)
    tau = jnp.stack([h0, h1, y0, y1])
    order = jnp.stack([group, group ^ 1, group ^ 2, group ^ 3])
    spin_of = jnp.take(jnp.transpose(dilution), order, axis=0)
    mask = spin_of[:, None, :] == jnp.arange(spins, dtype=jnp.int32)[None, :, None]
    view = tau.reshape(4, 1, 2, MASS, nsources, count // (MASS * nsources), owned)
    picked = jnp.where(mask[:, :, None, None, :, None, None], view, 0.0)
    result = jnp.sum(picked, axis=0).reshape(spins, 2, count, owned) * scale
    result = result.transpose(3, 0, 2, 1).reshape(1, owned, spins * count * 2)

    chosen = lines.reshape(nsources, -1, sites)[:, :comps]
    my_spins = lax.dynamic_index_in_dim(dilution, group, 1, keepdims=False)
    spin_mask = jnp.arange(spins, dtype=jnp.int32)[None, :] == my_spins[:, None]
    sources = jnp.where(
        spin_mask[:, :, None, None], chosen[:, None, :, :], jnp.zeros((), jnp.bfloat16)
    )
    return result, sources[None]


def solution(mesh):
    split = Mesh(mesh.devices.reshape(2, 2, 4, 4, 2), ("yl", "c", "z", "x", "yh"))
    grp, lat = ("yl", "c"), ("z", "x", "yh")
    return jax.shard_map(
        local,
        mesh=split,
        in_specs=(P(grp, None, None, lat), P(grp, None, None, None, lat), P(), P(), P()),
        out_specs=(P(lat, grp, None), P(grp, None, None, None, lat)),
        check_vma=False,
    )
```

```python
import functools
import math

import jax
import jax.numpy as jnp
from jax import lax
from jax.experimental import pallas as pl
from jax.experimental.pallas import tpu as pltpu
from jax.sharding import Mesh
from jax.sharding import PartitionSpec as P

MASS = 2
SWAP = [(0, 1), (1, 0)]


def swap(value, axis):
    return lax.ppermute(value, axis, SWAP)


ANY = pl.BlockSpec(memory_space=pl.ANY)
HINT = pl.CostEstimate(flops=1000, bytes_accessed=1000, transcendentals=0)


def by_time_kernel(cuts, block, *refs):
    outs, (given, turned, sems) = refs[-len(cuts) - 3 : -3], refs[-3:]
    pairs, comps = given.shape[0], given.shape[2]
    copies = [
        pltpu.make_async_copy(block.at[:, :, pl.ds(16 * i, 16)], given.at[i], sems.at[i])
        for i in range(pairs)
    ]
    for copy in copies:
        copy.start()
    sent = []
    for z in range(2 * pairs):
        if z % 2 == 0:
            copies[z // 2].wait()
        for k in range(comps):
            eight = pl.ds(8 * (z % 2), 8)
            turned[z, :, k] = jnp.swapaxes(given[z // 2, :, k, eight], 0, 1)
        for (low, high, x, nx, y, ny), out in zip(cuts, outs):
            for i in range(nx):
                at = len(sent)
                source = turned.at[z, pl.ds(2 * (x + i) + y, ny), :, pl.ds(low, high - low)]
                sent.append(pltpu.make_async_copy(source, out.at[i, z], sems.at[pairs + at]))
                sent[at].start()
    for copy in sent:
        copy.wait()


def by_time(block, cuts, *after):
    n, comps, times, sites = block.shape
    return pl.pallas_call(
        functools.partial(by_time_kernel, cuts),
        in_specs=[ANY] * (1 + len(after)),
        out_specs=[ANY] * len(cuts),
        out_shape=[
            jax.ShapeDtypeStruct((nx, 4, ny, comps, high - low, sites), block.dtype)
            for low, high, _, nx, _, ny in cuts
        ],
        scratch_shapes=[
            pltpu.VMEM((times // 16, n, comps, 16, sites), block.dtype),
            pltpu.VMEM((times // 8, 8, comps, n, sites), block.dtype),
            pltpu.SemaphoreType.DMA((times // 16 + sum(4 * cut[3] for cut in cuts),)),
        ],
        compiler_params=pltpu.CompilerParams(vmem_limit_bytes=56 * 2**20),
        cost_estimate=HINT,
        name="by_time",
    )(block, *after)


def rows_of(block):
    x, z, yh, comps, n, sites = block.shape
    return block.reshape(x, z * yh, comps // 2, 2 * n, sites)


def mark(value):
    while value.ndim > 2:
        value = value[0]
    return value


def hold_kernel(*refs):
    pass


def hold(value, *after):
    return pl.pallas_call(
        hold_kernel,
        in_specs=[ANY] * (1 + len(after)),
        out_specs=ANY,
        out_shape=jax.ShapeDtypeStruct(value.shape, value.dtype),
        input_output_aliases={0: 0},
        cost_estimate=HINT,
        name="hold",
    )(value, *after)


def choose_kernel(owned, index, when, vecs, out, lines, sems):
    count, comps, rows, _ = lines.shape
    group, time = 2 * lax.axis_index("yl") + lax.axis_index("c"), when[0]
    first = pl.multiple_of(time // rows * rows, rows)
    picks = [
        pltpu.make_async_copy(
            vecs.at[index[s] % owned, :, pl.ds(first, rows)], lines.at[s], sems.at[s]
        )
        for s in range(count)
    ]
    for copy in picks:
        copy.start()
    row = lax.broadcasted_iota(jnp.int32, lines.shape[1:], 1)
    for s in range(count):
        picks[s].wait()
        here = jnp.where(index[s] // owned == group, time % rows, -1)
        kept = jnp.sum(jnp.where(row == here, lines[s].astype(jnp.float32), 0.0), axis=1)
        out[s] = jnp.concatenate([kept, jnp.zeros_like(kept[:2])], axis=0).astype(out.dtype)


def choose(vecs, source_index, source_time, after):
    owned, comps, times, sites = vecs.shape
    count = source_index.shape[0]
    kernel = functools.partial(choose_kernel, owned)
    return pl.pallas_call(
        lambda index, when, vecs, after, *refs: kernel(index, when, vecs, *refs),
        in_specs=[pl.BlockSpec(memory_space=pltpu.SMEM)] * 2 + [ANY] * 2,
        out_specs=pl.BlockSpec(memory_space=pltpu.VMEM),
        out_shape=jax.ShapeDtypeStruct((count, 8, sites), vecs.dtype),
        scratch_shapes=[
            pltpu.VMEM((count, comps, 16, sites), vecs.dtype),
            pltpu.SemaphoreType.DMA((count,)),
        ],
        compiler_params=pltpu.CompilerParams(vmem_limit_bytes=60 * 2**20),
        cost_estimate=HINT,
        name="choose",
    )(source_index, source_time, vecs, after)


def product(cols, own, other):
    return lax.dot_general(
        jnp.concatenate(cols, axis=0),
        jnp.concatenate([own, other], axis=0),
        (((1,), (1,)), ((), ())),
        preferred_element_type=jnp.float32,
    )


def real_imag(total, row, n):
    width = total.shape[1] // 4
    re, im = total[row : row + n], total[row + n : row + 2 * n]
    real, imag = [], []
    for left in (0, 2 * width):
        mid, right = left + width, left + 2 * width
        real.append(re[:, left:mid] + im[:, mid:right])
        imag.append(im[:, left:mid] - re[:, mid:right])
    return jnp.concatenate(real, axis=1), jnp.concatenate(imag, axis=1)


def dot_kernel(count, *refs):
    cols, (own, other), out = refs[:count], refs[count : count + 2], refs[-1]
    for at in range(own.shape[1]):
        total = None
        for colour in range(own.shape[2]):
            term = product(
                [col[0, at, colour] for col in cols], own[0, at, colour], other[0, at, colour]
            )
            total = term if total is None else total + term
        row = 0
        for col in cols:
            n = col.shape[3] // 2
            real, imag = real_imag(total, 2 * row, n)
            out[0, at, 0, row : row + n], out[0, at, 1, row : row + n] = real, imag
            row += n


def pieces_kernel(col, own, other, *refs):
    total, out = None, refs[-1]
    for block in range(own.shape[0]):
        for colour in range(own.shape[2]):
            at = 2 * (block * own.shape[2] + colour)
            term = product([col[at], col[at + 1]], own[block, 0, colour], other[block, 0, colour])
            total = term if total is None else total + term
    out[0], out[1] = real_imag(total, 0, out.shape[1])


def project_pieces(cols, own, other, y, first, *after):
    _, _, *rest = own.shape
    count = cols.shape[0] // (2 * rest[0])
    vecs = pl.BlockSpec((count, 1, *rest), lambda i: (first // count, y, 0, 0, 0))
    rows = pl.BlockSpec((2 * count * rest[0], *cols.shape[1:]), lambda i: (0, 0, 0))
    return pl.pallas_call(
        pieces_kernel,
        grid=(1,),
        in_specs=[rows, vecs, vecs] + [ANY] * len(after),
        out_specs=pl.BlockSpec((2, cols.shape[1], own.shape[3]), lambda i: (0, 0, 0)),
        out_shape=jax.ShapeDtypeStruct((2, cols.shape[1], own.shape[3]), jnp.float32),
        compiler_params=pltpu.CompilerParams(vmem_limit_bytes=24 * 2**20),
        cost_estimate=HINT,
        name="project_pieces",
    )(cols, own, other, *after)


def project(cols, own, other, x, y, step, *after):
    size, inner, colours, _, sites = cols[0].shape
    rows, stride = own.shape[3], own.shape[1] // inner
    spec = lambda n, stride=1, x=0, y=0: pl.BlockSpec(
        (1, step, colours, n, sites), lambda i, j: (i + x, j * stride + y, 0, 0, 0)
    )
    in_specs = [spec(c.shape[3]) for c in cols] + [spec(rows, stride, x, y)] * 2
    in_specs += [ANY] * len(after)
    total = sum(c.shape[3] for c in cols) // 2
    out_specs = pl.BlockSpec((1, step, 2, total, rows), lambda i, j: (i, j, 0, 0, 0))
    out_shape = jax.ShapeDtypeStruct((size, inner, 2, total, rows), jnp.float32)
    return pl.pallas_call(
        functools.partial(dot_kernel, len(cols)),
        grid=(size, inner // step),
        in_specs=in_specs,
        out_specs=out_specs,
        out_shape=out_shape,
        compiler_params=pltpu.CompilerParams(vmem_limit_bytes=60 * 2**20),
        cost_estimate=HINT,
        name="project",
    )(*cols, own, other, *after)


def pick(value, index):
    return lax.dynamic_index_in_dim(value, index, 0, keepdims=False)


def share_z(slabs):
    me = lax.axis_index("z")
    got = [
        lax.ppermute(pick(slabs, (me + k) % 4), "z", [(i, (i + k) % 4) for i in range(4)])
        for k in (1, 3, 2)
    ]
    return [pick(slabs, me), *got]


def sum_z(slabs):
    got = share_z(slabs)
    return got[0] + got[1] + got[2] + got[3]


def sum_x(slabs):
    me = lax.axis_index("x")
    total = pick(slabs, me)
    for k in (1, 3, 2):
        pairs = [(i, (i + k) % 4) for i in range(4)]
        total = total + lax.ppermute(pick(slabs, (me + k) % 4), "x", pairs)
    return total


def sum_yh(part):
    me = lax.axis_index("yh")
    return pick(part, me) + swap(pick(part, 1 - me), "yh")


def local(eigvecs, solutions, source_index, source_time, dilution):
    owned, times, comps, sites = eigvecs.shape
    count = solutions.shape[1]
    nsources, spins = dilution.shape
    scale = 1.0 / math.sqrt(comps * sites * 32)
    core = lax.axis_index("c")
    group = 2 * lax.axis_index("yl") + core
    sols = solutions[0].transpose(0, 2, 1, 3)
    vecs = eigvecs.transpose(0, 2, 1, 3)

    other = swap(vecs, "c")
    mine = by_time(sols, ((0, count, 0, 3, 0, 2), (0, count, 3, 1, 0, 2)))
    mine = [rows_of(part) for part in mine]
    got = swap(mine[0], "yl")

    whole, late = (0, owned, 0, 4, 0, 2), (0, owned, 3, 1, 0, 2)
    own, own_late = by_time(vecs, (whole, late), mine[0])
    other = by_time(other, (whole,))[0]
    own, other = rows_of(own), rows_of(other)
    lines = choose(vecs, source_index, source_time, mark(other)).reshape(1, -1, sites)

    def against(parts, x, *after):
        out = project(parts, own, other, x, 0, 8, *after)
        return out.reshape(out.shape[0], 4, 2, 2 * count, 2 * owned)

    slabs = [v.reshape(4, 2, comps // 2, -1, sites) for v in (mine[1], own_late)]
    spread = share_z(jnp.concatenate(slabs, axis=3))
    first = [against(mine[:1], 0), against(mine[1:], 3)]
    spread[1] = hold(spread[1], mark(first[0]), mark(first[1]))
    spread = jnp.stack(spread)
    cut = 2 * count
    spread_s, spread_v = spread[:, :, :, :cut], spread[:, :, :, cut:]
    spread_w = swap(spread_v, "c")
    spread_s = [spread_s[:, y].reshape(-1, count, sites) for y in range(2)]

    first = sum_x(jnp.concatenate(first))
    cut = spread_s[1].shape[0] * 3 // 4
    part_a = hold(jnp.concatenate([spread_s[0], lines]), mark(first))
    part_b = hold(spread_s[1][:cut], mark(part_a))
    got_a, got_b = swap(part_a, "yl"), swap(part_b, "yl")
    late = against([got], 0)
    last_a = project_pieces(got_a, spread_v, spread_w, 0, 0)
    got_c = swap(hold(spread_s[1][cut:], mark(part_b)), "yl")
    last_b = project_pieces(got_b, spread_v, spread_w, 1, 0, last_a)
    lines = hold(lines[0] + got_a[-1], mark(last_b))
    lines = lines + swap(lines, "c")
    late = jnp.swapaxes(late, 0, 1).reshape(4, -1, 2 * owned)
    late = share_z(jnp.concatenate([first.reshape(4, -1, 2 * owned), late], axis=1))
    late = late[0] + late[1] + late[2] + hold(late[3], last_b)
    last_c = project_pieces(got_c, spread_v, spread_w, 1, 3, last_b, late[:8])
    cut = 4 * count
    first = late[:cut].reshape(2, -1, 2 * owned)
    late = late[cut:].reshape(6, -1, 2 * owned)
    late = jnp.concatenate([late, *(v.reshape(1, -1, 2 * owned) for v in (last_a, last_b + last_c))])
    late = sum_x(late.reshape(4, 2, -1, 2 * owned))

    here = sum_yh(jnp.concatenate([first, late], axis=1))
    there = swap(here, "c")

    def assemble(sums, half):
        sums = sums[:, half * owned : (half + 1) * owned].reshape(2, 2, count, owned)
        return sums[0], sums[1]

    h0, y0 = assemble(here, 0)
    h1, y1 = assemble(there, 1)
    tau = jnp.stack([h0, h1, y0, y1])
    order = jnp.stack([group, group ^ 1, group ^ 2, group ^ 3])
    spin_of = jnp.take(jnp.transpose(dilution), order, axis=0)
    mask = spin_of[:, None, :] == jnp.arange(spins, dtype=jnp.int32)[None, :, None]
    view = tau.reshape(4, 1, 2, MASS, nsources, count // (MASS * nsources), owned)
    picked = jnp.where(mask[:, :, None, None, :, None, None], view, 0.0)
    result = jnp.sum(picked, axis=0).reshape(spins, 2, count, owned) * scale
    result = result.transpose(3, 0, 2, 1).reshape(1, owned, spins * count * 2)

    chosen = lines.reshape(nsources, -1, sites)[:, :comps]
    my_spins = lax.dynamic_index_in_dim(dilution, group, 1, keepdims=False)
    spin_mask = jnp.arange(spins, dtype=jnp.int32)[None, :] == my_spins[:, None]
    sources = jnp.where(
        spin_mask[:, :, None, None], chosen[:, None, :, :], jnp.zeros((), jnp.bfloat16)
    )
    return result, sources[None]


def solution(mesh):
    split = Mesh(mesh.devices.reshape(2, 2, 4, 4, 2), ("yl", "c", "z", "x", "yh"))
    grp, lat = ("yl", "c"), ("z", "x", "yh")
    return jax.shard_map(
        local,
        mesh=split,
        in_specs=(P(grp, None, None, lat), P(grp, None, None, None, lat), P(), P(), P()),
        out_specs=(P(lat, grp, None), P(grp, None, None, None, lat)),
        check_vma=False,
    )
```

```python
import functools
import math

import jax
import jax.numpy as jnp
from jax import lax
from jax.experimental import pallas as pl
from jax.experimental.pallas import tpu as pltpu
from jax.sharding import Mesh
from jax.sharding import PartitionSpec as P

MASS = 2
SWAP = [(0, 1), (1, 0)]


def swap(value, axis):
    return lax.ppermute(value, axis, SWAP)


ANY = pl.BlockSpec(memory_space=pl.ANY)
HINT = pl.CostEstimate(flops=1000, bytes_accessed=1000, transcendentals=0)


def by_time_kernel(cuts, block, *refs):
    outs, (given, turned, sems) = refs[-len(cuts) - 3 : -3], refs[-3:]
    pairs, comps = given.shape[0], given.shape[2]
    copies = [
        pltpu.make_async_copy(block.at[:, :, pl.ds(16 * i, 16)], given.at[i], sems.at[i])
        for i in range(pairs)
    ]
    copies[0].start()
    sent = []
    for z in range(2 * pairs):
        if z % 2 == 0:
            copies[z // 2].wait()
            if z // 2 + 1 < pairs:
                copies[z // 2 + 1].start()
        for k in range(comps):
            eight = pl.ds(8 * (z % 2), 8)
            turned[z, :, k] = jnp.swapaxes(given[z // 2, :, k, eight], 0, 1)
        for (low, high, x, nx, y, ny), out in zip(cuts, outs):
            for i in range(nx):
                at = len(sent)
                source = turned.at[z, pl.ds(2 * (x + i) + y, ny), :, pl.ds(low, high - low)]
                sent.append(pltpu.make_async_copy(source, out.at[i, z], sems.at[pairs + at]))
                sent[at].start()
    for copy in sent:
        copy.wait()


def by_time(block, cuts, *after):
    n, comps, times, sites = block.shape
    return pl.pallas_call(
        functools.partial(by_time_kernel, cuts),
        in_specs=[ANY] * (1 + len(after)),
        out_specs=[ANY] * len(cuts),
        out_shape=[
            jax.ShapeDtypeStruct((nx, 4, ny, comps, high - low, sites), block.dtype)
            for low, high, _, nx, _, ny in cuts
        ],
        scratch_shapes=[
            pltpu.VMEM((times // 16, n, comps, 16, sites), block.dtype),
            pltpu.VMEM((times // 8, 8, comps, n, sites), block.dtype),
            pltpu.SemaphoreType.DMA((times // 16 + sum(4 * cut[3] for cut in cuts),)),
        ],
        compiler_params=pltpu.CompilerParams(vmem_limit_bytes=56 * 2**20),
        cost_estimate=HINT,
        name="by_time",
    )(block, *after)


def rows_of(block):
    x, z, yh, comps, n, sites = block.shape
    return block.reshape(x, z * yh, comps // 2, 2 * n, sites)


def mark(value):
    while value.ndim > 2:
        value = value[0]
    return value


def hold_kernel(*refs):
    pass


def hold(value, *after):
    return pl.pallas_call(
        hold_kernel,
        in_specs=[ANY] * (1 + len(after)),
        out_specs=ANY,
        out_shape=jax.ShapeDtypeStruct(value.shape, value.dtype),
        input_output_aliases={0: 0},
        cost_estimate=HINT,
        name="hold",
    )(value, *after)


def choose_kernel(owned, index, when, vecs, out, lines, sems):
    count, comps, rows, _ = lines.shape
    group, time = 2 * lax.axis_index("yl") + lax.axis_index("c"), when[0]
    first = pl.multiple_of(time // rows * rows, rows)
    picks = [
        pltpu.make_async_copy(
            vecs.at[index[s] % owned, :, pl.ds(first, rows)], lines.at[s], sems.at[s]
        )
        for s in range(count)
    ]
    for copy in picks:
        copy.start()
    row = lax.broadcasted_iota(jnp.int32, lines.shape[1:], 1)
    for s in range(count):
        picks[s].wait()
        here = jnp.where(index[s] // owned == group, time % rows, -1)
        kept = jnp.sum(jnp.where(row == here, lines[s].astype(jnp.float32), 0.0), axis=1)
        out[s] = jnp.concatenate([kept, jnp.zeros_like(kept[:2])], axis=0).astype(out.dtype)


def choose(vecs, source_index, source_time, after):
    owned, comps, times, sites = vecs.shape
    count = source_index.shape[0]
    kernel = functools.partial(choose_kernel, owned)
    return pl.pallas_call(
        lambda index, when, vecs, after, *refs: kernel(index, when, vecs, *refs),
        in_specs=[pl.BlockSpec(memory_space=pltpu.SMEM)] * 2 + [ANY] * 2,
        out_specs=pl.BlockSpec(memory_space=pltpu.VMEM),
        out_shape=jax.ShapeDtypeStruct((count, 8, sites), vecs.dtype),
        scratch_shapes=[
            pltpu.VMEM((count, comps, 16, sites), vecs.dtype),
            pltpu.SemaphoreType.DMA((count,)),
        ],
        compiler_params=pltpu.CompilerParams(vmem_limit_bytes=60 * 2**20),
        cost_estimate=HINT,
        name="choose",
    )(source_index, source_time, vecs, after)


def product(cols, own, other):
    return lax.dot_general(
        jnp.concatenate(cols, axis=0),
        jnp.concatenate([own, other], axis=0),
        (((1,), (1,)), ((), ())),
        preferred_element_type=jnp.float32,
    )


def real_imag(total, row, n):
    width = total.shape[1] // 4
    re, im = total[row : row + n], total[row + n : row + 2 * n]
    real, imag = [], []
    for left in (0, 2 * width):
        mid, right = left + width, left + 2 * width
        real.append(re[:, left:mid] + im[:, mid:right])
        imag.append(im[:, left:mid] - re[:, mid:right])
    return jnp.concatenate(real, axis=1), jnp.concatenate(imag, axis=1)


def dot_kernel(count, *refs):
    cols, (own, other), out = refs[:count], refs[count : count + 2], refs[-1]
    for at in range(own.shape[1]):
        total = None
        for colour in range(own.shape[2]):
            term = product(
                [col[0, at, colour] for col in cols], own[0, at, colour], other[0, at, colour]
            )
            total = term if total is None else total + term
        row = 0
        for col in cols:
            n = col.shape[3] // 2
            real, imag = real_imag(total, 2 * row, n)
            out[0, at, 0, row : row + n], out[0, at, 1, row : row + n] = real, imag
            row += n


def pieces_kernel(col, own, other, *refs):
    total, out = None, refs[-1]
    for block in range(own.shape[0]):
        for colour in range(own.shape[2]):
            at = 2 * (block * own.shape[2] + colour)
            term = product([col[at], col[at + 1]], own[block, 0, colour], other[block, 0, colour])
            total = term if total is None else total + term
    out[0], out[1] = real_imag(total, 0, out.shape[1])


def project_pieces(cols, own, other, y, *after):
    count, _, *rest = own.shape
    vecs = pl.BlockSpec((count, 1, *rest), lambda i: (0, y, 0, 0, 0))
    rows = pl.BlockSpec((2 * count * rest[0], *cols.shape[1:]), lambda i: (0, 0, 0))
    return pl.pallas_call(
        pieces_kernel,
        grid=(1,),
        in_specs=[rows, vecs, vecs] + [ANY] * len(after),
        out_specs=pl.BlockSpec((2, cols.shape[1], own.shape[3]), lambda i: (0, 0, 0)),
        out_shape=jax.ShapeDtypeStruct((2, cols.shape[1], own.shape[3]), jnp.float32),
        compiler_params=pltpu.CompilerParams(vmem_limit_bytes=24 * 2**20),
        cost_estimate=HINT,
        name="project_pieces",
    )(cols, own, other, *after)


def project(cols, own, other, x, y, step, *after):
    size, inner, colours, _, sites = cols[0].shape
    rows, stride = own.shape[3], own.shape[1] // inner
    spec = lambda n, stride=1, x=0, y=0: pl.BlockSpec(
        (1, step, colours, n, sites), lambda i, j: (i + x, j * stride + y, 0, 0, 0)
    )
    in_specs = [spec(c.shape[3]) for c in cols] + [spec(rows, stride, x, y)] * 2
    in_specs += [ANY] * len(after)
    total = sum(c.shape[3] for c in cols) // 2
    out_specs = pl.BlockSpec((1, step, 2, total, rows), lambda i, j: (i, j, 0, 0, 0))
    out_shape = jax.ShapeDtypeStruct((size, inner, 2, total, rows), jnp.float32)
    return pl.pallas_call(
        functools.partial(dot_kernel, len(cols)),
        grid=(size, inner // step),
        in_specs=in_specs,
        out_specs=out_specs,
        out_shape=out_shape,
        compiler_params=pltpu.CompilerParams(vmem_limit_bytes=60 * 2**20),
        cost_estimate=HINT,
        name="project",
    )(*cols, own, other, *after)


def pick(value, index):
    return lax.dynamic_index_in_dim(value, index, 0, keepdims=False)


def share_z(slabs):
    me = lax.axis_index("z")
    got = [
        lax.ppermute(pick(slabs, (me + k) % 4), "z", [(i, (i + k) % 4) for i in range(4)])
        for k in (1, 3, 2)
    ]
    return [pick(slabs, me), *got]


def sum_z(slabs):
    got = share_z(slabs)
    return got[0] + got[1] + got[2] + got[3]


def sum_x(slabs):
    me = lax.axis_index("x")
    total = pick(slabs, me)
    for k in (1, 3, 2):
        pairs = [(i, (i + k) % 4) for i in range(4)]
        total = total + lax.ppermute(pick(slabs, (me + k) % 4), "x", pairs)
    return total


def sum_yh(part):
    me = lax.axis_index("yh")
    return pick(part, me) + swap(pick(part, 1 - me), "yh")


def local(eigvecs, solutions, source_index, source_time, dilution):
    owned, times, comps, sites = eigvecs.shape
    count = solutions.shape[1]
    nsources, spins = dilution.shape
    scale = 1.0 / math.sqrt(comps * sites * 32)
    core = lax.axis_index("c")
    group = 2 * lax.axis_index("yl") + core
    sols = solutions[0].transpose(0, 2, 1, 3)
    vecs = eigvecs.transpose(0, 2, 1, 3)

    other = swap(vecs, "c")
    mine = by_time(sols, ((0, count, 0, 3, 0, 2), (0, count, 3, 1, 0, 2)))
    mine = [rows_of(part) for part in mine]
    got = swap(mine[0], "yl")

    whole, late = (0, owned, 0, 4, 0, 2), (0, owned, 3, 1, 0, 2)
    own, own_late = by_time(vecs, (whole, late), mine[0])
    other = by_time(other, (whole,))[0]
    own, other = rows_of(own), rows_of(other)
    lines = choose(vecs, source_index, source_time, mark(other)).reshape(1, -1, sites)

    def against(parts, x, *after):
        out = project(parts, own, other, x, 0, 8, *after)
        return out.reshape(out.shape[0], 4, 2, 2 * count, 2 * owned)

    slabs = [v.reshape(4, 2, comps // 2, -1, sites) for v in (mine[1], own_late)]
    spread = share_z(jnp.concatenate(slabs, axis=3))
    first = [against(mine[:1], 0), against(mine[1:], 3)]
    spread[1] = hold(spread[1], mark(first[0]), mark(first[1]))
    spread = jnp.stack(spread)
    cut = 2 * count
    spread_s, spread_v = spread[:, :, :, :cut], spread[:, :, :, cut:]
    spread_w = swap(spread_v, "c")
    spread_s = [spread_s[:, y].reshape(-1, count, sites) for y in range(2)]

    first = sum_x(jnp.concatenate(first))
    part_a = hold(jnp.concatenate([spread_s[0], lines]), mark(first))
    got_a = swap(part_a, "yl")
    got_b = swap(hold(spread_s[1], mark(part_a)), "yl")
    late = against([got], 0)
    last = [project_pieces(got_a, spread_v, spread_w, 0)]
    last.append(project_pieces(got_b, spread_v, spread_w, 1, last[0]))
    late = jnp.swapaxes(late, 0, 1).reshape(4, -1, 2 * owned)
    late = share_z(jnp.concatenate([first.reshape(4, -1, 2 * owned), late], axis=1))
    late = late[0] + late[1] + late[2] + hold(late[3], last[0])
    cut = 4 * count
    first = late[:cut].reshape(2, -1, 2 * owned)
    late = late[cut:].reshape(6, -1, 2 * owned)
    late = jnp.concatenate([late, *(v.reshape(1, -1, 2 * owned) for v in last)])
    late = sum_x(late.reshape(4, 2, -1, 2 * owned))

    here = sum_yh(jnp.concatenate([first, late], axis=1))
    there = swap(here, "c")

    lines = lines[0] + got_a[-1]
    lines = lines + swap(lines, "c")

    def assemble(sums, half):
        sums = sums[:, half * owned : (half + 1) * owned].reshape(2, 2, count, owned)
        return sums[0], sums[1]

    h0, y0 = assemble(here, 0)
    h1, y1 = assemble(there, 1)
    tau = jnp.stack([h0, h1, y0, y1])
    order = jnp.stack([group, group ^ 1, group ^ 2, group ^ 3])
    spin_of = jnp.take(jnp.transpose(dilution), order, axis=0)
    mask = spin_of[:, None, :] == jnp.arange(spins, dtype=jnp.int32)[None, :, None]
    view = tau.reshape(4, 1, 2, MASS, nsources, count // (MASS * nsources), owned)
    picked = jnp.where(mask[:, :, None, None, :, None, None], view, 0.0)
    result = jnp.sum(picked, axis=0).reshape(spins, 2, count, owned) * scale
    result = result.transpose(3, 0, 2, 1).reshape(1, owned, spins * count * 2)

    chosen = lines.reshape(nsources, -1, sites)[:, :comps]
    my_spins = lax.dynamic_index_in_dim(dilution, group, 1, keepdims=False)
    spin_mask = jnp.arange(spins, dtype=jnp.int32)[None, :] == my_spins[:, None]
    sources = jnp.where(
        spin_mask[:, :, None, None], chosen[:, None, :, :], jnp.zeros((), jnp.bfloat16)
    )
    return result, sources[None]


def solution(mesh):
    split = Mesh(mesh.devices.reshape(2, 2, 4, 4, 2), ("yl", "c", "z", "x", "yh"))
    grp, lat = ("yl", "c"), ("z", "x", "yh")
    return jax.shard_map(
        local,
        mesh=split,
        in_specs=(P(grp, None, None, lat), P(grp, None, None, None, lat), P(), P(), P()),
        out_specs=(P(lat, grp, None), P(grp, None, None, None, lat)),
        check_vma=False,
    )
```

```python
import functools
import math

import jax
import jax.numpy as jnp
from jax import lax
from jax.experimental import pallas as pl
from jax.experimental.pallas import tpu as pltpu
from jax.sharding import Mesh
from jax.sharding import PartitionSpec as P

MASS = 2
SPLIT = 4
SWAP = [(0, 1), (1, 0)]


def swap(value, axis):
    return lax.ppermute(value, axis, SWAP)


ANY = pl.BlockSpec(memory_space=pl.ANY)
HINT = pl.CostEstimate(flops=1000, bytes_accessed=1000, transcendentals=0)


def by_time_kernel(cuts, block, *refs):
    outs, (given, turned, sems) = refs[-len(cuts) - 3 : -3], refs[-3:]
    pairs, comps = given.shape[0], given.shape[2]
    span = given.shape[1] // SPLIT
    copies = [
        pltpu.make_async_copy(
            block.at[pl.ds(q * span, span), :, pl.ds(16 * i, 16)],
            given.at[i, pl.ds(q * span, span)],
            sems.at[SPLIT * i + q],
        )
        for i in range(pairs)
        for q in range(SPLIT)
    ]
    for copy in copies:
        copy.start()
    sent = []
    for z in range(2 * pairs):
        if z % 2 == 0:
            for copy in copies[SPLIT * z // 2 : SPLIT * (z // 2 + 1)]:
                copy.wait()
        for k in range(comps):
            eight = pl.ds(8 * (z % 2), 8)
            turned[z, :, k] = jnp.swapaxes(given[z // 2, :, k, eight], 0, 1)
        for (low, high, x, nx, y, ny), out in zip(cuts, outs):
            for i in range(nx):
                at = len(sent)
                source = turned.at[z, pl.ds(2 * (x + i) + y, ny), :, pl.ds(low, high - low)]
                sent.append(pltpu.make_async_copy(source, out.at[i, z], sems.at[SPLIT * pairs + at]))
                sent[at].start()
    for copy in sent:
        copy.wait()


def by_time(block, cuts, *after):
    n, comps, times, sites = block.shape
    return pl.pallas_call(
        functools.partial(by_time_kernel, cuts),
        in_specs=[ANY] * (1 + len(after)),
        out_specs=[ANY] * len(cuts),
        out_shape=[
            jax.ShapeDtypeStruct((nx, 4, ny, comps, high - low, sites), block.dtype)
            for low, high, _, nx, _, ny in cuts
        ],
        scratch_shapes=[
            pltpu.VMEM((times // 16, n, comps, 16, sites), block.dtype),
            pltpu.VMEM((times // 8, 8, comps, n, sites), block.dtype),
            pltpu.SemaphoreType.DMA((SPLIT * times // 16 + sum(4 * cut[3] for cut in cuts),)),
        ],
        compiler_params=pltpu.CompilerParams(vmem_limit_bytes=56 * 2**20),
        cost_estimate=HINT,
        name="by_time",
    )(block, *after)


def rows_of(block):
    x, z, yh, comps, n, sites = block.shape
    return block.reshape(x, z * yh, comps // 2, 2 * n, sites)


def mark(value):
    while value.ndim > 2:
        value = value[0]
    return value


def hold_kernel(*refs):
    pass


def hold(value, *after):
    return pl.pallas_call(
        hold_kernel,
        in_specs=[ANY] * (1 + len(after)),
        out_specs=ANY,
        out_shape=jax.ShapeDtypeStruct(value.shape, value.dtype),
        input_output_aliases={0: 0},
        cost_estimate=HINT,
        name="hold",
    )(value, *after)


def choose_kernel(owned, index, when, vecs, out, lines, sems):
    count, comps, rows, _ = lines.shape
    group, time = 2 * lax.axis_index("yl") + lax.axis_index("c"), when[0]
    first = pl.multiple_of(time // rows * rows, rows)
    picks = [
        pltpu.make_async_copy(
            vecs.at[index[s] % owned, :, pl.ds(first, rows)], lines.at[s], sems.at[s]
        )
        for s in range(count)
    ]
    for copy in picks:
        copy.start()
    row = lax.broadcasted_iota(jnp.int32, lines.shape[1:], 1)
    for s in range(count):
        picks[s].wait()
        here = jnp.where(index[s] // owned == group, time % rows, -1)
        kept = jnp.sum(jnp.where(row == here, lines[s].astype(jnp.float32), 0.0), axis=1)
        out[s] = jnp.concatenate([kept, jnp.zeros_like(kept[:2])], axis=0).astype(out.dtype)


def choose(vecs, source_index, source_time, after):
    owned, comps, times, sites = vecs.shape
    count = source_index.shape[0]
    kernel = functools.partial(choose_kernel, owned)
    return pl.pallas_call(
        lambda index, when, vecs, after, *refs: kernel(index, when, vecs, *refs),
        in_specs=[pl.BlockSpec(memory_space=pltpu.SMEM)] * 2 + [ANY] * 2,
        out_specs=pl.BlockSpec(memory_space=pltpu.VMEM),
        out_shape=jax.ShapeDtypeStruct((count, 8, sites), vecs.dtype),
        scratch_shapes=[
            pltpu.VMEM((count, comps, 16, sites), vecs.dtype),
            pltpu.SemaphoreType.DMA((count,)),
        ],
        compiler_params=pltpu.CompilerParams(vmem_limit_bytes=60 * 2**20),
        cost_estimate=HINT,
        name="choose",
    )(source_index, source_time, vecs, after)


def product(cols, own, other):
    return lax.dot_general(
        jnp.concatenate(cols, axis=0),
        jnp.concatenate([own, other], axis=0),
        (((1,), (1,)), ((), ())),
        preferred_element_type=jnp.float32,
    )


def real_imag(total, row, n):
    width = total.shape[1] // 4
    re, im = total[row : row + n], total[row + n : row + 2 * n]
    real, imag = [], []
    for left in (0, 2 * width):
        mid, right = left + width, left + 2 * width
        real.append(re[:, left:mid] + im[:, mid:right])
        imag.append(im[:, left:mid] - re[:, mid:right])
    return jnp.concatenate(real, axis=1), jnp.concatenate(imag, axis=1)


def dot_kernel(count, *refs):
    cols, (own, other), out = refs[:count], refs[count : count + 2], refs[-1]
    for at in range(own.shape[1]):
        total = None
        for colour in range(own.shape[2]):
            term = product(
                [col[0, at, colour] for col in cols], own[0, at, colour], other[0, at, colour]
            )
            total = term if total is None else total + term
        row = 0
        for col in cols:
            n = col.shape[3] // 2
            real, imag = real_imag(total, 2 * row, n)
            out[0, at, 0, row : row + n], out[0, at, 1, row : row + n] = real, imag
            row += n


def pieces_kernel(y, col, own, other, *refs):
    total, out = None, refs[-1]
    for block in range(own.shape[0]):
        for colour in range(own.shape[2]):
            at = 2 * (block * own.shape[2] + colour)
            term = product([col[at], col[at + 1]], own[block, y, colour], other[block, y, colour])
            total = term if total is None else total + term
    out[0], out[1] = real_imag(total, 0, out.shape[1])


def project_pieces(cols, own, other, y, *after):
    whole = pl.BlockSpec(memory_space=pltpu.VMEM)
    return pl.pallas_call(
        functools.partial(pieces_kernel, y),
        in_specs=[whole] * 3 + [ANY] * len(after),
        out_specs=whole,
        out_shape=jax.ShapeDtypeStruct((2, cols.shape[1], own.shape[3]), jnp.float32),
        compiler_params=pltpu.CompilerParams(vmem_limit_bytes=24 * 2**20),
        cost_estimate=HINT,
        name="project_pieces",
    )(cols, own, other, *after)


def project(cols, own, other, x, y, step, *after):
    size, inner, colours, _, sites = cols[0].shape
    rows, stride = own.shape[3], own.shape[1] // inner
    spec = lambda n, stride=1, x=0, y=0: pl.BlockSpec(
        (1, step, colours, n, sites), lambda i, j: (i + x, j * stride + y, 0, 0, 0)
    )
    in_specs = [spec(c.shape[3]) for c in cols] + [spec(rows, stride, x, y)] * 2
    in_specs += [ANY] * len(after)
    total = sum(c.shape[3] for c in cols) // 2
    out_specs = pl.BlockSpec((1, step, 2, total, rows), lambda i, j: (i, j, 0, 0, 0))
    out_shape = jax.ShapeDtypeStruct((size, inner, 2, total, rows), jnp.float32)
    return pl.pallas_call(
        functools.partial(dot_kernel, len(cols)),
        grid=(size, inner // step),
        in_specs=in_specs,
        out_specs=out_specs,
        out_shape=out_shape,
        compiler_params=pltpu.CompilerParams(vmem_limit_bytes=60 * 2**20),
        cost_estimate=HINT,
        name="project",
    )(*cols, own, other, *after)


def pick(value, index):
    return lax.dynamic_index_in_dim(value, index, 0, keepdims=False)


def share_z(slabs):
    me = lax.axis_index("z")
    got = [
        lax.ppermute(pick(slabs, (me + k) % 4), "z", [(i, (i + k) % 4) for i in range(4)])
        for k in (1, 3, 2)
    ]
    return [pick(slabs, me), *got]


def sum_z(slabs):
    got = share_z(slabs)
    return got[0] + got[1] + got[2] + got[3]


def sum_x(slabs):
    me = lax.axis_index("x")
    total = pick(slabs, me)
    for k in (1, 3, 2):
        pairs = [(i, (i + k) % 4) for i in range(4)]
        total = total + lax.ppermute(pick(slabs, (me + k) % 4), "x", pairs)
    return total


def sum_yh(part):
    me = lax.axis_index("yh")
    return pick(part, me) + swap(pick(part, 1 - me), "yh")


def local(eigvecs, solutions, source_index, source_time, dilution):
    owned, times, comps, sites = eigvecs.shape
    count = solutions.shape[1]
    nsources, spins = dilution.shape
    scale = 1.0 / math.sqrt(comps * sites * 32)
    core = lax.axis_index("c")
    group = 2 * lax.axis_index("yl") + core
    sols = solutions[0].transpose(0, 2, 1, 3)
    vecs = eigvecs.transpose(0, 2, 1, 3)

    other = swap(vecs, "c")
    mine = by_time(sols, ((0, count, 0, 3, 0, 2), (0, count, 3, 1, 0, 2)))
    mine = [rows_of(part) for part in mine]
    got = swap(mine[0], "yl")

    whole, late = (0, owned, 0, 4, 0, 2), (0, owned, 3, 1, 0, 2)
    own, own_late = by_time(vecs, (whole, late), mine[0])
    other = by_time(other, (whole,))[0]
    own, other = rows_of(own), rows_of(other)
    lines = choose(vecs, source_index, source_time, mark(other)).reshape(1, -1, sites)

    def against(parts, x, *after):
        out = project(parts, own, other, x, 0, 8, *after)
        return out.reshape(out.shape[0], 4, 2, 2 * count, 2 * owned)

    slabs = [v.reshape(4, 2, comps // 2, -1, sites) for v in (mine[1], own_late)]
    spread = share_z(jnp.concatenate(slabs, axis=3))
    first = [against(mine[:1], 0), against(mine[1:], 3)]
    spread[1] = hold(spread[1], mark(first[0]), mark(first[1]))
    spread = jnp.stack(spread)
    cut = 2 * count
    spread_s, spread_v = spread[:, :, :, :cut], spread[:, :, :, cut:]
    spread_w = swap(spread_v, "c")
    spread_s = [spread_s[:, y].reshape(-1, count, sites) for y in range(2)]

    first = sum_x(jnp.concatenate(first))
    got_a = swap(hold(jnp.concatenate([spread_s[0], lines]), mark(first)), "yl")
    late = against([got], 0)
    got_b = swap(hold(spread_s[1], mark(late)), "yl")
    last = [project_pieces(got_a, spread_v, spread_w, 0)]
    last.append(project_pieces(got_b, spread_v, spread_w, 1, last[0]))
    late = jnp.swapaxes(late, 0, 1).reshape(4, -1, 2 * owned)
    late = share_z(jnp.concatenate([first.reshape(4, -1, 2 * owned), late], axis=1))
    late = late[0] + late[1] + late[2] + hold(late[3], last[0])
    cut = 4 * count
    first = late[:cut].reshape(2, -1, 2 * owned)
    late = late[cut:].reshape(6, -1, 2 * owned)
    late = jnp.concatenate([late, *(v.reshape(1, -1, 2 * owned) for v in last)])
    late = sum_x(late.reshape(4, 2, -1, 2 * owned))

    here = sum_yh(jnp.concatenate([first, late], axis=1))
    there = swap(here, "c")

    lines = lines[0] + got_a[-1]
    lines = lines + swap(lines, "c")

    def assemble(sums, half):
        sums = sums[:, half * owned : (half + 1) * owned].reshape(2, 2, count, owned)
        return sums[0], sums[1]

    h0, y0 = assemble(here, 0)
    h1, y1 = assemble(there, 1)
    tau = jnp.stack([h0, h1, y0, y1])
    order = jnp.stack([group, group ^ 1, group ^ 2, group ^ 3])
    spin_of = jnp.take(jnp.transpose(dilution), order, axis=0)
    mask = spin_of[:, None, :] == jnp.arange(spins, dtype=jnp.int32)[None, :, None]
    view = tau.reshape(4, 1, 2, MASS, nsources, count // (MASS * nsources), owned)
    picked = jnp.where(mask[:, :, None, None, :, None, None], view, 0.0)
    result = jnp.sum(picked, axis=0).reshape(spins, 2, count, owned) * scale
    result = result.transpose(3, 0, 2, 1).reshape(1, owned, spins * count * 2)

    chosen = lines.reshape(nsources, -1, sites)[:, :comps]
    my_spins = lax.dynamic_index_in_dim(dilution, group, 1, keepdims=False)
    spin_mask = jnp.arange(spins, dtype=jnp.int32)[None, :] == my_spins[:, None]
    sources = jnp.where(
        spin_mask[:, :, None, None], chosen[:, None, :, :], jnp.zeros((), jnp.bfloat16)
    )
    return result, sources[None]


def solution(mesh):
    split = Mesh(mesh.devices.reshape(2, 2, 4, 4, 2), ("yl", "c", "z", "x", "yh"))
    grp, lat = ("yl", "c"), ("z", "x", "yh")
    return jax.shard_map(
        local,
        mesh=split,
        in_specs=(P(grp, None, None, lat), P(grp, None, None, None, lat), P(), P(), P()),
        out_specs=(P(lat, grp, None), P(grp, None, None, None, lat)),
        check_vma=False,
    )
```

```python
import functools
import math

import jax
import jax.numpy as jnp
from jax import lax
from jax.experimental import pallas as pl
from jax.experimental.pallas import tpu as pltpu
from jax.sharding import Mesh
from jax.sharding import PartitionSpec as P

MASS = 2
SWAP = [(0, 1), (1, 0)]


def swap(value, axis):
    return lax.ppermute(value, axis, SWAP)


ANY = pl.BlockSpec(memory_space=pl.ANY)
HINT = pl.CostEstimate(flops=1000, bytes_accessed=1000, transcendentals=0)


def by_time_kernel(cuts, block, *refs):
    outs, (given, turned, sems) = refs[-len(cuts) - 3 : -3], refs[-3:]
    pairs, comps = given.shape[0], given.shape[2]
    copies = [
        pltpu.make_async_copy(block.at[:, :, pl.ds(16 * i, 16)], given.at[i], sems.at[i])
        for i in range(pairs)
    ]
    for copy in copies:
        copy.start()
    sent = []
    for z in range(2 * pairs):
        if z % 2 == 0:
            copies[z // 2].wait()
        for k in range(comps):
            eight = pl.ds(8 * (z % 2), 8)
            turned[z, :, k] = jnp.swapaxes(given[z // 2, :, k, eight], 0, 1)
        for (low, high, x, nx, y, ny), out in zip(cuts, outs):
            for i in range(nx):
                at = len(sent)
                source = turned.at[z, pl.ds(2 * (x + i) + y, ny), :, pl.ds(low, high - low)]
                sent.append(pltpu.make_async_copy(source, out.at[i, z], sems.at[pairs + at]))
                sent[at].start()
    for copy in sent:
        copy.wait()


def by_time(block, cuts, *after):
    n, comps, times, sites = block.shape
    return pl.pallas_call(
        functools.partial(by_time_kernel, cuts),
        in_specs=[ANY] * (1 + len(after)),
        out_specs=[ANY] * len(cuts),
        out_shape=[
            jax.ShapeDtypeStruct((nx, 4, ny, comps, high - low, sites), block.dtype)
            for low, high, _, nx, _, ny in cuts
        ],
        scratch_shapes=[
            pltpu.VMEM((times // 16, n, comps, 16, sites), block.dtype),
            pltpu.VMEM((times // 8, 8, comps, n, sites), block.dtype),
            pltpu.SemaphoreType.DMA((times // 16 + sum(4 * cut[3] for cut in cuts),)),
        ],
        compiler_params=pltpu.CompilerParams(vmem_limit_bytes=56 * 2**20),
        cost_estimate=HINT,
        name="by_time",
    )(block, *after)


def rows_of(block):
    x, z, yh, comps, n, sites = block.shape
    return block.reshape(x, z * yh, comps // 2, 2 * n, sites)


def mark(value):
    while value.ndim > 2:
        value = value[0]
    return value


def hold_kernel(*refs):
    pass


def hold(value, *after):
    return pl.pallas_call(
        hold_kernel,
        in_specs=[ANY] * (1 + len(after)),
        out_specs=ANY,
        out_shape=jax.ShapeDtypeStruct(value.shape, value.dtype),
        input_output_aliases={0: 0},
        cost_estimate=HINT,
        name="hold",
    )(value, *after)


def choose_kernel(owned, index, when, vecs, out, lines, sems):
    count, comps, rows, _ = lines.shape
    group, time = 2 * lax.axis_index("yl") + lax.axis_index("c"), when[0]
    first = pl.multiple_of(time // rows * rows, rows)
    picks = [
        pltpu.make_async_copy(
            vecs.at[index[s] % owned, :, pl.ds(first, rows)], lines.at[s], sems.at[s]
        )
        for s in range(count)
    ]
    for copy in picks:
        copy.start()
    row = lax.broadcasted_iota(jnp.int32, lines.shape[1:], 1)
    for s in range(count):
        picks[s].wait()
        here = jnp.where(index[s] // owned == group, time % rows, -1)
        kept = jnp.sum(jnp.where(row == here, lines[s].astype(jnp.float32), 0.0), axis=1)
        out[s] = jnp.concatenate([kept, jnp.zeros_like(kept[:2])], axis=0).astype(out.dtype)


def choose(vecs, source_index, source_time, after):
    owned, comps, times, sites = vecs.shape
    count = source_index.shape[0]
    kernel = functools.partial(choose_kernel, owned)
    return pl.pallas_call(
        lambda index, when, vecs, after, *refs: kernel(index, when, vecs, *refs),
        in_specs=[pl.BlockSpec(memory_space=pltpu.SMEM)] * 2 + [ANY] * 2,
        out_specs=pl.BlockSpec(memory_space=pltpu.VMEM),
        out_shape=jax.ShapeDtypeStruct((count, 8, sites), vecs.dtype),
        scratch_shapes=[
            pltpu.VMEM((count, comps, 16, sites), vecs.dtype),
            pltpu.SemaphoreType.DMA((count,)),
        ],
        compiler_params=pltpu.CompilerParams(vmem_limit_bytes=60 * 2**20),
        cost_estimate=HINT,
        name="choose",
    )(source_index, source_time, vecs, after)


def product(cols, own, other):
    return lax.dot_general(
        jnp.concatenate(cols, axis=0),
        jnp.concatenate([own, other], axis=0),
        (((1,), (1,)), ((), ())),
        preferred_element_type=jnp.float32,
    )


def real_imag(total, row, n):
    width = total.shape[1] // 4
    re, im = total[row : row + n], total[row + n : row + 2 * n]
    real, imag = [], []
    for left in (0, 2 * width):
        mid, right = left + width, left + 2 * width
        real.append(re[:, left:mid] + im[:, mid:right])
        imag.append(im[:, left:mid] - re[:, mid:right])
    return jnp.concatenate(real, axis=1), jnp.concatenate(imag, axis=1)


def dot_kernel(count, *refs):
    cols, (own, other), out = refs[:count], refs[count : count + 2], refs[-1]
    for at in range(own.shape[1]):
        total = None
        for colour in range(own.shape[2]):
            term = product(
                [col[0, at, colour] for col in cols], own[0, at, colour], other[0, at, colour]
            )
            total = term if total is None else total + term
        row = 0
        for col in cols:
            n = col.shape[3] // 2
            real, imag = real_imag(total, 2 * row, n)
            out[0, at, 0, row : row + n], out[0, at, 1, row : row + n] = real, imag
            row += n


def pieces_kernel(col, own, other, *refs):
    total, out = None, refs[-1]
    for block in range(own.shape[0]):
        for colour in range(own.shape[2]):
            at = 2 * (block * own.shape[2] + colour)
            term = product([col[at], col[at + 1]], own[block, 0, colour], other[block, 0, colour])
            total = term if total is None else total + term
    out[0], out[1] = real_imag(total, 0, out.shape[1])


def project_pieces(cols, own, other, y, *after):
    count, _, *rest = own.shape
    vecs = pl.BlockSpec((count, 1, *rest), lambda i: (0, y, 0, 0, 0))
    rows = pl.BlockSpec((2 * count * rest[0], *cols.shape[1:]), lambda i: (0, 0, 0))
    return pl.pallas_call(
        pieces_kernel,
        grid=(1,),
        in_specs=[rows, vecs, vecs] + [ANY] * len(after),
        out_specs=pl.BlockSpec((2, cols.shape[1], own.shape[3]), lambda i: (0, 0, 0)),
        out_shape=jax.ShapeDtypeStruct((2, cols.shape[1], own.shape[3]), jnp.float32),
        compiler_params=pltpu.CompilerParams(vmem_limit_bytes=24 * 2**20),
        cost_estimate=HINT,
        name="project_pieces",
    )(cols, own, other, *after)


def project(cols, own, other, x, y, step, *after):
    size, inner, colours, _, sites = cols[0].shape
    rows, stride = own.shape[3], own.shape[1] // inner
    spec = lambda n, stride=1, x=0, y=0: pl.BlockSpec(
        (1, step, colours, n, sites), lambda i, j: (i + x, j * stride + y, 0, 0, 0)
    )
    in_specs = [spec(c.shape[3]) for c in cols] + [spec(rows, stride, x, y)] * 2
    in_specs += [ANY] * len(after)
    total = sum(c.shape[3] for c in cols) // 2
    out_specs = pl.BlockSpec((1, step, 2, total, rows), lambda i, j: (i, j, 0, 0, 0))
    out_shape = jax.ShapeDtypeStruct((size, inner, 2, total, rows), jnp.float32)
    return pl.pallas_call(
        functools.partial(dot_kernel, len(cols)),
        grid=(size, inner // step),
        in_specs=in_specs,
        out_specs=out_specs,
        out_shape=out_shape,
        compiler_params=pltpu.CompilerParams(vmem_limit_bytes=60 * 2**20),
        cost_estimate=HINT,
        name="project",
    )(*cols, own, other, *after)


def pick(value, index):
    return lax.dynamic_index_in_dim(value, index, 0, keepdims=False)


def share_z(slabs, pick=pick):
    me = lax.axis_index("z")
    got = [
        lax.ppermute(pick(slabs, (me + k) % 4), "z", [(i, (i + k) % 4) for i in range(4)])
        for k in (1, 3, 2)
    ]
    return [pick(slabs, me), *got]


def sum_z(slabs):
    got = share_z(slabs)
    return got[0] + got[1] + got[2] + got[3]


def sum_x(slabs):
    me = lax.axis_index("x")
    total = pick(slabs, me)
    for k in (1, 3, 2):
        pairs = [(i, (i + k) % 4) for i in range(4)]
        total = total + lax.ppermute(pick(slabs, (me + k) % 4), "x", pairs)
    return total


def sum_yh(part):
    me = lax.axis_index("yh")
    return pick(part, me) + swap(pick(part, 1 - me), "yh")


def local(eigvecs, solutions, source_index, source_time, dilution):
    owned, times, comps, sites = eigvecs.shape
    count = solutions.shape[1]
    nsources, spins = dilution.shape
    scale = 1.0 / math.sqrt(comps * sites * 32)
    core = lax.axis_index("c")
    group = 2 * lax.axis_index("yl") + core
    sols = solutions[0].transpose(0, 2, 1, 3)
    vecs = eigvecs.transpose(0, 2, 1, 3)

    other = swap(vecs, "c")
    mine = by_time(sols, ((0, count, 0, 3, 0, 2), (0, count, 3, 1, 0, 2)))
    mine = [rows_of(part) for part in mine]
    got = swap(mine[0], "yl")

    whole, late = (0, owned, 0, 4, 0, 2), (0, owned, 3, 1, 0, 2)
    own, own_late = by_time(vecs, (whole, late), mine[0])
    other = by_time(other, (whole,))[0]
    own, other = rows_of(own), rows_of(other)
    lines = choose(vecs, source_index, source_time, mark(other)).reshape(1, -1, sites)

    def against(parts, x, *after):
        out = project(parts, own, other, x, 0, 8, *after)
        return out.reshape(out.shape[0], 4, 2, 2 * count, 2 * owned)

    slabs = [v.reshape(4, 2, comps // 2, -1, sites) for v in (mine[1], own_late)]
    spread = share_z(jnp.concatenate(slabs, axis=3))
    first = [against(mine[:1], 0), against(mine[1:], 3)]
    spread[1] = hold(spread[1], mark(first[0]), mark(first[1]))
    spread = jnp.stack(spread)
    cut = 2 * count
    spread_s, spread_v = spread[:, :, :, :cut], spread[:, :, :, cut:]
    spread_w = swap(spread_v, "c")
    spread_s = [spread_s[:, y].reshape(-1, count, sites) for y in range(2)]

    first = sum_x(jnp.concatenate(first))
    got_a = swap(hold(jnp.concatenate([spread_s[0], lines]), mark(first)), "yl")
    late = against([got], 0)
    got_b = swap(hold(spread_s[1], mark(late)), "yl")
    last = [project_pieces(got_a, spread_v, spread_w, 0)]
    last.append(project_pieces(got_b, spread_v, spread_w, 1, last[0]))
    late = share_z(
        (first, late),
        lambda v, z: jnp.concatenate(
            [
                pick(v[0], z).reshape(-1, 2 * owned),
                lax.dynamic_index_in_dim(v[1], z, 1, keepdims=False).reshape(-1, 2 * owned),
            ]
        ),
    )
    late = late[0] + late[1] + late[2] + hold(late[3], last[0])
    cut = 4 * count
    first = late[:cut].reshape(2, -1, 2 * owned)
    late = late[cut:].reshape(6, -1, 2 * owned)
    late = jnp.concatenate([late, *(v.reshape(1, -1, 2 * owned) for v in last)])
    late = sum_x(late.reshape(4, 2, -1, 2 * owned))

    here = sum_yh(jnp.concatenate([first, late], axis=1))
    there = swap(here, "c")

    lines = lines[0] + got_a[-1]
    lines = lines + swap(lines, "c")

    def assemble(sums, half):
        sums = sums[:, half * owned : (half + 1) * owned].reshape(2, 2, count, owned)
        return sums[0], sums[1]

    h0, y0 = assemble(here, 0)
    h1, y1 = assemble(there, 1)
    tau = jnp.stack([h0, h1, y0, y1])
    order = jnp.stack([group, group ^ 1, group ^ 2, group ^ 3])
    spin_of = jnp.take(jnp.transpose(dilution), order, axis=0)
    mask = spin_of[:, None, :] == jnp.arange(spins, dtype=jnp.int32)[None, :, None]
    view = tau.reshape(4, 1, 2, MASS, nsources, count // (MASS * nsources), owned)
    picked = jnp.where(mask[:, :, None, None, :, None, None], view, 0.0)
    result = jnp.sum(picked, axis=0).reshape(spins, 2, count, owned) * scale
    result = result.transpose(3, 0, 2, 1).reshape(1, owned, spins * count * 2)

    chosen = lines.reshape(nsources, -1, sites)[:, :comps]
    my_spins = lax.dynamic_index_in_dim(dilution, group, 1, keepdims=False)
    spin_mask = jnp.arange(spins, dtype=jnp.int32)[None, :] == my_spins[:, None]
    sources = jnp.where(
        spin_mask[:, :, None, None], chosen[:, None, :, :], jnp.zeros((), jnp.bfloat16)
    )
    return result, sources[None]


def solution(mesh):
    split = Mesh(mesh.devices.reshape(2, 2, 4, 4, 2), ("yl", "c", "z", "x", "yh"))
    grp, lat = ("yl", "c"), ("z", "x", "yh")
    return jax.shard_map(
        local,
        mesh=split,
        in_specs=(P(grp, None, None, lat), P(grp, None, None, None, lat), P(), P(), P()),
        out_specs=(P(lat, grp, None), P(grp, None, None, None, lat)),
        check_vma=False,
    )
```
